32 devices in a mesh: row: 4 (over y, core), col: 8 (over z, x).
Axes of the slice: x: 2, y: 2, z: 4, core: 2. Of those that a mesh axis runs over, the one named last changes fastest.
Arguments:
- diag_tile: float32 [1024, 1024], P('row', 'col'), as said below
- panel_left: float32 [128, 1024, 96], P('row', 'col'), may hold values from -0.625 to 0.625
- panel_right: float32 [128, 1024, 96], P('row', 'col'), may hold values from -2.5 to 2.5
- ranks: int32 [128], replicated, may hold values from 32 to 96, as said below
- tile_rows: int32 [128], replicated, may hold values from 0 to 127, each once
Outputs:
- solved_right: float32 [128, 1024, 96], P('row', 'col')
- update_left: float32 [128, 8, 1024, 96], P('row', 'col')
The draws below stay inside these ranges and needn't reach their ends.
Inputs may be any that keep to these rules, and one draw needn't show every extreme that they name: `ranks`: each slot's rank lies in 32 to 96; both ends occur in every draw. `tile_rows`: every tile row 0 to 127 stands in exactly one slot. diag_tile is a Matern covariance with smoothness nu = 3/2 of points in the unit square plus a positive nugget on its diagonal; it is symmetric positive definite.
All inputs are finite; a program needn't handle non-finite values.
Results may differ from the reference program's by a relative error of at most 0.0003.
Values sent between devices are 32-bit elements; how exact they have to be, the bound alone decides.
No kernel may reach another device: no remote copies, remote signals or barrier semaphores. Data moves between devices by JAX's collectives and lax.ppermute only.
A program may use at most 192 MiB of HBM per device.

```python
import math
import jax
import jax.numpy as jnp
from jax import lax

NB = 1024
RMAX = 96
M = 128
NTC = 8


def draw_diag_tile(key, part):
    key_across, key_along, key_nugget, key_order = jax.random.split(key, 4)
    length_scale = 0.35
    nugget_low = 0.05
    nugget_high = 0.2
    grid_side = math.isqrt(NB)
    position = jnp.arange(NB, dtype=jnp.int32)
    order = jax.random.permutation(key_order, NB).astype(jnp.int32)
    across = (order // grid_side).astype(jnp.float32)
    along = (order % grid_side).astype(jnp.float32)
    jitter_across = jax.random.uniform(key_across, (NB,), jnp.float32, 0.0, 1.0)
    jitter_along = jax.random.uniform(key_along, (NB,), jnp.float32, 0.0, 1.0)
    place_across = (across + jitter_across) / grid_side
    place_along = (along + jitter_along) / grid_side
    diff_across = place_across[:, None] - place_across[None, :]
    diff_along = place_along[:, None] - place_along[None, :]
    distance = jnp.sqrt(diff_across * diff_across + diff_along * diff_along)
    scaled = distance * (math.sqrt(3.0) / length_scale)
    kernel = (1.0 + scaled) * jnp.exp(-scaled)
    nugget = jax.random.uniform(key_nugget, (NB,), jnp.float32, nugget_low, nugget_high)
    eye_mask = position[:, None] == position[None, :]
    return kernel + jnp.where(eye_mask, nugget[:, None], 0.0)


def draw_ranks(key, part):
    key_values, key_spots = jax.random.split(key)
    values = jax.random.randint(key_values, (M,), RMAX // 3, RMAX + 1)
    places = jax.random.permutation(key_spots, M)
    values = values.at[places[0]].set(RMAX)
    values = values.at[places[1]].set(RMAX // 3)
    return values.astype(jnp.int32)


def levels(rng, extent, cuts, least, high):
    factor_of, own = 1.0, jax.random.fold_in(rng, 6)
    for dim, blocks in cuts:
        draws = jnp.exp(jax.random.uniform(jax.random.fold_in(own, dim), (blocks,), jnp.float32, least / len(cuts), high / len(cuts)))
        factor_of = factor_of * jnp.repeat(draws, extent[dim] // blocks).reshape([-1 if axis == dim else 1 for axis in range(len(extent))])
    return factor_of


def scatter_about(key, extent, scale, most, pieces=(), kind=jnp.bfloat16):
    array = scale * jax.random.normal(key, extent, jnp.float32)
    if pieces:
        array = array * levels(key, extent, pieces, -0.22, 0.18)
    return jnp.clip(array, -most, most).astype(kind)


def setup_inputs(seed: int = 0) -> dict:
    streams_of = jax.random.split(jax.random.key(seed), 6)
    diag_tile = draw_diag_tile(jax.random.fold_in(streams_of[5], 71), 0)
    panel_left = scatter_about(streams_of[1], (M, NB, RMAX), RMAX ** -0.5, 0.625, ((0, 4), (1, 8)), jnp.float32)
    panel_right = scatter_about(streams_of[2], (M, NB, RMAX), 0.18, 2.5, ((0, 4), (1, 8)), jnp.float32)
    ranks = draw_ranks(jax.random.fold_in(streams_of[5], 71), 0)
    tile_rows = jax.random.permutation(streams_of[4], M).astype(jnp.int32)
    return dict(diag_tile=diag_tile, panel_left=panel_left, panel_right=panel_right, ranks=ranks, tile_rows=tile_rows)


def reference(diag_tile, panel_left, panel_right, ranks, tile_rows):
    highest = lax.Precision.HIGHEST
    factor = jnp.linalg.cholesky(diag_tile)
    keep_mask = (jnp.arange(RMAX, dtype=jnp.int32)[None, :] < ranks[:, None]).astype(jnp.float32)
    left_kept = panel_left * keep_mask[:, None, :]
    right_kept = panel_right * keep_mask[:, None, :]
    flat = jnp.transpose(right_kept, (1, 0, 2)).reshape(NB, M * RMAX)
    solved_flat = jax.scipy.linalg.solve_triangular(factor, flat, lower=True)
    solved = jnp.transpose(solved_flat.reshape(NB, M, RMAX), (1, 0, 2))
    position = jnp.zeros((M,), jnp.int32).at[tile_rows].set(jnp.arange(M, dtype=jnp.int32))
    targets = solved[position[:NTC]]
    core_block = jnp.einsum('snr,jnq->sjrq', solved, targets, precision=highest)
    update = jnp.einsum('snr,sjrq->sjnq', left_kept, core_block, precision=highest)
    live = (tile_rows[:, None] >= jnp.arange(NTC, dtype=jnp.int32)[None, :]).astype(jnp.float32)
    update = update * live[:, :, None, None]
    return (solved, update)
```

```python
import functools
import jax
import jax.numpy as jnp
from jax import lax
from jax.experimental import pallas as pl
from jax.experimental.pallas import tpu as pltpu
from jax.sharding import PartitionSpec as P

F32 = jnp.float32
BF16 = jnp.bfloat16
HIGHEST = lax.Precision.HIGHEST
B = 128
MIB = 2**20


def sub_row(v, k):
    return jnp.broadcast_to(v[k : k + 1, :], v.shape)


def lane_col(v, c):
    return jnp.broadcast_to(v[:, c : c + 1], v.shape)


def inverse_factor(rows):
    lane = lax.broadcasted_iota(jnp.int32, (8, B), 1)
    sub = lax.broadcasted_iota(jnp.int32, (8, B), 0)
    work, out = list(rows), []
    for p in range(len(rows)):
        base = 8 * p
        cols = {q: [lane_col(work[q], base + j) for j in range(8)] for q in range(p, len(rows))}
        t = list(cols[p])
        in_panel = (lane >= base) & (lane < base + 8)
        r = jnp.where(in_panel, jnp.where(lane - base == sub, 1.0, 0.0).astype(F32), work[p])
        g = jnp.zeros((8, B), F32)
        for k in range(0, 8, 2):
            a, b, c = sub_row(t[k], k), sub_row(t[k], k + 1), sub_row(t[k + 1], k + 1)
            det = a * c - b * b
            inv = 1.0 / det
            pivot = (sub == k) | (sub == k + 1)
            t0 = jnp.where(pivot, jnp.where(sub == k, -1.0, 0.0).astype(F32), t[k])
            t1 = jnp.where(pivot, jnp.where(sub == k, 0.0, -1.0).astype(F32), t[k + 1])
            alpha = (t0 * c - t1 * b) * inv
            beta = (t1 * a - t0 * b) * inv
            x, y = sub_row(r, k), sub_row(r, k + 1)
            g0 = x * lax.rsqrt(a)
            g1 = (a * y - b * x) * lax.rsqrt(a * det)
            g = jnp.where(sub == k, g0, jnp.where(sub == k + 1, g1, g))
            r = jnp.where(pivot, 0.0, r) - alpha * x - beta * y
            for j in range(k + 2, 8):
                t[j] = jnp.where(pivot, 0.0, t[j]) - alpha * sub_row(t[j], k) - beta * sub_row(t[j], k + 1)
        out.append(jnp.where(lane <= sub + base, g, 0.0))
        z = [sub_row(r, j) for j in range(8)]
        for q in range(p + 1, len(rows)):
            acc = jnp.where(in_panel, 0.0, work[q])
            for j in range(8):
                acc = acc - cols[q][j] * z[j]
            work[q] = acc
    return out


def eliminate(w, g, y, k0, k1, blocks):
    for k in range(k0, k1):
        lo = B * k
        rows = [w[lo + 8 * q : lo + 8 * q + 8, lo : lo + B] for q in range(B // 8)]
        for q, piece in enumerate(inverse_factor(rows)):
            g[8 * q : 8 * q + 8, :] = piece
        y[...] = jnp.dot(g[...], w[lo : lo + B, :], precision=HIGHEST, preferred_element_type=F32)
        y[:, lo : lo + B] = g[...]
        w[lo : lo + B, :] = y[...]

        def body(i, carry):
            at = pl.multiple_of(i * B, B)
            w[pl.ds(at, B), lo : lo + B] = jnp.zeros((B, B), F32)
            w[pl.ds(at, B), :] -= lax.dot_general(
                y[:, pl.ds(at, B)], y[...], (((0,), (0,)), ((), ())), precision=HIGHEST, preferred_element_type=F32
            )
            return carry

        if k + 1 < blocks:
            lax.fori_loop(k + 1, blocks, body, 0)


def first_kernel(k1, blocks, masks, place, near, far, w, g, y):
    height, width = near.shape[1:]
    me_row, me_col = place[0], place[1]
    core = me_row % 2
    for m, (even, odd) in enumerate(masks):
        for flip, buf in ((0, near), (1, far)):
            odd_core = (core + flip) % 2
            row = (me_row ^ flip) ^ jnp.where(odd_core == 0, even[0], odd[0])
            col = me_col ^ jnp.where(odd_core == 0, even[1], odd[1])
            w[pl.ds(pl.multiple_of(row * height, 8), height), pl.ds(pl.multiple_of(col * width, B), width)] = buf[m]
    eliminate(w, g, y, 0, k1, blocks)


def whole_kernel(k1, blocks, w_in, w, g, y):
    w[...] = w_in[...]
    eliminate(w, g, y, 0, k1, blocks)


def next_kernel(k0, k1, blocks, w_in, w, g, y):
    w[...] = w_in[...]
    eliminate(w, g, y, k0, k1, blocks)


VM = pl.BlockSpec(memory_space=pltpu.VMEM)
SM = pl.BlockSpec(memory_space=pltpu.SMEM)


def elimination_call(kernel, order, specs, args):
    return pl.pallas_call(
        kernel,
        out_shape=jax.ShapeDtypeStruct((order, order), F32),
        in_specs=specs,
        out_specs=VM,
        scratch_shapes=[pltpu.VMEM((B, B), F32), pltpu.VMEM((B, order), F32)],
        compiler_params=pltpu.CompilerParams(vmem_limit_bytes=20 * MIB),
        cost_estimate=pl.CostEstimate(flops=4 * 10**9, bytes_accessed=8 * MIB, transcendentals=0),
    )(*args)


def split(v):
    high = v.astype(BF16)
    return high, (v - high.astype(F32)).astype(BF16)


def dot_tt(a, b):
    return lax.dot_general(a, b, (((1,), (1,)), ((), ())), preferred_element_type=F32)


def solve_kernel(masks, joined, n_own, n_all, width_cols, rank_max, *refs):
    if joined:
        inv, own, tgt, solved, core, xh, xl, ih, il, sh, sl = refs
    else:
        place, inv, own, near, far, solved, core, xh, xl, ih, il, sh, sl = refs
    blocks = inv.shape[0] // B
    for i in range(blocks):
        rows = slice(B * i, B * i + B)
        wide = B * (i + 1)
        ih[rows, :wide], il[rows, :wide] = split(inv[rows, :wide])
        if i % 2 == 0:
            ih[rows, wide : wide + B] = jnp.zeros((B, B), BF16)
            il[rows, wide : wide + B] = jnp.zeros((B, B), BF16)
    for c in range(blocks):
        xh[:n_own, B * c : B * c + B], xl[:n_own, B * c : B * c + B] = split(own[c])
        if joined:
            xh[n_own:, B * c : B * c + B], xl[n_own:, B * c : B * c + B] = split(tgt[c])
    if not joined:
        height, width = near.shape[1:]
        me_row, me_col = place[0], place[1]
        core_bit = me_row % 2
        for m, (even, odd) in enumerate(masks):
            for flip, buf in ((0, near), (1, far)):
                odd_core = (core_bit + flip) % 2
                row = (me_row ^ flip) ^ jnp.where(odd_core == 0, even[0], odd[0])
                col = me_col ^ jnp.where(odd_core == 0, even[1], odd[1])
                part = place[2 + row]
                high, low = split(buf[m])
                at = (pl.ds(pl.multiple_of(n_own + part * height, 16), height), pl.ds(pl.multiple_of(col * width, B), width))
                xh[at] = high
                xl[at] = low
    chunk = n_own

    def body(t, carry):
        at = pl.ds(pl.multiple_of(t * chunk, 16), chunk)
        for i in range(blocks // 2):
            deep = 2 * B * (i + 1)
            out = slice(2 * B * i, deep)
            h, l = xh[at, :deep], xl[at, :deep]
            gh, gl = ih[out, :deep], il[out, :deep]
            res = dot_tt(h, gh) + dot_tt(h, gl) + dot_tt(l, gh)
            sh[at, out], sl[at, out] = split(res)

            @pl.when(t == 0)
            def _():
                solved[2 * i] = res[:, :B]
                solved[2 * i + 1] = res[:, B:]

        return carry

    lax.fori_loop(0, n_all // chunk, body, 0)
    oh, ol = sh.at[:n_own], sl.at[:n_own]

    def core_body(j, carry):
        at = pl.ds(pl.multiple_of(n_own + j * rank_max, 16), rank_max)
        h, l = sh[at, :], sl[at, :]
        core[j] = dot_tt(h, oh[...]) + dot_tt(h, ol[...]) + dot_tt(l, oh[...])
        return carry

    lax.fori_loop(0, width_cols, core_body, 0)


def update_kernel(n, group, offs, ranks, tiles, col, core, *refs):
    own, fw, bw, out, us = refs[0], refs[1 : n], refs[n : 2 * n - 1], refs[2 * n - 1], refs[2 * n]
    step = pl.program_id(0)
    count = pl.num_programs(0)
    rank_max = own.shape[1]
    width = own.shape[2]
    row_id = lax.broadcasted_iota(jnp.int32, (rank_max, rank_max), 1)
    for s in range(group):
        def place(at, v):
            high, low = split(v)
            us[:rank_max, at] = high
            us[rank_max:, at] = low

        def spot(i):
            return pl.ds(pl.multiple_of(offs[i], width), width)

        place(spot(0), own[s])

        @pl.when(step < count // 2)
        def _():
            for k in range(n - 1):
                place(spot(1 + k), fw[k][s])

        @pl.when(step >= count // 2)
        def _():
            for k in range(n - 1):
                place(spot(n + k), bw[k][s])

        slot = step * group + s
        keep = (row_id < ranks[slot]) & (tiles[slot] >= col[0])
        c = jnp.where(keep, core[0, :, rank_max * s : rank_max * s + rank_max], 0.0)
        ch, cl = split(c)
        u = us[...]
        lhs = jnp.concatenate([ch, ch], axis=1)
        res = jnp.dot(lhs, u, preferred_element_type=F32)
        res = res + jnp.dot(cl, u[:rank_max], preferred_element_type=F32)
        out[s, 0] = res


def pick_kernel(slots, mine, ranks, right, out):
    j = pl.program_id(0)
    rank_max = right.shape[1]
    rows = lax.broadcasted_iota(jnp.int32, right.shape[1:], 0)
    keep = rows < jnp.where(mine[j] == 1, ranks[j], 0)
    out[0] = jnp.where(keep, right[0], 0.0)


def phases(rows, cols):
    even = []
    bit = cols // 2
    while bit > 1:
        even.append((0, bit))
        bit //= 2
    bit = rows // 2
    while bit > 2:
        even.append((bit, 0))
        bit //= 2
    odd = even + [(2, 0), (0, 1)]
    even = even + [(0, 1), (2, 0)]
    return even, odd


def gather_masks(rows, cols):
    even, odd = phases(rows, cols)

    def masks(steps):
        got = [(0, 0)]
        for r, c in steps:
            got = got + [(a ^ r, b ^ c) for a, b in got]
        return got

    return list(zip(masks(even), masks(odd)))


def gather_halves(piece, rows, cols):
    even, odd = phases(rows, cols)
    buf = piece[None]
    for e, o in zip(even, odd):
        pairs = []
        for r in range(rows):
            dr, dc = o if r % 2 else e
            for c in range(cols):
                pairs.append((r * cols + c, (r ^ dr) * cols + (c ^ dc)))
        buf = jnp.concatenate([buf, lax.ppermute(buf, ("row", "col"), pairs)], axis=0)
    swap = [(r, r ^ 1) for r in range(rows)]
    return buf, lax.ppermute(buf, "row", swap)


def ring_order(n):
    return list(range(0, n, 2)) + list(range(n - 1, 0, -2))


def shards(rows, cols, diag_tile, panel_left, panel_right, ranks, tile_rows):
    slots, piece_rows, rank_max = panel_left.shape
    order = piece_rows * cols
    blocks = order // B
    group = slots // cols
    row_index = lax.axis_index("row")
    col_index = lax.axis_index("col")
    masks = gather_masks(rows, cols)
    fits = piece_rows % B == 0 and blocks == cols
    left = jnp.transpose(panel_left, (0, 2, 1))
    right = jnp.transpose(panel_right, (0, 2, 1))
    own_ranks = lax.dynamic_slice_in_dim(ranks, row_index * slots, slots)
    own_tiles = lax.dynamic_slice_in_dim(tile_rows, row_index * slots, slots)

    def source_flat():
        even = jnp.array([e for e, _ in masks], jnp.int32)
        odd = jnp.array([o for _, o in masks], jnp.int32)
        is_odd = row_index % 2
        near = jnp.where(is_odd == 0, even, odd)
        far = jnp.where(is_odd == 0, odd, even)
        r = jnp.concatenate([row_index ^ near[:, 0], row_index ^ 1 ^ far[:, 0]])
        c = jnp.concatenate([col_index ^ near[:, 1], col_index ^ far[:, 1]])
        return r, c

    near, far = gather_halves(diag_tile, rows, cols)

    keep = jnp.arange(rank_max, dtype=jnp.int32)[None, :] < own_ranks[:, None]
    right_part = jnp.where(keep[:, :, None], right, 0.0)
    own = lax.all_to_all(right_part.reshape(cols, group, rank_max, piece_rows), "col", split_axis=0, concat_axis=0, tiled=True)
    own = own.reshape(cols, group * rank_max, piece_rows)

    wanted = jnp.arange(cols, dtype=jnp.int32)
    every_slot = jnp.arange(tile_rows.shape[0], dtype=jnp.int32)
    holder = jnp.sum(jnp.where(tile_rows[None, :] == wanted[:, None], every_slot[None, :], 0), axis=1)
    mine = (holder // slots == row_index).astype(jnp.int32)
    target_ranks = jnp.sum(jnp.where(tile_rows[None, :] == wanted[:, None], ranks[None, :], 0), axis=1)
    part = pl.pallas_call(
        pick_kernel,
        out_shape=jax.ShapeDtypeStruct((cols, rank_max, piece_rows), F32),
        grid_spec=pltpu.PrefetchScalarGridSpec(
            num_scalar_prefetch=3,
            grid=(cols,),
            in_specs=[pl.BlockSpec((1, rank_max, piece_rows), lambda j, s, m, r: (s[j], 0, 0))],
            out_specs=pl.BlockSpec((1, rank_max, piece_rows), lambda j, s, m, r: (j, 0, 0)),
        ),
    )(holder % slots, mine, target_ranks, right)
    bit = 1
    while bit < rows:
        half = part.shape[0] // 2
        side = (row_index // bit) % 2
        kept = lax.dynamic_slice_in_dim(part, side * half, half, 0)
        sent = lax.dynamic_slice_in_dim(part, (1 - side) * half, half, 0)
        part = kept + lax.ppermute(sent, "row", [(r, r ^ bit) for r in range(rows)])
        bit *= 2
    per = part.shape[0]
    places = []
    for r in range(rows):
        at, half, b = 0, rows // 2, 1
        while b < rows:
            at += half * ((r // b) % 2)
            half //= 2
            b *= 2
        places.append(at)
    t_near, t_far = gather_halves(part.reshape(per * rank_max, piece_rows), rows, cols)

    cycle = ring_order(cols)
    forward = [(cycle[i], cycle[(i + 1) % cols]) for i in range(cols)]
    backward = [(b, a) for a, b in forward]
    half = slots // 2
    fw, bw = [], []
    a, b = left[:half], left[half:]
    for _ in range(cols - 1):
        a = lax.ppermute(a, "col", forward)
        b = lax.ppermute(b, "col", backward)
        fw.append(a)
        bw.append(b)

    place = jnp.concatenate([jnp.stack([row_index, col_index]).astype(jnp.int32), jnp.array(places, jnp.int32)])
    per_call = 2
    if fits:
        inv = elimination_call(
            functools.partial(first_kernel, per_call, blocks, masks), order, [SM, VM, VM], (place, near, far)
        )
    else:
        r, c = source_flat()
        pieces = jnp.concatenate([near, far], axis=0)
        tile = jnp.zeros((rows * cols,) + pieces.shape[1:], F32).at[r * cols + c].set(pieces)
        tile = tile.reshape(rows, cols, order // rows, piece_rows).transpose(0, 2, 1, 3).reshape(order, order)
        inv = elimination_call(functools.partial(whole_kernel, per_call, blocks), order, [VM], (tile,))
    for k in range(per_call, blocks, per_call):
        inv = elimination_call(functools.partial(next_kernel, k, k + per_call, blocks), order, [VM], (inv,))

    n_own, n_tgt = group * rank_max, cols * rank_max
    n_all = n_own + n_tgt
    if fits:
        extra, specs = (t_near, t_far), [SM, VM, VM, VM, VM]
        args = (place, inv, own) + extra
    else:
        own = own.transpose(1, 0, 2).reshape(n_own, blocks, B).transpose(1, 0, 2)
        r, c = source_flat()
        spots = jnp.array(places, jnp.int32)[r]
        pieces = jnp.concatenate([t_near, t_far], axis=0)
        tgt = jnp.zeros((rows * cols,) + pieces.shape[1:], F32).at[spots * cols + c].set(pieces)
        tgt = tgt.reshape(rows, cols, per * rank_max, piece_rows).transpose(0, 2, 1, 3).reshape(n_tgt, blocks, B)
        args, specs = (inv, own, tgt.transpose(1, 0, 2)), [VM, VM, VM]
    solved, core = pl.pallas_call(
        functools.partial(solve_kernel, masks, not fits, n_own, n_all, cols, rank_max),
        out_shape=[
            jax.ShapeDtypeStruct((blocks, n_own, B), F32),
            jax.ShapeDtypeStruct((cols, rank_max, n_own), F32),
        ],
        in_specs=specs,
        out_specs=[VM, VM],
        scratch_shapes=[
            pltpu.VMEM((n_all, order), BF16),
            pltpu.VMEM((n_all, order), BF16),
            pltpu.VMEM((order, order), BF16),
            pltpu.VMEM((order, order), BF16),
            pltpu.VMEM((n_all, order), BF16),
            pltpu.VMEM((n_all, order), BF16),
        ],
        compiler_params=pltpu.CompilerParams(vmem_limit_bytes=50 * MIB),
        cost_estimate=pl.CostEstimate(flops=6 * 10**9, bytes_accessed=12 * MIB, transcendentals=0),
    )(*args)
    core = lax.all_to_all(core, "col", split_axis=0, concat_axis=0, tiled=True)
    if not fits:
        solved = solved.transpose(1, 0, 2).reshape(n_own, cols, piece_rows).transpose(1, 0, 2)
    back = lax.all_to_all(solved, "col", split_axis=0, concat_axis=0, tiled=True)
    own_rows = back.reshape(slots, rank_max, piece_rows)

    at = jnp.array([cycle.index(c) for c in range(cols)], jnp.int32)[col_index]
    cyc = jnp.array(cycle, jnp.int32)
    ks = jnp.arange(1, cols, dtype=jnp.int32)
    offs = jnp.concatenate([col_index[None], cyc[(at - ks) % cols], cyc[(at + ks) % cols]]).astype(jnp.int32) * piece_rows
    if fits:
        last = cols // 2 - 1
        u_spec = pl.BlockSpec((group, rank_max, piece_rows), lambda c, *_: (c, 0, 0))
        f_spec = pl.BlockSpec((group, rank_max, piece_rows), lambda c, *_: (jnp.minimum(c, last), 0, 0))
        b_spec = pl.BlockSpec((group, rank_max, piece_rows), lambda c, *_: (jnp.maximum(c - last - 1, 0), 0, 0))
        update = pl.pallas_call(
            functools.partial(update_kernel, cols, group),
            out_shape=jax.ShapeDtypeStruct((slots, 1, rank_max, order), F32),
            grid_spec=pltpu.PrefetchScalarGridSpec(
                num_scalar_prefetch=4,
                grid=(cols,),
                in_specs=[pl.BlockSpec((1, rank_max, n_own), lambda c, *_: (c, 0, 0)), u_spec]
                + [f_spec] * (cols - 1)
                + [b_spec] * (cols - 1),
                out_specs=pl.BlockSpec((group, 1, rank_max, order), lambda c, *_: (c, 0, 0, 0)),
                scratch_shapes=[pltpu.VMEM((2 * rank_max, order), BF16)],
            ),
            compiler_params=pltpu.CompilerParams(vmem_limit_bytes=40 * MIB),
        )(offs, own_ranks, own_tiles, col_index[None].astype(jnp.int32), core, left, *fw, *bw)
        update = jnp.transpose(update, (0, 1, 3, 2))
    else:
        spots = offs // piece_rows
        halves = []
        for h, ring in enumerate((fw, bw)):
            pieces = jnp.stack([left[h * half : h * half + half]] + ring)
            where = jnp.concatenate([spots[:1], spots[1 + h * (cols - 1) : 1 + (h + 1) * (cols - 1)]])
            halves.append(jnp.zeros_like(pieces).at[where].set(pieces))
        full = jnp.concatenate(halves, axis=1).transpose(1, 2, 0, 3).reshape(slots, rank_max, order)
        core = core.reshape(cols, rank_max, group, rank_max).transpose(0, 2, 3, 1).reshape(slots, rank_max, rank_max)
        live = (own_tiles >= col_index)[:, None, None] & keep[:, :, None]
        core = jnp.where(live, core, 0.0)
        update = jnp.einsum("srn,srq->snq", full, core, precision=HIGHEST)[:, None]
    return (jnp.transpose(own_rows, (0, 2, 1)), update)


def solution(mesh):
    return jax.shard_map(
        functools.partial(shards, mesh.shape["row"], mesh.shape["col"]),
        mesh=mesh,
        in_specs=(P("row", "col"), P("row", "col", None), P("row", "col", None), P(), P()),
        out_specs=(P("row", "col", None), P("row", "col", None, None)),
        check_vma=False,
    )
```

```python
import functools
import jax
import jax.numpy as jnp
from jax import lax
from jax.experimental import pallas as pl
from jax.experimental.pallas import tpu as pltpu
from jax.sharding import PartitionSpec as P

F32 = jnp.float32
BF16 = jnp.bfloat16
HIGHEST = lax.Precision.HIGHEST
B = 128
MIB = 2**20


def sub_row(v, k):
    return jnp.broadcast_to(v[k : k + 1, :], v.shape)


def lane_col(v, c):
    return jnp.broadcast_to(v[:, c : c + 1], v.shape)


def inverse_factor(rows):
    lane = lax.broadcasted_iota(jnp.int32, (8, B), 1)
    sub = lax.broadcasted_iota(jnp.int32, (8, B), 0)
    work, out = list(rows), []
    for p in range(len(rows)):
        base = 8 * p
        cols = {q: [lane_col(work[q], base + j) for j in range(8)] for q in range(p, len(rows))}
        t = list(cols[p])
        in_panel = (lane >= base) & (lane < base + 8)
        r = jnp.where(in_panel, jnp.where(lane - base == sub, 1.0, 0.0).astype(F32), work[p])
        g = jnp.zeros((8, B), F32)
        for k in range(0, 8, 2):
            a, b, c = sub_row(t[k], k), sub_row(t[k], k + 1), sub_row(t[k + 1], k + 1)
            det = a * c - b * b
            inv = 1.0 / det
            pivot = (sub == k) | (sub == k + 1)
            t0 = jnp.where(pivot, jnp.where(sub == k, -1.0, 0.0).astype(F32), t[k])
            t1 = jnp.where(pivot, jnp.where(sub == k, 0.0, -1.0).astype(F32), t[k + 1])
            alpha = (t0 * c - t1 * b) * inv
            beta = (t1 * a - t0 * b) * inv
            x, y = sub_row(r, k), sub_row(r, k + 1)
            g0 = x * lax.rsqrt(a)
            g1 = (a * y - b * x) * lax.rsqrt(a * det)
            g = jnp.where(sub == k, g0, jnp.where(sub == k + 1, g1, g))
            r = jnp.where(pivot, 0.0, r) - alpha * x - beta * y
            for j in range(k + 2, 8):
                t[j] = jnp.where(pivot, 0.0, t[j]) - alpha * sub_row(t[j], k) - beta * sub_row(t[j], k + 1)
        out.append(jnp.where(lane <= sub + base, g, 0.0))
        z = [sub_row(r, j) for j in range(8)]
        for q in range(p + 1, len(rows)):
            acc = jnp.where(in_panel, 0.0, work[q])
            for j in range(8):
                acc = acc - cols[q][j] * z[j]
            work[q] = acc
    return out


def eliminate(w, g, y, k0, k1, blocks):
    for k in range(k0, k1):
        lo = B * k
        rows = [w[lo + 8 * q : lo + 8 * q + 8, lo : lo + B] for q in range(B // 8)]
        for q, piece in enumerate(inverse_factor(rows)):
            g[8 * q : 8 * q + 8, :] = piece
        y[...] = jnp.dot(g[...], w[lo : lo + B, :], precision=HIGHEST, preferred_element_type=F32)
        y[:, lo : lo + B] = g[...]
        w[lo : lo + B, :] = y[...]

        def body(i, carry):
            at = pl.multiple_of(i * B, B)
            w[pl.ds(at, B), lo : lo + B] = jnp.zeros((B, B), F32)
            w[pl.ds(at, B), :] -= lax.dot_general(
                y[:, pl.ds(at, B)], y[...], (((0,), (0,)), ((), ())), precision=HIGHEST, preferred_element_type=F32
            )
            return carry

        if k + 1 < blocks:
            lax.fori_loop(k + 1, blocks, body, 0)


def first_kernel(k1, blocks, masks, place, near, far, w, g, y):
    height, width = near.shape[1:]
    me_row, me_col = place[0], place[1]
    core = me_row % 2
    for m, (even, odd) in enumerate(masks):
        for flip, buf in ((0, near), (1, far)):
            odd_core = (core + flip) % 2
            row = (me_row ^ flip) ^ jnp.where(odd_core == 0, even[0], odd[0])
            col = me_col ^ jnp.where(odd_core == 0, even[1], odd[1])
            w[pl.ds(pl.multiple_of(row * height, 8), height), pl.ds(pl.multiple_of(col * width, B), width)] = buf[m]
    eliminate(w, g, y, 0, k1, blocks)


def whole_kernel(k1, blocks, w_in, w, g, y):
    w[...] = w_in[...]
    eliminate(w, g, y, 0, k1, blocks)


def next_kernel(k0, k1, blocks, w_in, w, g, y):
    w[...] = w_in[...]
    eliminate(w, g, y, k0, k1, blocks)


VM = pl.BlockSpec(memory_space=pltpu.VMEM)
SM = pl.BlockSpec(memory_space=pltpu.SMEM)


def elimination_call(kernel, order, specs, args):
    return pl.pallas_call(
        kernel,
        out_shape=jax.ShapeDtypeStruct((order, order), F32),
        in_specs=specs,
        out_specs=VM,
        scratch_shapes=[pltpu.VMEM((B, B), F32), pltpu.VMEM((B, order), F32)],
        compiler_params=pltpu.CompilerParams(vmem_limit_bytes=20 * MIB),
        cost_estimate=pl.CostEstimate(flops=4 * 10**9, bytes_accessed=8 * MIB, transcendentals=0),
    )(*args)


def split(v):
    high = v.astype(BF16)
    return high, (v - high.astype(F32)).astype(BF16)


def dot_tt(a, b):
    return lax.dot_general(a, b, (((1,), (1,)), ((), ())), preferred_element_type=F32)


def solve_kernel(masks, joined, n_own, n_all, width_cols, rank_max, *refs):
    if joined:
        inv, own, tgt, solved, core, xh, xl, ih, il, sh, sl = refs
    else:
        place, inv, own, near, far, solved, core, xh, xl, ih, il, sh, sl = refs
    blocks = inv.shape[0] // B
    for i in range(blocks):
        rows = slice(B * i, B * i + B)
        wide = B * (i + 1)
        ih[rows, :wide], il[rows, :wide] = split(inv[rows, :wide])
        if i % 2 == 0:
            ih[rows, wide : wide + B] = jnp.zeros((B, B), BF16)
            il[rows, wide : wide + B] = jnp.zeros((B, B), BF16)
    for c in range(blocks):
        xh[:n_own, B * c : B * c + B], xl[:n_own, B * c : B * c + B] = split(own[c])
        if joined:
            xh[n_own:, B * c : B * c + B], xl[n_own:, B * c : B * c + B] = split(tgt[c])
    if not joined:
        height, width = near.shape[1:]
        me_row, me_col = place[0], place[1]
        core_bit = me_row % 2
        for m, (even, odd) in enumerate(masks):
            for flip, buf in ((0, near), (1, far)):
                odd_core = (core_bit + flip) % 2
                row = (me_row ^ flip) ^ jnp.where(odd_core == 0, even[0], odd[0])
                col = me_col ^ jnp.where(odd_core == 0, even[1], odd[1])
                part = place[2 + row]
                high, low = split(buf[m])
                at = (pl.ds(pl.multiple_of(n_own + part * height, 16), height), pl.ds(pl.multiple_of(col * width, B), width))
                xh[at] = high
                xl[at] = low
    own_rows, tgt_rows = slice(0, n_own), (n_all - n_own) // 2

    def rows_of(at, keep):
        for i in range(blocks // 2):
            deep = 2 * B * (i + 1)
            out = slice(2 * B * i, deep)
            h, l = xh[at, :deep], xl[at, :deep]
            gh, gl = ih[out, :deep], il[out, :deep]
            res = dot_tt(h, gh) + dot_tt(h, gl) + dot_tt(l, gh)
            sh[at, out], sl[at, out] = split(res)
            if keep:
                solved[2 * i] = res[:, :B]
                solved[2 * i + 1] = res[:, B:]

    rows_of(own_rows, True)

    def body(t, carry):
        rows_of(pl.ds(pl.multiple_of(n_own + t * tgt_rows, 16), tgt_rows), False)
        return carry

    lax.fori_loop(0, 2, body, 0)
    oh, ol = sh.at[:n_own], sl.at[:n_own]

    def core_body(j, carry):
        at = pl.ds(pl.multiple_of(n_own + 2 * j * rank_max, 16), 2 * rank_max)
        h, l = sh[at, :], sl[at, :]
        res = dot_tt(oh[...], h) + dot_tt(oh[...], l) + dot_tt(ol[...], h)
        core[2 * j, :, :rank_max] = res[:, :rank_max]
        core[2 * j + 1, :, :rank_max] = res[:, rank_max:]
        return carry

    lax.fori_loop(0, width_cols // 2, core_body, 0)


def rows_iota(shape):
    return lax.broadcasted_iota(jnp.int32, shape, 0)


def aligned(i):
    return pl.multiple_of(i, 8)


def pack_kernel(offs, ranks, t_slot, t_rank, left, right, v, ua, ub, t, pv, pu):
    slots, rank_max, width = right.shape
    total, half = v.shape[0], ua.shape[0]
    rows = rows_iota((rank_max, width))
    for j in range(t.shape[0]):
        t[j] = jnp.where(rows < t_rank[j], right[t_slot[j]], 0.0)
    pv[...] = jnp.zeros_like(pv)
    pu[...] = jnp.zeros_like(pu)
    for s in range(slots):
        at = pl.ds(aligned(offs[s]), rank_max)
        keep = rows < ranks[s]
        pv[at, :] = jnp.where(keep, right[s], 0.0)
        pu[at, :] = jnp.where(keep, left[s], 0.0)
    v[...] = pv[:total]
    ua[...] = pu[:half]
    ub[...] = pu[half:total]


def unpack_kernel(offs, ranks, packed, out, held):
    slots, rank_max, width = out.shape
    held[: packed.shape[0]] = packed[...]
    rows = rows_iota((rank_max, width))
    for s in range(slots):
        out[s] = jnp.where(rows < ranks[s], held[pl.ds(aligned(offs[s]), rank_max), :], 0.0)


def update_kernel(n, group, spots, offs, ranks, tiles, col, core, *refs):
    pieces, out, us, cs, u, sems = refs[: 2 * n], refs[2 * n], refs[2 * n + 1], refs[2 * n + 2], refs[2 * n + 3], refs[2 * n + 4]
    step = pl.program_id(0)
    rank_max = out.shape[2]
    half = pieces[0].shape[0]
    total = 2 * half

    @pl.when(step == 0)
    def _():
        copies = [pltpu.make_async_copy(core, cs.at[:total], sems.at[2 * n])]
        for i, piece in enumerate(pieces):
            lo = 0 if i < n else half
            copies.append(pltpu.make_async_copy(piece, us.at[spots[i], lo : lo + half], sems.at[i]))
        for c in copies:
            c.start()
        us[:, total:] = jnp.zeros((n, rank_max, B), F32)
        for c in copies:
            c.wait()

    rows = rows_iota((rank_max, B))
    for s in range(group):
        slot = step * group + s
        at = pl.ds(aligned(offs[slot]), rank_max)
        for k in range(n):
            lanes = slice(B * k, B * k + B)
            u[:rank_max, lanes], u[rank_max:, lanes] = split(us[k, at, :])
        keep = rows < jnp.where(tiles[slot] >= col[0], ranks[slot], 0)
        c = jnp.where(keep, cs[at, :], 0.0)
        ch, cl = split(jnp.transpose(c)[:rank_max])
        w = u[...]
        res = jnp.dot(jnp.concatenate([ch, ch], axis=1), w, preferred_element_type=F32)
        out[s, 0] = res + jnp.dot(cl, w[:rank_max], preferred_element_type=F32)


def phases(rows, cols):
    even = []
    bit = cols // 2
    while bit > 1:
        even.append((0, bit))
        bit //= 2
    bit = rows // 2
    while bit > 2:
        even.append((bit, 0))
        bit //= 2
    odd = even + [(2, 0), (0, 1)]
    even = even + [(0, 1), (2, 0)]
    return even, odd


def gather_masks(rows, cols):
    even, odd = phases(rows, cols)

    def masks(steps):
        got = [(0, 0)]
        for r, c in steps:
            got = got + [(a ^ r, b ^ c) for a, b in got]
        return got

    return list(zip(masks(even), masks(odd)))


def link_pairs(rows, cols, even, odd):
    pairs = []
    for r in range(rows):
        dr, dc = odd if r % 2 else even
        for c in range(cols):
            pairs.append((r * cols + c, (r ^ dr) * cols + (c ^ dc)))
    return pairs


def tie(*values):
    return lax.optimization_barrier(values)


def ring_order(n):
    return list(range(0, n, 2)) + list(range(n - 1, 0, -2))


def table(values, index):
    return jnp.array(values, jnp.int32)[index]


def body(rows, cols, total, args):
    diag_tile, left, right, ranks, tile_rows = args
    slots, rank_max, piece_rows = left.shape
    order = piece_rows * cols
    blocks = order // B
    group = slots // cols
    n_own, n_tgt, half = total // cols, cols * rank_max, total // 2
    n_all = n_own + n_tgt
    row_index = lax.axis_index("row")
    col_index = lax.axis_index("col")
    masks = gather_masks(rows, cols)
    fits = piece_rows % B == 0 and blocks == cols
    own_ranks = lax.dynamic_slice_in_dim(ranks, row_index * slots, slots)
    own_tiles = lax.dynamic_slice_in_dim(tile_rows, row_index * slots, slots)
    padded = (own_ranks + 7) // 8 * 8
    before = jnp.arange(slots, dtype=jnp.int32)
    offs = jnp.sum(jnp.where(before[None, :] < before[:, None], padded[None, :], 0), axis=1)
    wanted = jnp.arange(cols, dtype=jnp.int32)
    every_slot = jnp.arange(tile_rows.shape[0], dtype=jnp.int32)
    hit = tile_rows[None, :] == wanted[:, None]
    holder = jnp.sum(jnp.where(hit, every_slot[None, :], 0), axis=1)
    t_rank = jnp.sum(jnp.where(hit, ranks[None, :], 0), axis=1)
    t_rank = jnp.where(holder // slots == row_index, t_rank, 0)

    v, a, b, part = pl.pallas_call(
        pack_kernel,
        out_shape=[
            jax.ShapeDtypeStruct((total, piece_rows), F32),
            jax.ShapeDtypeStruct((half, piece_rows), F32),
            jax.ShapeDtypeStruct((half, piece_rows), F32),
            jax.ShapeDtypeStruct((cols, rank_max, piece_rows), F32),
        ],
        in_specs=[SM] * 4 + [VM] * 2,
        out_specs=[VM] * 4,
        scratch_shapes=[pltpu.VMEM((total + rank_max, piece_rows), F32)] * 2,
        compiler_params=pltpu.CompilerParams(vmem_limit_bytes=24 * MIB),
    )(offs, own_ranks, holder % slots, t_rank, left, right)

    cycle = ring_order(cols)
    forward = [(cycle[i], cycle[(i + 1) % cols]) for i in range(cols)]
    backward = [(y, x) for x, y in forward]
    fw, bw = [a], [b]

    def ring_step():
        fw.append(lax.ppermute(fw[-1], "col", forward))
        bw.append(lax.ppermute(bw[-1], "col", backward))

    even, odd = phases(rows, cols)
    links = len(even)
    swap = [(r, r ^ 1) for r in range(rows)]

    t_steps = []
    bit = 1
    while bit < rows:
        t_steps.append(("sum", bit))
        bit *= 2
    t_steps += [("link", i) for i in range(links)] + [("core", 0)]
    state = dict(part=part, t=None, t_far=None)

    def t_step():
        if not t_steps:
            return
        kind, which = t_steps.pop(0)
        if kind == "sum":
            p = state["part"]
            h = p.shape[0] // 2
            side = (row_index // which) % 2
            kept = lax.dynamic_slice_in_dim(p, side * h, h, 0)
            sent = lax.dynamic_slice_in_dim(p, (1 - side) * h, h, 0)
            state["part"] = kept + lax.ppermute(sent, "row", [(r, r ^ which) for r in range(rows)])
            if t_steps[0][0] == "link":
                p = state["part"]
                state["per"] = p.shape[0]
                state["t"] = p.reshape(1, p.shape[0] * rank_max, piece_rows)
        elif kind == "link":
            t = state["t"]
            got = lax.ppermute(t, ("row", "col"), link_pairs(rows, cols, even[which], odd[which]))
            state["t"] = jnp.concatenate([t, got], axis=0)
        else:
            state["t_far"] = lax.ppermute(state["t"], "row", swap)

    def t_tie(x):
        key = "t" if state["t"] is not None else "part"
        x, state[key] = tie(x, state[key])
        return x

    near = diag_tile[None]
    ring_step()
    for i in range(links):
        got = lax.ppermute(near, ("row", "col"), link_pairs(rows, cols, even[i], odd[i]))
        t_step()
        near = jnp.concatenate([near, got], axis=0)
        near = t_tie(near)
    near, fw[-1], bw[-1] = tie(near, fw[-1], bw[-1])
    far = lax.ppermute(near, "row", swap)
    t_step()
    far = t_tie(far)

    far, v = tie(far, v)
    own = lax.all_to_all(v.reshape(cols, n_own, piece_rows), "col", split_axis=0, concat_axis=0, tiled=True)

    places = []
    for r in range(rows):
        at, h, bb = 0, rows // 2, 1
        while bb < rows:
            at += h * ((r // bb) % 2)
            h //= 2
            bb *= 2
        places.append(at)

    def sources():
        near_m = jnp.where(row_index % 2 == 0, table([e for e, _ in masks], slice(None)), table([o for _, o in masks], slice(None)))
        far_m = jnp.where(row_index % 2 == 0, table([o for _, o in masks], slice(None)), table([e for e, _ in masks], slice(None)))
        r = jnp.concatenate([row_index ^ near_m[:, 0], row_index ^ 1 ^ far_m[:, 0]])
        c = jnp.concatenate([col_index ^ near_m[:, 1], col_index ^ far_m[:, 1]])
        return r, c

    place = jnp.concatenate([jnp.stack([row_index, col_index]).astype(jnp.int32), jnp.array(places, jnp.int32)])
    per_call = 2
    t_step()
    if fits:
        inv = elimination_call(
            functools.partial(first_kernel, per_call, blocks, masks), order, [SM, VM, VM], (place, near, far)
        )
    else:
        r, c = sources()
        pieces = jnp.concatenate([near, far], axis=0)
        tile = jnp.zeros((rows * cols,) + pieces.shape[1:], F32).at[r * cols + c].set(pieces)
        tile = tile.reshape(rows, cols, order // rows, piece_rows).transpose(0, 2, 1, 3).reshape(order, order)
        inv = elimination_call(functools.partial(whole_kernel, per_call, blocks), order, [VM], (tile,))
    inv = t_tie(inv)
    for k in range(per_call, blocks, per_call):
        while t_steps:
            t_step()
        if RING_AT(k // per_call):
            inv, fw[-1], bw[-1] = tie(inv, fw[-1], bw[-1])
            ring_step()
        inv = elimination_call(functools.partial(next_kernel, k, k + per_call, blocks), order, [VM], (inv,))
    t_near, t_far = state["t"], state["t_far"]
    per = state["per"]

    inv, fw[-1], bw[-1] = tie(inv, fw[-1], bw[-1])
    ring_step()
    own = own.reshape(cols, n_own, piece_rows)
    if fits:
        specs, operands = [SM, VM, VM, VM, VM], (place, inv, own, t_near, t_far)
    else:
        own = own.transpose(1, 0, 2).reshape(n_own, blocks, B).transpose(1, 0, 2)
        r, c = sources()
        spots = table(places, r)
        pieces = jnp.concatenate([t_near, t_far], axis=0)
        tgt = jnp.zeros((rows * cols,) + pieces.shape[1:], F32).at[spots * cols + c].set(pieces)
        tgt = tgt.reshape(rows, cols, per * rank_max, piece_rows).transpose(0, 2, 1, 3).reshape(n_tgt, blocks, B)
        specs, operands = [VM, VM, VM], (inv, own, tgt.transpose(1, 0, 2))
    solved, core = pl.pallas_call(
        functools.partial(solve_kernel, masks, not fits, n_own, n_all, cols, rank_max),
        out_shape=[
            jax.ShapeDtypeStruct((blocks, n_own, B), F32),
            jax.ShapeDtypeStruct((cols, n_own, B), F32),
        ],
        in_specs=specs,
        out_specs=[VM, VM],
        scratch_shapes=[pltpu.VMEM((n_all, order), BF16)] * 2
        + [pltpu.VMEM((order, order), BF16)] * 2
        + [pltpu.VMEM((n_all, order), BF16)] * 2,
        compiler_params=pltpu.CompilerParams(vmem_limit_bytes=50 * MIB),
        cost_estimate=pl.CostEstimate(flops=6 * 10**9, bytes_accessed=12 * MIB, transcendentals=0),
    )(*operands)
    core = lax.all_to_all(core, "col", split_axis=0, concat_axis=0, tiled=True).reshape(total, B)
    if not fits:
        solved = solved.transpose(1, 0, 2).reshape(n_own, cols, piece_rows).transpose(1, 0, 2)
    while len(fw) < cols:
        ring_step()
    solved = tie(solved, fw[-2], bw[-2])[0]
    back = lax.all_to_all(solved, "col", split_axis=0, concat_axis=0, tiled=True).reshape(total, piece_rows)
    own_rows = pl.pallas_call(
        unpack_kernel,
        out_shape=jax.ShapeDtypeStruct((slots, rank_max, piece_rows), F32),
        in_specs=[SM, SM, VM],
        out_specs=VM,
        scratch_shapes=[pltpu.VMEM((total + rank_max, piece_rows), F32)],
        compiler_params=pltpu.CompilerParams(vmem_limit_bytes=16 * MIB),
    )(offs, own_ranks, back)

    spot = table([cycle.index(c) for c in range(cols)], col_index)
    cyc = table(cycle, slice(None))
    ks = jnp.arange(cols, dtype=jnp.int32)
    spots = jnp.concatenate([cyc[(spot - ks) % cols], cyc[(spot + ks) % cols]]).astype(jnp.int32)
    if fits:
        anyspec = pl.BlockSpec(memory_space=pl.ANY)
        update = pl.pallas_call(
            functools.partial(update_kernel, cols, group),
            out_shape=jax.ShapeDtypeStruct((slots, 1, rank_max, order), F32),
            grid_spec=pltpu.PrefetchScalarGridSpec(
                num_scalar_prefetch=5,
                grid=(cols,),
                in_specs=[anyspec] * (2 * cols + 1),
                out_specs=pl.BlockSpec((group, 1, rank_max, order), lambda c, *_: (c, 0, 0, 0)),
                scratch_shapes=[
                    pltpu.VMEM((cols, total + rank_max, B), F32),
                    pltpu.VMEM((total + rank_max, B), F32),
                    pltpu.VMEM((2 * rank_max, order), BF16),
                    pltpu.SemaphoreType.DMA((2 * cols + 1,)),
                ],
            ),
            compiler_params=pltpu.CompilerParams(vmem_limit_bytes=32 * MIB),
            cost_estimate=pl.CostEstimate(flops=2 * 10**9, bytes_accessed=24 * MIB, transcendentals=0),
        )(spots, offs, own_ranks, own_tiles, col_index[None].astype(jnp.int32), core, *fw, *bw)
        update = jnp.transpose(update, (0, 1, 3, 2))
    else:
        halves = []
        for i, ring in enumerate((fw, bw)):
            pieces = jnp.stack(ring)
            halves.append(jnp.zeros_like(pieces).at[spots[i * cols : (i + 1) * cols]].set(pieces))
        full = jnp.concatenate(halves, axis=1).transpose(1, 0, 2).reshape(total, order)
        index = offs[:, None] + jnp.arange(rank_max, dtype=jnp.int32)[None, :]
        index = jnp.minimum(index, total - 1)
        keep = (jnp.arange(rank_max, dtype=jnp.int32)[None, :] < own_ranks[:, None]) & (own_tiles >= col_index)[:, None]
        cs = jnp.where(keep[:, :, None], core[index][:, :, :rank_max], 0.0)
        update = jnp.einsum("srn,srq->snq", full[index], cs, precision=HIGHEST)[:, None]
    return (jnp.transpose(own_rows, (0, 2, 1)), update)


def RING_AT(i):
    return i != 2


def shards(rows, cols, diag_tile, panel_left, panel_right, ranks, tile_rows):
    slots, _, rank_max = panel_left.shape
    args = (diag_tile, jnp.transpose(panel_left, (0, 2, 1)), jnp.transpose(panel_right, (0, 2, 1)), ranks, tile_rows)
    most = slots * rank_max
    grain = 16 * cols
    some = -(-(most * 25) // (32 * grain)) * grain
    sums = jnp.sum(((ranks + 7) // 8 * 8).reshape(rows, slots), axis=1)
    return lax.cond(
        jnp.max(sums) <= some,
        functools.partial(body, rows, cols, some),
        functools.partial(body, rows, cols, most),
        args,
    )


def solution(mesh):
    return jax.shard_map(
        functools.partial(shards, mesh.shape["row"], mesh.shape["col"]),
        mesh=mesh,
        in_specs=(P("row", "col"), P("row", "col", None), P("row", "col", None), P(), P()),
        out_specs=(P("row", "col", None), P("row", "col", None, None)),
        check_vma=False,
    )
```

```python
import functools
import jax
import jax.numpy as jnp
from jax import lax
from jax.experimental import pallas as pl
from jax.experimental.pallas import tpu as pltpu
from jax.sharding import PartitionSpec as P

F32 = jnp.float32
BF16 = jnp.bfloat16
HIGHEST = lax.Precision.HIGHEST
B = 128
MIB = 2**20


def sub_row(v, k):
    return jnp.broadcast_to(v[k : k + 1, :], v.shape)


def lane_col(v, c):
    return jnp.broadcast_to(v[:, c : c + 1], v.shape)


def inverse_factor(rows):
    lane = lax.broadcasted_iota(jnp.int32, (8, B), 1)
    sub = lax.broadcasted_iota(jnp.int32, (8, B), 0)
    work, out = list(rows), []
    for p in range(len(rows)):
        base = 8 * p
        cols = {q: [lane_col(work[q], base + j) for j in range(8)] for q in range(p, len(rows))}
        t = list(cols[p])
        in_panel = (lane >= base) & (lane < base + 8)
        r = jnp.where(in_panel, jnp.where(lane - base == sub, 1.0, 0.0).astype(F32), work[p])
        g = jnp.zeros((8, B), F32)
        for k in range(0, 8, 2):
            a, b, c = sub_row(t[k], k), sub_row(t[k], k + 1), sub_row(t[k + 1], k + 1)
            det = a * c - b * b
            inv = 1.0 / det
            pivot = (sub == k) | (sub == k + 1)
            t0 = jnp.where(pivot, jnp.where(sub == k, -1.0, 0.0).astype(F32), t[k])
            t1 = jnp.where(pivot, jnp.where(sub == k, 0.0, -1.0).astype(F32), t[k + 1])
            alpha = (t0 * c - t1 * b) * inv
            beta = (t1 * a - t0 * b) * inv
            x, y = sub_row(r, k), sub_row(r, k + 1)
            g0 = x * lax.rsqrt(a)
            g1 = (a * y - b * x) * lax.rsqrt(a * det)
            g = jnp.where(sub == k, g0, jnp.where(sub == k + 1, g1, g))
            r = jnp.where(pivot, 0.0, r) - alpha * x - beta * y
            for j in range(k + 2, 8):
                t[j] = jnp.where(pivot, 0.0, t[j]) - alpha * sub_row(t[j], k) - beta * sub_row(t[j], k + 1)
        out.append(jnp.where(lane <= sub + base, g, 0.0))
        z = [sub_row(r, j) for j in range(8)]
        for q in range(p + 1, len(rows)):
            acc = jnp.where(in_panel, 0.0, work[q])
            for j in range(8):
                acc = acc - cols[q][j] * z[j]
            work[q] = acc
    return out


def eliminate(w, g, y, k0, k1, blocks):
    for k in range(k0, k1):
        lo = B * k
        rows = [w[lo + 8 * q : lo + 8 * q + 8, lo : lo + B] for q in range(B // 8)]
        for q, piece in enumerate(inverse_factor(rows)):
            g[8 * q : 8 * q + 8, :] = piece
        y[...] = jnp.dot(g[...], w[lo : lo + B, :], precision=HIGHEST, preferred_element_type=F32)
        y[:, lo : lo + B] = g[...]
        w[lo : lo + B, :] = y[...]

        def body(i, carry):
            at = pl.multiple_of(i * B, B)
            w[pl.ds(at, B), lo : lo + B] = jnp.zeros((B, B), F32)
            w[pl.ds(at, B), :] -= lax.dot_general(
                y[:, pl.ds(at, B)], y[...], (((0,), (0,)), ((), ())), precision=HIGHEST, preferred_element_type=F32
            )
            return carry

        if k + 1 < blocks:
            lax.fori_loop(k + 1, blocks, body, 0)


def first_kernel(k1, blocks, masks, place, near, far, w, g, y):
    height, width = near.shape[1:]
    me_row, me_col = place[0], place[1]
    core = me_row % 2
    for m, (even, odd) in enumerate(masks):
        for flip, buf in ((0, near), (1, far)):
            odd_core = (core + flip) % 2
            row = (me_row ^ flip) ^ jnp.where(odd_core == 0, even[0], odd[0])
            col = me_col ^ jnp.where(odd_core == 0, even[1], odd[1])
            w[pl.ds(pl.multiple_of(row * height, 8), height), pl.ds(pl.multiple_of(col * width, B), width)] = buf[m]
    eliminate(w, g, y, 0, k1, blocks)


def whole_kernel(k1, blocks, w_in, w, g, y):
    w[...] = w_in[...]
    eliminate(w, g, y, 0, k1, blocks)


def next_kernel(k0, k1, blocks, w_in, w, g, y):
    w[...] = w_in[...]
    eliminate(w, g, y, k0, k1, blocks)


VM = pl.BlockSpec(memory_space=pltpu.VMEM)
SM = pl.BlockSpec(memory_space=pltpu.SMEM)


def elimination_call(kernel, order, specs, args):
    return pl.pallas_call(
        kernel,
        out_shape=jax.ShapeDtypeStruct((order, order), F32),
        in_specs=specs,
        out_specs=VM,
        scratch_shapes=[pltpu.VMEM((B, B), F32), pltpu.VMEM((B, order), F32)],
        compiler_params=pltpu.CompilerParams(vmem_limit_bytes=20 * MIB),
        cost_estimate=pl.CostEstimate(flops=4 * 10**9, bytes_accessed=8 * MIB, transcendentals=0),
    )(*args)


def split(v):
    high = v.astype(BF16)
    return high, (v - high.astype(F32)).astype(BF16)


def dot_tt(a, b):
    return lax.dot_general(a, b, (((1,), (1,)), ((), ())), preferred_element_type=F32)


def solve_kernel(masks, joined, n_own, n_all, width_cols, rank_max, *refs):
    if joined:
        inv, own, tgt, solved, core, xh, xl, ih, il, sh, sl = refs
    else:
        place, inv, own, near, far, solved, core, xh, xl, ih, il, sh, sl = refs
    blocks = inv.shape[0] // B
    for i in range(blocks):
        rows = slice(B * i, B * i + B)
        wide = B * (i + 1)
        ih[rows, :wide], il[rows, :wide] = split(inv[rows, :wide])
        if i % 2 == 0:
            ih[rows, wide : wide + B] = jnp.zeros((B, B), BF16)
            il[rows, wide : wide + B] = jnp.zeros((B, B), BF16)
    for c in range(blocks):
        xh[:n_own, B * c : B * c + B], xl[:n_own, B * c : B * c + B] = split(own[c])
        if joined:
            xh[n_own:, B * c : B * c + B], xl[n_own:, B * c : B * c + B] = split(tgt[c])
    if not joined:
        height, width = near.shape[1:]
        me_row, me_col = place[0], place[1]
        core_bit = me_row % 2
        for m, (even, odd) in enumerate(masks):
            for flip, buf in ((0, near), (1, far)):
                odd_core = (core_bit + flip) % 2
                row = (me_row ^ flip) ^ jnp.where(odd_core == 0, even[0], odd[0])
                col = me_col ^ jnp.where(odd_core == 0, even[1], odd[1])
                part = place[2 + row]
                high, low = split(buf[m])
                at = (pl.ds(pl.multiple_of(n_own + part * height, 16), height), pl.ds(pl.multiple_of(col * width, B), width))
                xh[at] = high
                xl[at] = low
    own_rows, tgt_rows = slice(0, n_own), (n_all - n_own) // 2

    def rows_of(at, keep):
        for i in range(blocks // 2):
            deep = 2 * B * (i + 1)
            out = slice(2 * B * i, deep)
            h, l = xh[at, :deep], xl[at, :deep]
            gh, gl = ih[out, :deep], il[out, :deep]
            res = dot_tt(h, gh) + dot_tt(h, gl) + dot_tt(l, gh)
            sh[at, out], sl[at, out] = split(res)
            if keep:
                solved[2 * i] = res[:, :B]
                solved[2 * i + 1] = res[:, B:]

    rows_of(own_rows, True)

    def body(t, carry):
        rows_of(pl.ds(pl.multiple_of(n_own + t * tgt_rows, 16), tgt_rows), False)
        return carry

    lax.fori_loop(0, 2, body, 0)
    oh, ol = sh.at[:n_own], sl.at[:n_own]

    def core_body(j, carry):
        at = pl.ds(pl.multiple_of(n_own + 2 * j * rank_max, 16), 2 * rank_max)
        h, l = sh[at, :], sl[at, :]
        res = dot_tt(oh[...], h) + dot_tt(oh[...], l) + dot_tt(ol[...], h)
        core[2 * j, :, :rank_max] = res[:, :rank_max]
        core[2 * j + 1, :, :rank_max] = res[:, rank_max:]
        return carry

    lax.fori_loop(0, width_cols // 2, core_body, 0)


def rows_iota(shape):
    return lax.broadcasted_iota(jnp.int32, shape, 0)


def aligned(i):
    return pl.multiple_of(i, 8)


def pack_kernel(offs, ranks, t_slot, t_rank, left, right, v, u, t, pv, pu):
    slots, rank_max, width = right.shape
    total = v.shape[0]
    rows = rows_iota((rank_max, width))
    for j in range(t.shape[0]):
        t[j] = jnp.where(rows < t_rank[j], right[t_slot[j]], 0.0)
    pv[...] = jnp.zeros_like(pv)
    pu[...] = jnp.zeros_like(pu)
    for s in range(slots):
        at = pl.ds(aligned(offs[s]), rank_max)
        keep = rows < ranks[s]
        pv[at, :] = jnp.where(keep, right[s], 0.0)
        pu[at, :] = jnp.where(keep, left[s], 0.0)
    v[...] = pv[:total]
    u[...] = pu[:total]


def unpack_kernel(offs, ranks, packed, out, held):
    slots, rank_max, width = out.shape
    held[: packed.shape[0]] = packed[...]
    rows = rows_iota((rank_max, width))
    for s in range(slots):
        out[s] = jnp.where(rows < ranks[s], held[pl.ds(aligned(offs[s]), rank_max), :], 0.0)


def update_kernel(n, group, count, spots, offs, ranks, tiles, col, core, *refs):
    pieces, (out, us, cs, u, sems) = refs[:count], refs[count:]
    step = pl.program_id(0)
    rank_max = out.shape[2]
    total = pieces[0].shape[0]

    @pl.when(step == 0)
    def _():
        def fetch(i):
            return pltpu.make_async_copy(pieces[i], us.at[jnp.maximum(spots[i], 0), :total], sems.at[i])

        cores = pltpu.make_async_copy(core, cs.at[:total], sems.at[count])
        cores.start()
        for i in range(count):
            pl.when(spots[i] >= 0)(fetch(i).start)
        us[:, total:] = jnp.zeros((n, rank_max, B), F32)
        cores.wait()
        for i in range(count):
            pl.when(spots[i] >= 0)(fetch(i).wait)

    rows = rows_iota((rank_max, B))
    for s in range(group):
        slot = step * group + s
        at = pl.ds(aligned(offs[slot]), rank_max)
        for k in range(n):
            lanes = slice(B * k, B * k + B)
            u[:rank_max, lanes], u[rank_max:, lanes] = split(us[k, at, :])
        keep = rows < jnp.where(tiles[slot] >= col[0], ranks[slot], 0)
        c = jnp.where(keep, cs[at, :], 0.0)
        ch, cl = split(jnp.transpose(c)[:rank_max])
        w = u[...]
        res = jnp.dot(jnp.concatenate([ch, ch], axis=1), w, preferred_element_type=F32)
        out[s, 0] = res + jnp.dot(cl, w[:rank_max], preferred_element_type=F32)


def phases(rows, cols):
    even = []
    bit = cols // 2
    while bit > 1:
        even.append((0, bit))
        bit //= 2
    bit = rows // 2
    while bit > 2:
        even.append((bit, 0))
        bit //= 2
    odd = even + [(2, 0), (0, 1)]
    even = even + [(0, 1), (2, 0)]
    return even, odd


def gather_masks(rows, cols):
    even, odd = phases(rows, cols)

    def masks(steps):
        got = [(0, 0)]
        for r, c in steps:
            got = got + [(a ^ r, b ^ c) for a, b in got]
        return got

    return list(zip(masks(even), masks(odd)))


def link_pairs(rows, cols, even, odd):
    pairs = []
    for r in range(rows):
        dr, dc = odd if r % 2 else even
        for c in range(cols):
            pairs.append((r * cols + c, (r ^ dr) * cols + (c ^ dc)))
    return pairs


def tie(*values):
    return lax.optimization_barrier(values)


def table(values, index):
    return jnp.array(values, jnp.int32)[index]


def body(rows, cols, total, args):
    diag_tile, left, right, ranks, tile_rows = args
    slots, rank_max, piece_rows = left.shape
    order = piece_rows * cols
    blocks = order // B
    group = slots // cols
    n_own, n_tgt = total // cols, cols * rank_max
    n_all = n_own + n_tgt
    row_index = lax.axis_index("row")
    col_index = lax.axis_index("col")
    masks = gather_masks(rows, cols)
    fits = piece_rows % B == 0 and blocks == cols
    own_ranks = lax.dynamic_slice_in_dim(ranks, row_index * slots, slots)
    own_tiles = lax.dynamic_slice_in_dim(tile_rows, row_index * slots, slots)
    padded = (own_ranks + 7) // 8 * 8
    before = jnp.arange(slots, dtype=jnp.int32)
    offs = jnp.sum(jnp.where(before[None, :] < before[:, None], padded[None, :], 0), axis=1)
    wanted = jnp.arange(cols, dtype=jnp.int32)
    every_slot = jnp.arange(tile_rows.shape[0], dtype=jnp.int32)
    hit = tile_rows[None, :] == wanted[:, None]
    holder = jnp.sum(jnp.where(hit, every_slot[None, :], 0), axis=1)
    t_rank = jnp.sum(jnp.where(hit, ranks[None, :], 0), axis=1)
    t_rank = jnp.where(holder // slots == row_index, t_rank, 0)

    v, u, part = pl.pallas_call(
        pack_kernel,
        out_shape=[
            jax.ShapeDtypeStruct((total, piece_rows), F32),
            jax.ShapeDtypeStruct((total, piece_rows), F32),
            jax.ShapeDtypeStruct((cols, rank_max, piece_rows), F32),
        ],
        in_specs=[SM] * 4 + [VM] * 2,
        out_specs=[VM] * 3,
        scratch_shapes=[pltpu.VMEM((total + rank_max, piece_rows), F32)] * 2,
        compiler_params=pltpu.CompilerParams(vmem_limit_bytes=24 * MIB),
    )(offs, own_ranks, holder % slots, t_rank, left, right)

    length = cols // 2
    up, down, cross = [u], [u], []

    def along(step):
        if step < length:
            up.append(lax.ppermute(up[-1], "col", [(c, c + 2) for c in range(2 * step - 2, cols - 2)]))
            down.append(lax.ppermute(down[-1], "col", [(c + 2, c) for c in range(cols - 2 * step)]))

    def over(step):
        if 0 < step < length:
            cross.append(lax.ppermute(up[step], "col", [(c, c ^ 1) for c in range(2 * step, cols)]))
            cross.append(lax.ppermute(down[step], "col", [(c, c ^ 1) for c in range(cols - 2 * step)]))

    def far_tie(x, step):
        if step < length:
            x, up[step], down[step] = tie(x, up[step], down[step])
        return x

    even, odd = phases(rows, cols)
    links = len(even)
    swap = [(r, r ^ 1) for r in range(rows)]

    t_steps = []
    bit = 1
    while bit < rows:
        t_steps.append(("sum", bit))
        bit *= 2
    t_steps += [("link", i) for i in range(links)] + [("core", 0)]
    state = dict(part=part, t=None, t_far=None)

    def t_step():
        if not t_steps:
            return
        kind, which = t_steps.pop(0)
        if kind == "sum":
            p = state["part"]
            h = p.shape[0] // 2
            side = (row_index // which) % 2
            kept = lax.dynamic_slice_in_dim(p, side * h, h, 0)
            sent = lax.dynamic_slice_in_dim(p, (1 - side) * h, h, 0)
            state["part"] = kept + lax.ppermute(sent, "row", [(r, r ^ which) for r in range(rows)])
            if t_steps[0][0] == "link":
                p = state["part"]
                state["per"] = p.shape[0]
                state["t"] = p.reshape(1, p.shape[0] * rank_max, piece_rows)
        elif kind == "link":
            t = state["t"]
            got = lax.ppermute(t, ("row", "col"), link_pairs(rows, cols, even[which], odd[which]))
            state["t"] = jnp.concatenate([t, got], axis=0)
        else:
            state["t_far"] = lax.ppermute(state["t"], "row", swap)

    def t_tie(x):
        key = "t" if state["t"] is not None else "part"
        x, state[key] = tie(x, state[key])
        return x

    near = diag_tile[None]
    for i in range(links):
        got = lax.ppermute(near, ("row", "col"), link_pairs(rows, cols, even[i], odd[i]))
        t_step()
        near = jnp.concatenate([near, got], axis=0)
        near = t_tie(near)
        if i == 0:
            near, u = tie(near, u)
            up[0] = down[0] = u
            cross.append(lax.ppermute(u, "col", [(c, c ^ 1) for c in range(cols)]))
            along(1)
    far = lax.ppermute(near, "row", swap)
    t_step()
    far = t_tie(far)

    far, v = tie(far, v)
    own = lax.all_to_all(v.reshape(cols, n_own, piece_rows), "col", split_axis=0, concat_axis=0, tiled=True)

    places = []
    for r in range(rows):
        at, h, bb = 0, rows // 2, 1
        while bb < rows:
            at += h * ((r // bb) % 2)
            h //= 2
            bb *= 2
        places.append(at)

    def sources():
        near_m = jnp.where(row_index % 2 == 0, table([e for e, _ in masks], slice(None)), table([o for _, o in masks], slice(None)))
        far_m = jnp.where(row_index % 2 == 0, table([o for _, o in masks], slice(None)), table([e for e, _ in masks], slice(None)))
        r = jnp.concatenate([row_index ^ near_m[:, 0], row_index ^ 1 ^ far_m[:, 0]])
        c = jnp.concatenate([col_index ^ near_m[:, 1], col_index ^ far_m[:, 1]])
        return r, c

    place = jnp.concatenate([jnp.stack([row_index, col_index]).astype(jnp.int32), jnp.array(places, jnp.int32)])
    per_call = 2
    t_step()
    if fits:
        inv = elimination_call(
            functools.partial(first_kernel, per_call, blocks, masks), order, [SM, VM, VM], (place, near, far)
        )
    else:
        r, c = sources()
        pieces = jnp.concatenate([near, far], axis=0)
        tile = jnp.zeros((rows * cols,) + pieces.shape[1:], F32).at[r * cols + c].set(pieces)
        tile = tile.reshape(rows, cols, order // rows, piece_rows).transpose(0, 2, 1, 3).reshape(order, order)
        inv = elimination_call(functools.partial(whole_kernel, per_call, blocks), order, [VM], (tile,))
    inv = t_tie(inv)
    for k in range(per_call, blocks, per_call):
        while t_steps:
            t_step()
        if k == 2 * per_call:
            inv = far_tie(inv, 1)
            along(2)
            over(1)
        inv = elimination_call(functools.partial(next_kernel, k, k + per_call, blocks), order, [VM], (inv,))
    t_near, t_far = state["t"], state["t_far"]
    per = state["per"]

    inv = far_tie(inv, 2)
    along(3)
    over(2)
    own = own.reshape(cols, n_own, piece_rows)
    if fits:
        specs, operands = [SM, VM, VM, VM, VM], (place, inv, own, t_near, t_far)
    else:
        own = own.transpose(1, 0, 2).reshape(n_own, blocks, B).transpose(1, 0, 2)
        r, c = sources()
        spots = table(places, r)
        pieces = jnp.concatenate([t_near, t_far], axis=0)
        tgt = jnp.zeros((rows * cols,) + pieces.shape[1:], F32).at[spots * cols + c].set(pieces)
        tgt = tgt.reshape(rows, cols, per * rank_max, piece_rows).transpose(0, 2, 1, 3).reshape(n_tgt, blocks, B)
        specs, operands = [VM, VM, VM], (inv, own, tgt.transpose(1, 0, 2))
    solved, core = pl.pallas_call(
        functools.partial(solve_kernel, masks, not fits, n_own, n_all, cols, rank_max),
        out_shape=[
            jax.ShapeDtypeStruct((blocks, n_own, B), F32),
            jax.ShapeDtypeStruct((cols, n_own, B), F32),
        ],
        in_specs=specs,
        out_specs=[VM, VM],
        scratch_shapes=[pltpu.VMEM((n_all, order), BF16)] * 2
        + [pltpu.VMEM((order, order), BF16)] * 2
        + [pltpu.VMEM((n_all, order), BF16)] * 2,
        compiler_params=pltpu.CompilerParams(vmem_limit_bytes=50 * MIB),
        cost_estimate=pl.CostEstimate(flops=6 * 10**9, bytes_accessed=12 * MIB, transcendentals=0),
    )(*operands)
    core = lax.all_to_all(core, "col", split_axis=0, concat_axis=0, tiled=True).reshape(total, B)
    if not fits:
        solved = solved.transpose(1, 0, 2).reshape(n_own, cols, piece_rows).transpose(1, 0, 2)
    for step in range(3, length):
        core = far_tie(core, step)
        along(step + 1)
        over(step)
    solved, core = tie(solved, core)
    back = lax.all_to_all(solved, "col", split_axis=0, concat_axis=0, tiled=True).reshape(total, piece_rows)
    own_rows = pl.pallas_call(
        unpack_kernel,
        out_shape=jax.ShapeDtypeStruct((slots, rank_max, piece_rows), F32),
        in_specs=[SM, SM, VM],
        out_specs=VM,
        scratch_shapes=[pltpu.VMEM((total + rank_max, piece_rows), F32)],
        compiler_params=pltpu.CompilerParams(vmem_limit_bytes=16 * MIB),
    )(offs, own_ranks, back)

    pieces = [u] + up[1:] + down[1:] + cross
    spots = [col_index]
    for flip in (0, 1):
        ups = [jnp.where(col_index >= 2 * k, (col_index - 2 * k) ^ flip, -1) for k in range(1, length)]
        downs = [jnp.where(col_index < cols - 2 * k, (col_index + 2 * k) ^ flip, -1) for k in range(1, length)]
        if flip:
            spots += [col_index ^ 1] + [x for pair in zip(ups, downs) for x in pair]
        else:
            spots += ups + downs
    spots = jnp.stack(spots).astype(jnp.int32)
    if fits:
        anyspec = pl.BlockSpec(memory_space=pl.ANY)
        update = pl.pallas_call(
            functools.partial(update_kernel, cols, group, len(pieces)),
            out_shape=jax.ShapeDtypeStruct((slots, 1, rank_max, order), F32),
            grid_spec=pltpu.PrefetchScalarGridSpec(
                num_scalar_prefetch=5,
                grid=(cols,),
                in_specs=[anyspec] * (len(pieces) + 1),
                out_specs=pl.BlockSpec((group, 1, rank_max, order), lambda c, *_: (c, 0, 0, 0)),
                scratch_shapes=[
                    pltpu.VMEM((cols, total + rank_max, B), F32),
                    pltpu.VMEM((total + rank_max, B), F32),
                    pltpu.VMEM((2 * rank_max, order), BF16),
                    pltpu.SemaphoreType.DMA((len(pieces) + 1,)),
                ],
            ),
            compiler_params=pltpu.CompilerParams(vmem_limit_bytes=60 * MIB),
            cost_estimate=pl.CostEstimate(flops=2 * 10**9, bytes_accessed=24 * MIB, transcendentals=0),
        )(spots, offs, own_ranks, own_tiles, col_index[None].astype(jnp.int32), core, *pieces)
        update = jnp.transpose(update, (0, 1, 3, 2))
    else:
        where = jnp.where(spots < 0, cols, spots)
        full = jnp.zeros((cols + 1, total, piece_rows), F32)
        for i, piece in enumerate(pieces):
            full = lax.dynamic_update_index_in_dim(full, piece, where[i], 0)
        full = full[:cols].transpose(1, 0, 2).reshape(total, order)
        index = offs[:, None] + jnp.arange(rank_max, dtype=jnp.int32)[None, :]
        index = jnp.minimum(index, total - 1)
        keep = (jnp.arange(rank_max, dtype=jnp.int32)[None, :] < own_ranks[:, None]) & (own_tiles >= col_index)[:, None]
        cs = jnp.where(keep[:, :, None], core[index][:, :, :rank_max], 0.0)
        update = jnp.einsum("srn,srq->snq", full[index], cs, precision=HIGHEST)[:, None]
    return (jnp.transpose(own_rows, (0, 2, 1)), update)


def shards(rows, cols, diag_tile, panel_left, panel_right, ranks, tile_rows):
    slots, _, rank_max = panel_left.shape
    args = (diag_tile, jnp.transpose(panel_left, (0, 2, 1)), jnp.transpose(panel_right, (0, 2, 1)), ranks, tile_rows)
    most = slots * rank_max
    grain = 16 * cols
    some = -(-(most * 25) // (32 * grain)) * grain
    sums = jnp.sum(((ranks + 7) // 8 * 8).reshape(rows, slots), axis=1)
    return lax.cond(
        jnp.max(sums) <= some,
        functools.partial(body, rows, cols, some),
        functools.partial(body, rows, cols, most),
        args,
    )


def solution(mesh):
    return jax.shard_map(
        functools.partial(shards, mesh.shape["row"], mesh.shape["col"]),
        mesh=mesh,
        in_specs=(P("row", "col"), P("row", "col", None), P("row", "col", None), P(), P()),
        out_specs=(P("row", "col", None), P("row", "col", None, None)),
        check_vma=False,
    )
```

```python
import functools
import jax
import jax.numpy as jnp
from jax import lax
from jax.experimental import pallas as pl
from jax.experimental.pallas import tpu as pltpu
from jax.sharding import PartitionSpec as P

F32 = jnp.float32
BF16 = jnp.bfloat16
HIGHEST = lax.Precision.HIGHEST
B = 128
MIB = 2**20


def sub_row(v, k):
    return jnp.broadcast_to(v[k : k + 1, :], v.shape)


def lane_col(v, c):
    return jnp.broadcast_to(v[:, c : c + 1], v.shape)


def inverse_factor(rows):
    lane = lax.broadcasted_iota(jnp.int32, (8, B), 1)
    sub = lax.broadcasted_iota(jnp.int32, (8, B), 0)
    work, out = list(rows), []
    for p in range(len(rows)):
        base = 8 * p
        cols = {q: [lane_col(work[q], base + j) for j in range(8)] for q in range(p, len(rows))}
        t = list(cols[p])
        in_panel = (lane >= base) & (lane < base + 8)
        r = jnp.where(in_panel, jnp.where(lane - base == sub, 1.0, 0.0).astype(F32), work[p])
        g = jnp.zeros((8, B), F32)
        for k in range(0, 8, 2):
            a, b, c = sub_row(t[k], k), sub_row(t[k], k + 1), sub_row(t[k + 1], k + 1)
            det = a * c - b * b
            inv = 1.0 / det
            pivot = (sub == k) | (sub == k + 1)
            t0 = jnp.where(pivot, jnp.where(sub == k, -1.0, 0.0).astype(F32), t[k])
            t1 = jnp.where(pivot, jnp.where(sub == k, 0.0, -1.0).astype(F32), t[k + 1])
            alpha = (t0 * c - t1 * b) * inv
            beta = (t1 * a - t0 * b) * inv
            x, y = sub_row(r, k), sub_row(r, k + 1)
            g0 = x * lax.rsqrt(a)
            g1 = (a * y - b * x) * lax.rsqrt(a * det)
            g = jnp.where(sub == k, g0, jnp.where(sub == k + 1, g1, g))
            r = jnp.where(pivot, 0.0, r) - alpha * x - beta * y
            for j in range(k + 2, 8):
                t[j] = jnp.where(pivot, 0.0, t[j]) - alpha * sub_row(t[j], k) - beta * sub_row(t[j], k + 1)
        out.append(jnp.where(lane <= sub + base, g, 0.0))
        z = [sub_row(r, j) for j in range(8)]
        for q in range(p + 1, len(rows)):
            acc = jnp.where(in_panel, 0.0, work[q])
            for j in range(8):
                acc = acc - cols[q][j] * z[j]
            work[q] = acc
    return out


def eliminate(w, g, y, k0, k1, blocks):
    for k in range(k0, k1):
        lo = B * k
        rows = [w[lo + 8 * q : lo + 8 * q + 8, lo : lo + B] for q in range(B // 8)]
        for q, piece in enumerate(inverse_factor(rows)):
            g[8 * q : 8 * q + 8, :] = piece
        y[...] = jnp.dot(g[...], w[lo : lo + B, :], precision=HIGHEST, preferred_element_type=F32)
        y[:, lo : lo + B] = g[...]
        w[lo : lo + B, :] = y[...]

        def body(i, carry):
            at = pl.multiple_of(i * B, B)
            w[pl.ds(at, B), lo : lo + B] = jnp.zeros((B, B), F32)
            w[pl.ds(at, B), :] -= lax.dot_general(
                y[:, pl.ds(at, B)], y[...], (((0,), (0,)), ((), ())), precision=HIGHEST, preferred_element_type=F32
            )
            return carry

        if k + 1 < blocks:
            lax.fori_loop(k + 1, blocks, body, 0)


def first_kernel(k1, blocks, masks, place, near, far, w, g, y):
    height, width = near.shape[1:]
    me_row, me_col = place[0], place[1]
    core = me_row % 2
    for m, (even, odd) in enumerate(masks):
        for flip, buf in ((0, near), (1, far)):
            odd_core = (core + flip) % 2
            row = (me_row ^ flip) ^ jnp.where(odd_core == 0, even[0], odd[0])
            col = me_col ^ jnp.where(odd_core == 0, even[1], odd[1])
            w[pl.ds(pl.multiple_of(row * height, 8), height), pl.ds(pl.multiple_of(col * width, B), width)] = buf[m]
    eliminate(w, g, y, 0, k1, blocks)


def whole_kernel(k1, blocks, w_in, w, g, y):
    w[...] = w_in[...]
    eliminate(w, g, y, 0, k1, blocks)


def next_kernel(k0, k1, blocks, w_in, w, g, y):
    w[...] = w_in[...]
    eliminate(w, g, y, k0, k1, blocks)


VM = pl.BlockSpec(memory_space=pltpu.VMEM)
SM = pl.BlockSpec(memory_space=pltpu.SMEM)


def elimination_call(kernel, order, specs, args):
    return pl.pallas_call(
        kernel,
        out_shape=jax.ShapeDtypeStruct((order, order), F32),
        in_specs=specs,
        out_specs=VM,
        scratch_shapes=[pltpu.VMEM((B, B), F32), pltpu.VMEM((B, order), F32)],
        compiler_params=pltpu.CompilerParams(vmem_limit_bytes=20 * MIB),
        cost_estimate=pl.CostEstimate(flops=4 * 10**9, bytes_accessed=8 * MIB, transcendentals=0),
    )(*args)


def split(v):
    high = v.astype(BF16)
    return high, (v - high.astype(F32)).astype(BF16)


def dot_tt(a, b):
    return lax.dot_general(a, b, (((1,), (1,)), ((), ())), preferred_element_type=F32)


def solve_kernel(masks, joined, n_own, n_all, width_cols, rank_max, *refs):
    if joined:
        inv, own, tgt, solved, core, xh, xl, ih, il, sh, sl = refs
    else:
        place, inv, own, near, far, solved, core, xh, xl, ih, il, sh, sl = refs
    blocks = inv.shape[0] // B
    for i in range(blocks):
        rows = slice(B * i, B * i + B)
        wide = B * (i + 1)
        ih[rows, :wide], il[rows, :wide] = split(inv[rows, :wide])
        if i % 2 == 0:
            ih[rows, wide : wide + B] = jnp.zeros((B, B), BF16)
            il[rows, wide : wide + B] = jnp.zeros((B, B), BF16)
    for c in range(blocks):
        xh[:n_own, B * c : B * c + B], xl[:n_own, B * c : B * c + B] = split(own[c])
        if joined:
            xh[n_own:, B * c : B * c + B], xl[n_own:, B * c : B * c + B] = split(tgt[c])
    if not joined:
        height, width = near.shape[1:]
        me_row, me_col = place[0], place[1]
        core_bit = me_row % 2
        for m, (even, odd) in enumerate(masks):
            for flip, buf in ((0, near), (1, far)):
                odd_core = (core_bit + flip) % 2
                row = (me_row ^ flip) ^ jnp.where(odd_core == 0, even[0], odd[0])
                col = me_col ^ jnp.where(odd_core == 0, even[1], odd[1])
                part = place[2 + row]
                high, low = split(buf[m])
                at = (pl.ds(pl.multiple_of(n_own + part * height, 16), height), pl.ds(pl.multiple_of(col * width, B), width))
                xh[at] = high
                xl[at] = low
    own_rows, tgt_rows = slice(0, n_own), (n_all - n_own) // 2

    def rows_of(at, keep):
        for i in range(blocks // 2):
            deep = 2 * B * (i + 1)
            out = slice(2 * B * i, deep)
            h, l = xh[at, :deep], xl[at, :deep]
            gh, gl = ih[out, :deep], il[out, :deep]
            res = dot_tt(h, gh) + dot_tt(h, gl) + dot_tt(l, gh)
            sh[at, out], sl[at, out] = split(res)
            if keep:
                solved[2 * i] = res[:, :B]
                solved[2 * i + 1] = res[:, B:]

    rows_of(own_rows, True)

    def body(t, carry):
        rows_of(pl.ds(pl.multiple_of(n_own + t * tgt_rows, 16), tgt_rows), False)
        return carry

    lax.fori_loop(0, 2, body, 0)
    oh, ol = sh.at[:n_own], sl.at[:n_own]

    def core_body(j, carry):
        at = pl.ds(pl.multiple_of(n_own + 2 * j * rank_max, 16), 2 * rank_max)
        h, l = sh[at, :], sl[at, :]
        res = dot_tt(oh[...], h) + dot_tt(oh[...], l) + dot_tt(ol[...], h)
        core[2 * j, :, :rank_max] = res[:, :rank_max]
        core[2 * j + 1, :, :rank_max] = res[:, rank_max:]
        return carry

    lax.fori_loop(0, width_cols // 2, core_body, 0)


def rows_iota(shape):
    return lax.broadcasted_iota(jnp.int32, shape, 0)


def aligned(i):
    return pl.multiple_of(i, 8)


def pack_kernel(offs, ranks, t_slot, t_rank, left, right, v, u, t, pv, pu):
    slots, rank_max, width = right.shape
    total = v.shape[0]
    rows = rows_iota((rank_max, width))
    for j in range(t.shape[0]):
        t[j] = jnp.where(rows < t_rank[j], right[t_slot[j]], 0.0)
    pv[...] = jnp.zeros_like(pv)
    pu[...] = jnp.zeros_like(pu)
    for s in range(slots):
        at = pl.ds(aligned(offs[s]), rank_max)
        keep = rows < ranks[s]
        pv[at, :] = jnp.where(keep, right[s], 0.0)
        pu[at, :] = jnp.where(keep, left[s], 0.0)
    v[...] = pv[:total]
    u[...] = pu[:total]


def unpack_kernel(offs, ranks, packed, out, held):
    slots, rank_max, width = out.shape
    held[: packed.shape[0]] = packed[...]
    rows = rows_iota((rank_max, width))
    for s in range(slots):
        out[s] = jnp.where(rows < ranks[s], held[pl.ds(aligned(offs[s]), rank_max), :], 0.0)


def update_kernel(n, group, count, spots, offs, ranks, tiles, col, core, *refs):
    pieces, (out, us, cs, u, sems) = refs[:count], refs[count:]
    step = pl.program_id(0)
    rank_max = out.shape[2]
    total = pieces[0].shape[0]

    @pl.when(step == 0)
    def _():
        def fetch(i):
            return pltpu.make_async_copy(pieces[i], us.at[jnp.maximum(spots[i], 0), :total], sems.at[i])

        cores = pltpu.make_async_copy(core, cs.at[:total], sems.at[count])
        cores.start()
        for i in range(count):
            pl.when(spots[i] >= 0)(fetch(i).start)
        us[:, total:] = jnp.zeros((n, rank_max, B), F32)
        cores.wait()
        for i in range(count):
            pl.when(spots[i] >= 0)(fetch(i).wait)

    rows = rows_iota((rank_max, B))
    for s in range(group):
        slot = step * group + s
        at = pl.ds(aligned(offs[slot]), rank_max)
        for k in range(n):
            lanes = slice(B * k, B * k + B)
            u[:rank_max, lanes], u[rank_max:, lanes] = split(us[k, at, :])
        keep = rows < jnp.where(tiles[slot] >= col[0], ranks[slot], 0)
        c = jnp.where(keep, cs[at, :], 0.0)
        ch, cl = split(jnp.transpose(c)[:rank_max])
        w = u[...]
        res = jnp.dot(jnp.concatenate([ch, ch], axis=1), w, preferred_element_type=F32)
        out[s, 0] = res + jnp.dot(cl, w[:rank_max], preferred_element_type=F32)


def phases(rows, cols):
    even = []
    bit = cols // 2
    while bit > 1:
        even.append((0, bit))
        bit //= 2
    bit = rows // 2
    while bit > 2:
        even.append((bit, 0))
        bit //= 2
    odd = even + [(2, 0), (0, 1)]
    even = even + [(0, 1), (2, 0)]
    return even, odd


def gather_masks(rows, cols):
    even, odd = phases(rows, cols)

    def masks(steps):
        got = [(0, 0)]
        for r, c in steps:
            got = got + [(a ^ r, b ^ c) for a, b in got]
        return got

    return list(zip(masks(even), masks(odd)))


def link_pairs(rows, cols, even, odd):
    pairs = []
    for r in range(rows):
        dr, dc = odd if r % 2 else even
        for c in range(cols):
            pairs.append((r * cols + c, (r ^ dr) * cols + (c ^ dc)))
    return pairs


def tie(*values):
    return lax.optimization_barrier(values)


def table(values, index):
    return jnp.array(values, jnp.int32)[index]


def body(rows, cols, total, args):
    diag_tile, left, right, ranks, tile_rows = args
    slots, rank_max, piece_rows = left.shape
    order = piece_rows * cols
    blocks = order // B
    group = slots // cols
    n_own, n_tgt = total // cols, cols * rank_max
    n_all = n_own + n_tgt
    row_index = lax.axis_index("row")
    col_index = lax.axis_index("col")
    masks = gather_masks(rows, cols)
    fits = piece_rows % B == 0 and blocks == cols
    own_ranks = lax.dynamic_slice_in_dim(ranks, row_index * slots, slots)
    own_tiles = lax.dynamic_slice_in_dim(tile_rows, row_index * slots, slots)
    padded = (own_ranks + 7) // 8 * 8
    before = jnp.arange(slots, dtype=jnp.int32)
    offs = jnp.sum(jnp.where(before[None, :] < before[:, None], padded[None, :], 0), axis=1)
    wanted = jnp.arange(cols, dtype=jnp.int32)
    every_slot = jnp.arange(tile_rows.shape[0], dtype=jnp.int32)
    hit = tile_rows[None, :] == wanted[:, None]
    holder = jnp.sum(jnp.where(hit, every_slot[None, :], 0), axis=1)
    t_rank = jnp.sum(jnp.where(hit, ranks[None, :], 0), axis=1)
    t_rank = jnp.where(holder // slots == row_index, t_rank, 0)

    v, u, part = pl.pallas_call(
        pack_kernel,
        out_shape=[
            jax.ShapeDtypeStruct((total, piece_rows), F32),
            jax.ShapeDtypeStruct((total, piece_rows), F32),
            jax.ShapeDtypeStruct((cols, rank_max, piece_rows), F32),
        ],
        in_specs=[SM] * 4 + [VM] * 2,
        out_specs=[VM] * 3,
        scratch_shapes=[pltpu.VMEM((total + rank_max, piece_rows), F32)] * 2,
        compiler_params=pltpu.CompilerParams(vmem_limit_bytes=24 * MIB),
    )(offs, own_ranks, holder % slots, t_rank, left, right)

    length = cols // 2
    up, down, cross = [u], [u], []

    def along(step):
        if step < length:
            up.append(lax.ppermute(up[-1], "col", [(c, c + 2) for c in range(2 * step - 2, cols - 2)]))
            down.append(lax.ppermute(down[-1], "col", [(c + 2, c) for c in range(cols - 2 * step)]))

    def over(step):
        if 0 < step < length:
            cross.append(lax.ppermute(up[step], "col", [(c, c ^ 1) for c in range(2 * step, cols)]))
            cross.append(lax.ppermute(down[step], "col", [(c, c ^ 1) for c in range(cols - 2 * step)]))

    def far_tie(x, step):
        if step < length:
            x, up[step], down[step] = tie(x, up[step], down[step])
        sent = slice(2 * step - 3, 2 * step - 1) if step > 1 else slice(0, 1)
        x, *cross[sent] = tie(x, *cross[sent])
        return x

    even, odd = phases(rows, cols)
    links = len(even)
    swap = [(r, r ^ 1) for r in range(rows)]

    t_steps = []
    bit = 1
    while bit < rows:
        t_steps.append(("sum", bit))
        bit *= 2
    t_steps += [("link", i) for i in range(links)] + [("core", 0)]
    state = dict(part=part, t=None, t_far=None)

    def t_step():
        if not t_steps:
            return
        kind, which = t_steps.pop(0)
        if kind == "sum":
            p = state["part"]
            h = p.shape[0] // 2
            side = (row_index // which) % 2
            kept = lax.dynamic_slice_in_dim(p, side * h, h, 0)
            sent = lax.dynamic_slice_in_dim(p, (1 - side) * h, h, 0)
            state["part"] = kept + lax.ppermute(sent, "row", [(r, r ^ which) for r in range(rows)])
            if t_steps[0][0] == "link":
                p = state["part"]
                state["per"] = p.shape[0]
                state["t"] = p.reshape(1, p.shape[0] * rank_max, piece_rows)
        elif kind == "link":
            t = state["t"]
            got = lax.ppermute(t, ("row", "col"), link_pairs(rows, cols, even[which], odd[which]))
            state["t"] = jnp.concatenate([t, got], axis=0)
        else:
            state["t_far"] = lax.ppermute(state["t"], "row", swap)

    def t_tie(x):
        key = "t" if state["t"] is not None else "part"
        x, state[key] = tie(x, state[key])
        return x

    near = diag_tile[None]
    for i in range(links):
        got = lax.ppermute(near, ("row", "col"), link_pairs(rows, cols, even[i], odd[i]))
        t_step()
        near = jnp.concatenate([near, got], axis=0)
        near = t_tie(near)
        if i == 0:
            near, u = tie(near, u)
            up[0] = down[0] = u
            cross.append(lax.ppermute(u, "col", [(c, c ^ 1) for c in range(cols)]))
            along(1)
    far = lax.ppermute(near, "row", swap)
    t_step()
    far = t_tie(far)

    far, v = tie(far, v)
    own = lax.all_to_all(v.reshape(cols, n_own, piece_rows), "col", split_axis=0, concat_axis=0, tiled=True)

    places = []
    for r in range(rows):
        at, h, bb = 0, rows // 2, 1
        while bb < rows:
            at += h * ((r // bb) % 2)
            h //= 2
            bb *= 2
        places.append(at)

    def sources():
        near_m = jnp.where(row_index % 2 == 0, table([e for e, _ in masks], slice(None)), table([o for _, o in masks], slice(None)))
        far_m = jnp.where(row_index % 2 == 0, table([o for _, o in masks], slice(None)), table([e for e, _ in masks], slice(None)))
        r = jnp.concatenate([row_index ^ near_m[:, 0], row_index ^ 1 ^ far_m[:, 0]])
        c = jnp.concatenate([col_index ^ near_m[:, 1], col_index ^ far_m[:, 1]])
        return r, c

    place = jnp.concatenate([jnp.stack([row_index, col_index]).astype(jnp.int32), jnp.array(places, jnp.int32)])
    per_call = 2
    t_step()
    if fits:
        inv = elimination_call(
            functools.partial(first_kernel, per_call, blocks, masks), order, [SM, VM, VM], (place, near, far)
        )
    else:
        r, c = sources()
        pieces = jnp.concatenate([near, far], axis=0)
        tile = jnp.zeros((rows * cols,) + pieces.shape[1:], F32).at[r * cols + c].set(pieces)
        tile = tile.reshape(rows, cols, order // rows, piece_rows).transpose(0, 2, 1, 3).reshape(order, order)
        inv = elimination_call(functools.partial(whole_kernel, per_call, blocks), order, [VM], (tile,))
    inv = t_tie(inv)
    for k in range(per_call, blocks, per_call):
        while t_steps:
            t_step()
        if k == per_call:
            inv = far_tie(inv, 1)
            along(2)
            over(1)
        inv = elimination_call(functools.partial(next_kernel, k, k + per_call, blocks), order, [VM], (inv,))
    t_near, t_far = state["t"], state["t_far"]
    per = state["per"]

    inv = far_tie(inv, 2)
    along(3)
    over(2)
    own = own.reshape(cols, n_own, piece_rows)
    if fits:
        specs, operands = [SM, VM, VM, VM, VM], (place, inv, own, t_near, t_far)
    else:
        own = own.transpose(1, 0, 2).reshape(n_own, blocks, B).transpose(1, 0, 2)
        r, c = sources()
        spots = table(places, r)
        pieces = jnp.concatenate([t_near, t_far], axis=0)
        tgt = jnp.zeros((rows * cols,) + pieces.shape[1:], F32).at[spots * cols + c].set(pieces)
        tgt = tgt.reshape(rows, cols, per * rank_max, piece_rows).transpose(0, 2, 1, 3).reshape(n_tgt, blocks, B)
        specs, operands = [VM, VM, VM], (inv, own, tgt.transpose(1, 0, 2))
    solved, core = pl.pallas_call(
        functools.partial(solve_kernel, masks, not fits, n_own, n_all, cols, rank_max),
        out_shape=[
            jax.ShapeDtypeStruct((blocks, n_own, B), F32),
            jax.ShapeDtypeStruct((cols, n_own, B), F32),
        ],
        in_specs=specs,
        out_specs=[VM, VM],
        scratch_shapes=[pltpu.VMEM((n_all, order), BF16)] * 2
        + [pltpu.VMEM((order, order), BF16)] * 2
        + [pltpu.VMEM((n_all, order), BF16)] * 2,
        compiler_params=pltpu.CompilerParams(vmem_limit_bytes=34 * MIB),
        cost_estimate=pl.CostEstimate(flops=6 * 10**9, bytes_accessed=12 * MIB, transcendentals=0),
    )(*operands)
    core = lax.all_to_all(core, "col", split_axis=0, concat_axis=0, tiled=True).reshape(total, B)
    if not fits:
        solved = solved.transpose(1, 0, 2).reshape(n_own, cols, piece_rows).transpose(1, 0, 2)
    for step in range(3, length):
        core = far_tie(core, step)
        along(step + 1)
        over(step)
    solved, core = tie(solved, core)
    back = lax.all_to_all(solved, "col", split_axis=0, concat_axis=0, tiled=True).reshape(total, piece_rows)
    own_rows = pl.pallas_call(
        unpack_kernel,
        out_shape=jax.ShapeDtypeStruct((slots, rank_max, piece_rows), F32),
        in_specs=[SM, SM, VM],
        out_specs=VM,
        scratch_shapes=[pltpu.VMEM((total + rank_max, piece_rows), F32)],
        compiler_params=pltpu.CompilerParams(vmem_limit_bytes=16 * MIB),
    )(offs, own_ranks, back)

    pieces = [u] + up[1:] + down[1:] + cross
    spots = [col_index]
    for flip in (0, 1):
        ups = [jnp.where(col_index >= 2 * k, (col_index - 2 * k) ^ flip, -1) for k in range(1, length)]
        downs = [jnp.where(col_index < cols - 2 * k, (col_index + 2 * k) ^ flip, -1) for k in range(1, length)]
        if flip:
            spots += [col_index ^ 1] + [x for pair in zip(ups, downs) for x in pair]
        else:
            spots += ups + downs
    spots = jnp.stack(spots).astype(jnp.int32)
    if fits:
        anyspec = pl.BlockSpec(memory_space=pl.ANY)
        update = pl.pallas_call(
            functools.partial(update_kernel, cols, group, len(pieces)),
            out_shape=jax.ShapeDtypeStruct((slots, 1, rank_max, order), F32),
            grid_spec=pltpu.PrefetchScalarGridSpec(
                num_scalar_prefetch=5,
                grid=(cols,),
                in_specs=[anyspec] * (len(pieces) + 1),
                out_specs=pl.BlockSpec((group, 1, rank_max, order), lambda c, *_: (c, 0, 0, 0)),
                scratch_shapes=[
                    pltpu.VMEM((cols, total + rank_max, B), F32),
                    pltpu.VMEM((total + rank_max, B), F32),
                    pltpu.VMEM((2 * rank_max, order), BF16),
                    pltpu.SemaphoreType.DMA((len(pieces) + 1,)),
                ],
            ),
            compiler_params=pltpu.CompilerParams(vmem_limit_bytes=60 * MIB),
            cost_estimate=pl.CostEstimate(flops=2 * 10**9, bytes_accessed=24 * MIB, transcendentals=0),
        )(spots, offs, own_ranks, own_tiles, col_index[None].astype(jnp.int32), core, *pieces)
        update = jnp.transpose(update, (0, 1, 3, 2))
    else:
        where = jnp.where(spots < 0, cols, spots)
        full = jnp.zeros((cols + 1, total, piece_rows), F32)
        for i, piece in enumerate(pieces):
            full = lax.dynamic_update_index_in_dim(full, piece, where[i], 0)
        full = full[:cols].transpose(1, 0, 2).reshape(total, order)
        index = offs[:, None] + jnp.arange(rank_max, dtype=jnp.int32)[None, :]
        index = jnp.minimum(index, total - 1)
        keep = (jnp.arange(rank_max, dtype=jnp.int32)[None, :] < own_ranks[:, None]) & (own_tiles >= col_index)[:, None]
        cs = jnp.where(keep[:, :, None], core[index][:, :, :rank_max], 0.0)
        update = jnp.einsum("srn,srq->snq", full[index], cs, precision=HIGHEST)[:, None]
    return (jnp.transpose(own_rows, (0, 2, 1)), update)


def shards(rows, cols, diag_tile, panel_left, panel_right, ranks, tile_rows):
    slots, _, rank_max = panel_left.shape
    args = (diag_tile, jnp.transpose(panel_left, (0, 2, 1)), jnp.transpose(panel_right, (0, 2, 1)), ranks, tile_rows)
    most = slots * rank_max
    grain = 16 * cols
    some = -(-(most * 25) // (32 * grain)) * grain
    sums = jnp.sum(((ranks + 7) // 8 * 8).reshape(rows, slots), axis=1)
    return lax.cond(
        jnp.max(sums) <= some,
        functools.partial(body, rows, cols, some),
        functools.partial(body, rows, cols, most),
        args,
    )


def solution(mesh):
    return jax.shard_map(
        functools.partial(shards, mesh.shape["row"], mesh.shape["col"]),
        mesh=mesh,
        in_specs=(P("row", "col"), P("row", "col", None), P("row", "col", None), P(), P()),
        out_specs=(P("row", "col", None), P("row", "col", None, None)),
        check_vma=False,
    )
```

```python
import functools
import jax
import jax.numpy as jnp
from jax import lax
from jax.experimental import pallas as pl
from jax.experimental.pallas import tpu as pltpu
from jax.sharding import PartitionSpec as P

F32 = jnp.float32
BF16 = jnp.bfloat16
HIGHEST = lax.Precision.HIGHEST
B = 128
MIB = 2**20


def sub_row(v, k):
    return jnp.broadcast_to(v[k : k + 1, :], v.shape)


def lane_col(v, c):
    return jnp.broadcast_to(v[:, c : c + 1], v.shape)


def inverse_factor(rows):
    lane = lax.broadcasted_iota(jnp.int32, (8, B), 1)
    sub = lax.broadcasted_iota(jnp.int32, (8, B), 0)
    work, out = list(rows), []
    for p in range(len(rows)):
        base = 8 * p
        cols = {q: [lane_col(work[q], base + j) for j in range(8)] for q in range(p, len(rows))}
        t = list(cols[p])
        in_panel = (lane >= base) & (lane < base + 8)
        r = jnp.where(in_panel, jnp.where(lane - base == sub, 1.0, 0.0).astype(F32), work[p])
        g = jnp.zeros((8, B), F32)
        for k in range(0, 8, 2):
            a, b, c = sub_row(t[k], k), sub_row(t[k], k + 1), sub_row(t[k + 1], k + 1)
            det = a * c - b * b
            inv = 1.0 / det
            pivot = (sub == k) | (sub == k + 1)
            t0 = jnp.where(pivot, jnp.where(sub == k, -1.0, 0.0).astype(F32), t[k])
            t1 = jnp.where(pivot, jnp.where(sub == k, 0.0, -1.0).astype(F32), t[k + 1])
            alpha = (t0 * c - t1 * b) * inv
            beta = (t1 * a - t0 * b) * inv
            x, y = sub_row(r, k), sub_row(r, k + 1)
            g0 = x * lax.rsqrt(a)
            g1 = (a * y - b * x) * lax.rsqrt(a * det)
            g = jnp.where(sub == k, g0, jnp.where(sub == k + 1, g1, g))
            r = jnp.where(pivot, 0.0, r) - alpha * x - beta * y
            for j in range(k + 2, 8):
                t[j] = jnp.where(pivot, 0.0, t[j]) - alpha * sub_row(t[j], k) - beta * sub_row(t[j], k + 1)
        out.append(jnp.where(lane <= sub + base, g, 0.0))
        z = [sub_row(r, j) for j in range(8)]
        for q in range(p + 1, len(rows)):
            acc = jnp.where(in_panel, 0.0, work[q])
            for j in range(8):
                acc = acc - cols[q][j] * z[j]
            work[q] = acc
    return out


def eliminate(w, g, y, k0, k1, blocks):
    for k in range(k0, k1):
        lo = B * k
        rows = [w[lo + 8 * q : lo + 8 * q + 8, lo : lo + B] for q in range(B // 8)]
        for q, piece in enumerate(inverse_factor(rows)):
            g[8 * q : 8 * q + 8, :] = piece
        y[...] = jnp.dot(g[...], w[lo : lo + B, :], precision=HIGHEST, preferred_element_type=F32)
        y[:, lo : lo + B] = g[...]
        w[lo : lo + B, :] = y[...]

        def body(i, carry):
            at = pl.multiple_of(i * B, B)
            w[pl.ds(at, B), lo : lo + B] = jnp.zeros((B, B), F32)
            w[pl.ds(at, B), :] -= lax.dot_general(
                y[:, pl.ds(at, B)], y[...], (((0,), (0,)), ((), ())), precision=HIGHEST, preferred_element_type=F32
            )
            return carry

        if k + 1 < blocks:
            lax.fori_loop(k + 1, blocks, body, 0)


def first_kernel(k1, blocks, masks, place, near, far, w, g, y):
    height, width = near.shape[1:]
    me_row, me_col = place[0], place[1]
    core = me_row % 2
    for m, (even, odd) in enumerate(masks):
        for flip, buf in ((0, near), (1, far)):
            odd_core = (core + flip) % 2
            row = (me_row ^ flip) ^ jnp.where(odd_core == 0, even[0], odd[0])
            col = me_col ^ jnp.where(odd_core == 0, even[1], odd[1])
            w[pl.ds(pl.multiple_of(row * height, 8), height), pl.ds(pl.multiple_of(col * width, B), width)] = buf[m]
    eliminate(w, g, y, 0, k1, blocks)


def whole_kernel(k1, blocks, w_in, w, g, y):
    w[...] = w_in[...]
    eliminate(w, g, y, 0, k1, blocks)


def next_kernel(k0, k1, blocks, w_in, w, g, y):
    w[...] = w_in[...]
    eliminate(w, g, y, k0, k1, blocks)


VM = pl.BlockSpec(memory_space=pltpu.VMEM)
SM = pl.BlockSpec(memory_space=pltpu.SMEM)


def elimination_call(kernel, order, specs, args):
    return pl.pallas_call(
        kernel,
        out_shape=jax.ShapeDtypeStruct((order, order), F32),
        in_specs=specs,
        out_specs=VM,
        scratch_shapes=[pltpu.VMEM((B, B), F32), pltpu.VMEM((B, order), F32)],
        compiler_params=pltpu.CompilerParams(vmem_limit_bytes=20 * MIB),
        cost_estimate=pl.CostEstimate(flops=4 * 10**9, bytes_accessed=8 * MIB, transcendentals=0),
    )(*args)


def split(v):
    high = v.astype(BF16)
    return high, (v - high.astype(F32)).astype(BF16)


def dot_tt(a, b):
    return lax.dot_general(a, b, (((1,), (1,)), ((), ())), preferred_element_type=F32)


def solve_kernel(masks, joined, n_own, n_all, width_cols, rank_max, *refs):
    if joined:
        inv, own, tgt, solved, core, xh, xl, ih, il, sh, sl = refs
    else:
        place, inv, own, near, far, solved, core, xh, xl, ih, il, sh, sl = refs
    blocks = inv.shape[0] // B
    for i in range(blocks):
        rows = slice(B * i, B * i + B)
        wide = B * (i + 1)
        ih[rows, :wide], il[rows, :wide] = split(inv[rows, :wide])
        if i % 2 == 0:
            ih[rows, wide : wide + B] = jnp.zeros((B, B), BF16)
            il[rows, wide : wide + B] = jnp.zeros((B, B), BF16)
    for c in range(blocks):
        xh[:n_own, B * c : B * c + B], xl[:n_own, B * c : B * c + B] = split(own[c])
        if joined:
            xh[n_own:, B * c : B * c + B], xl[n_own:, B * c : B * c + B] = split(tgt[c])
    if not joined:
        height, width = near.shape[1:]
        me_row, me_col = place[0], place[1]
        core_bit = me_row % 2
        for m, (even, odd) in enumerate(masks):
            for flip, buf in ((0, near), (1, far)):
                odd_core = (core_bit + flip) % 2
                row = (me_row ^ flip) ^ jnp.where(odd_core == 0, even[0], odd[0])
                col = me_col ^ jnp.where(odd_core == 0, even[1], odd[1])
                part = place[2 + row]
                high, low = split(buf[m])
                at = (pl.ds(pl.multiple_of(n_own + part * height, 16), height), pl.ds(pl.multiple_of(col * width, B), width))
                xh[at] = high
                xl[at] = low
    own_rows, tgt_rows = slice(0, n_own), (n_all - n_own) // 2

    def rows_of(at, keep):
        for i in range(blocks // 2):
            deep = 2 * B * (i + 1)
            out = slice(2 * B * i, deep)
            h, l = xh[at, :deep], xl[at, :deep]
            gh, gl = ih[out, :deep], il[out, :deep]
            res = dot_tt(h, gh) + dot_tt(h, gl) + dot_tt(l, gh)
            sh[at, out], sl[at, out] = split(res)
            if keep:
                solved[2 * i] = res[:, :B]
                solved[2 * i + 1] = res[:, B:]

    rows_of(own_rows, True)

    def body(t, carry):
        rows_of(pl.ds(pl.multiple_of(n_own + t * tgt_rows, 16), tgt_rows), False)
        return carry

    lax.fori_loop(0, 2, body, 0)
    oh, ol = sh.at[:n_own], sl.at[:n_own]

    def core_body(j, carry):
        at = pl.ds(pl.multiple_of(n_own + 2 * j * rank_max, 16), 2 * rank_max)
        h, l = sh[at, :], sl[at, :]
        res = dot_tt(oh[...], h) + dot_tt(oh[...], l) + dot_tt(ol[...], h)
        core[2 * j, :, :rank_max] = res[:, :rank_max]
        core[2 * j + 1, :, :rank_max] = res[:, rank_max:]
        return carry

    lax.fori_loop(0, width_cols // 2, core_body, 0)


def rows_iota(shape):
    return lax.broadcasted_iota(jnp.int32, shape, 0)


def aligned(i):
    return pl.multiple_of(i, 8)


def pack_kernel(offs, ranks, t_slot, t_rank, left, right, v, u, t, pv, pu):
    slots, rank_max, width = right.shape
    total = v.shape[0]
    rows = rows_iota((rank_max, width))
    for j in range(t.shape[0]):
        t[j] = jnp.where(rows < t_rank[j], right[t_slot[j]], 0.0)
    pv[...] = jnp.zeros_like(pv)
    pu[...] = jnp.zeros_like(pu)
    for s in range(slots):
        at = pl.ds(aligned(offs[s]), rank_max)
        keep = rows < ranks[s]
        pv[at, :] = jnp.where(keep, right[s], 0.0)
        pu[at, :] = jnp.where(keep, left[s], 0.0)
    v[...] = pv[:total]
    u[...] = pu[:total]


def unpack_kernel(offs, ranks, packed, out, held):
    slots, rank_max, width = out.shape
    held[: packed.shape[0]] = packed[...]
    rows = rows_iota((rank_max, width))
    for s in range(slots):
        out[s] = jnp.where(rows < ranks[s], held[pl.ds(aligned(offs[s]), rank_max), :], 0.0)


def update_kernel(n, group, count, spots, offs, ranks, tiles, col, core, *refs):
    pieces, (out, us, cs, u, sems) = refs[:count], refs[count:]
    step = pl.program_id(0)
    rank_max = out.shape[2]
    total = pieces[0].shape[0]

    @pl.when(step == 0)
    def _():
        def fetch(i):
            return pltpu.make_async_copy(pieces[i], us.at[jnp.maximum(spots[i], 0), :total], sems.at[i])

        cores = pltpu.make_async_copy(core, cs.at[:total], sems.at[count])
        cores.start()
        for i in range(count):
            pl.when(spots[i] >= 0)(fetch(i).start)
        us[:, total:] = jnp.zeros((n, rank_max, B), F32)
        cores.wait()
        for i in range(count):
            pl.when(spots[i] >= 0)(fetch(i).wait)

    rows = rows_iota((rank_max, B))
    for s in range(group):
        slot = step * group + s
        at = pl.ds(aligned(offs[slot]), rank_max)
        for k in range(n):
            lanes = slice(B * k, B * k + B)
            u[:rank_max, lanes], u[rank_max:, lanes] = split(us[k, at, :])
        keep = rows < jnp.where(tiles[slot] >= col[0], ranks[slot], 0)
        c = jnp.where(keep, cs[at, :], 0.0)
        ch, cl = split(jnp.transpose(c)[:rank_max])
        w = u[...]
        res = jnp.dot(jnp.concatenate([ch, ch], axis=1), w, preferred_element_type=F32)
        out[s, 0] = res + jnp.dot(cl, w[:rank_max], preferred_element_type=F32)


def phases(rows, cols):
    even = []
    bit = cols // 2
    while bit > 1:
        even.append((0, bit))
        bit //= 2
    bit = rows // 2
    while bit > 2:
        even.append((bit, 0))
        bit //= 2
    odd = even + [(2, 0), (0, 1)]
    even = even + [(0, 1), (2, 0)]
    return even, odd


def gather_masks(rows, cols):
    even, odd = phases(rows, cols)

    def masks(steps):
        got = [(0, 0)]
        for r, c in steps:
            got = got + [(a ^ r, b ^ c) for a, b in got]
        return got

    return list(zip(masks(even), masks(odd)))


def link_pairs(rows, cols, even, odd):
    pairs = []
    for r in range(rows):
        dr, dc = odd if r % 2 else even
        for c in range(cols):
            pairs.append((r * cols + c, (r ^ dr) * cols + (c ^ dc)))
    return pairs


def tie(*values):
    return lax.optimization_barrier(values)


def table(values, index):
    return jnp.array(values, jnp.int32)[index]


def body(rows, cols, total, args):
    diag_tile, left, right, ranks, tile_rows = args
    slots, rank_max, piece_rows = left.shape
    order = piece_rows * cols
    blocks = order // B
    group = slots // cols
    n_own, n_tgt = total // cols, cols * rank_max
    n_all = n_own + n_tgt
    row_index = lax.axis_index("row")
    col_index = lax.axis_index("col")
    masks = gather_masks(rows, cols)
    fits = piece_rows % B == 0 and blocks == cols
    own_ranks = lax.dynamic_slice_in_dim(ranks, row_index * slots, slots)
    own_tiles = lax.dynamic_slice_in_dim(tile_rows, row_index * slots, slots)
    padded = (own_ranks + 7) // 8 * 8
    before = jnp.arange(slots, dtype=jnp.int32)
    offs = jnp.sum(jnp.where(before[None, :] < before[:, None], padded[None, :], 0), axis=1)
    wanted = jnp.arange(cols, dtype=jnp.int32)
    every_slot = jnp.arange(tile_rows.shape[0], dtype=jnp.int32)
    hit = tile_rows[None, :] == wanted[:, None]
    holder = jnp.sum(jnp.where(hit, every_slot[None, :], 0), axis=1)
    t_rank = jnp.sum(jnp.where(hit, ranks[None, :], 0), axis=1)
    t_rank = jnp.where(holder // slots == row_index, t_rank, 0)

    v, u, part = pl.pallas_call(
        pack_kernel,
        out_shape=[
            jax.ShapeDtypeStruct((total, piece_rows), F32),
            jax.ShapeDtypeStruct((total, piece_rows), F32),
            jax.ShapeDtypeStruct((cols, rank_max, piece_rows), F32),
        ],
        in_specs=[SM] * 4 + [VM] * 2,
        out_specs=[VM] * 3,
        scratch_shapes=[pltpu.VMEM((total + rank_max, piece_rows), F32)] * 2,
        compiler_params=pltpu.CompilerParams(vmem_limit_bytes=24 * MIB),
    )(offs, own_ranks, holder % slots, t_rank, left, right)

    length = cols // 2
    up, down, cross = [u], [u], []

    def along(step):
        if step < length:
            up.append(lax.ppermute(up[-1], "col", [(c, c + 2) for c in range(2 * step - 2, cols - 2)]))
            down.append(lax.ppermute(down[-1], "col", [(c + 2, c) for c in range(cols - 2 * step)]))

    def over(step):
        if 0 < step < length:
            cross.append(lax.ppermute(up[step], "col", [(c, c ^ 1) for c in range(2 * step, cols)]))
            cross.append(lax.ppermute(down[step], "col", [(c, c ^ 1) for c in range(cols - 2 * step)]))

    def far_tie(x, step):
        if step < length:
            x, up[step], down[step] = tie(x, up[step], down[step])
        sent = slice(2 * step - 3, 2 * step - 1) if step > 1 else slice(0, 1)
        x, *cross[sent] = tie(x, *cross[sent])
        return x

    even, odd = phases(rows, cols)
    links = len(even)
    swap = [(r, r ^ 1) for r in range(rows)]

    t_steps = []
    bit = 1
    while bit < rows:
        t_steps.append(("sum", bit))
        bit *= 2
    t_steps += [("link", i) for i in range(links)] + [("core", 0)]
    state = dict(part=part, t=None, t_far=None)

    def t_step():
        if not t_steps:
            return
        kind, which = t_steps.pop(0)
        if kind == "sum":
            p = state["part"]
            h = p.shape[0] // 2
            side = (row_index // which) % 2
            kept = lax.dynamic_slice_in_dim(p, side * h, h, 0)
            sent = lax.dynamic_slice_in_dim(p, (1 - side) * h, h, 0)
            state["part"] = kept + lax.ppermute(sent, "row", [(r, r ^ which) for r in range(rows)])
            if t_steps[0][0] == "link":
                p = state["part"]
                state["per"] = p.shape[0]
                state["t"] = p.reshape(1, p.shape[0] * rank_max, piece_rows)
        elif kind == "link":
            t = state["t"]
            got = lax.ppermute(t, ("row", "col"), link_pairs(rows, cols, even[which], odd[which]))
            state["t"] = jnp.concatenate([t, got], axis=0)
        else:
            state["t_far"] = lax.ppermute(state["t"], "row", swap)

    def t_tie(x):
        key = "t" if state["t"] is not None else "part"
        x, state[key] = tie(x, state[key])
        return x

    near = diag_tile[None]
    for i in range(links):
        got = lax.ppermute(near, ("row", "col"), link_pairs(rows, cols, even[i], odd[i]))
        t_step()
        near = jnp.concatenate([near, got], axis=0)
        near = t_tie(near)
        if i == 0:
            near, u = tie(near, u)
            up[0] = down[0] = u
            cross.append(lax.ppermute(u, "col", [(c, c ^ 1) for c in range(cols)]))
            along(1)
    near, up[1], down[1] = tie(near, up[1], down[1])
    far = lax.ppermute(near, "row", swap)
    t_step()
    far = t_tie(far)

    far, v = tie(far, v)
    own = lax.all_to_all(v.reshape(cols, n_own, piece_rows), "col", split_axis=0, concat_axis=0, tiled=True)

    places = []
    for r in range(rows):
        at, h, bb = 0, rows // 2, 1
        while bb < rows:
            at += h * ((r // bb) % 2)
            h //= 2
            bb *= 2
        places.append(at)

    def sources():
        near_m = jnp.where(row_index % 2 == 0, table([e for e, _ in masks], slice(None)), table([o for _, o in masks], slice(None)))
        far_m = jnp.where(row_index % 2 == 0, table([o for _, o in masks], slice(None)), table([e for e, _ in masks], slice(None)))
        r = jnp.concatenate([row_index ^ near_m[:, 0], row_index ^ 1 ^ far_m[:, 0]])
        c = jnp.concatenate([col_index ^ near_m[:, 1], col_index ^ far_m[:, 1]])
        return r, c

    place = jnp.concatenate([jnp.stack([row_index, col_index]).astype(jnp.int32), jnp.array(places, jnp.int32)])
    per_call = 2
    t_step()
    if fits:
        inv = elimination_call(
            functools.partial(first_kernel, per_call, blocks, masks), order, [SM, VM, VM], (place, near, far)
        )
    else:
        r, c = sources()
        pieces = jnp.concatenate([near, far], axis=0)
        tile = jnp.zeros((rows * cols,) + pieces.shape[1:], F32).at[r * cols + c].set(pieces)
        tile = tile.reshape(rows, cols, order // rows, piece_rows).transpose(0, 2, 1, 3).reshape(order, order)
        inv = elimination_call(functools.partial(whole_kernel, per_call, blocks), order, [VM], (tile,))
    inv = t_tie(inv)
    for k in range(per_call, blocks, per_call):
        while t_steps:
            t_step()
        if k == per_call:
            inv = far_tie(inv, 1)
            along(2)
            over(1)
        inv = elimination_call(functools.partial(next_kernel, k, k + per_call, blocks), order, [VM], (inv,))
    t_near, t_far = state["t"], state["t_far"]
    per = state["per"]

    inv = far_tie(inv, 2)
    along(3)
    over(2)
    own = own.reshape(cols, n_own, piece_rows)
    if fits:
        specs, operands = [SM, VM, VM, VM, VM], (place, inv, own, t_near, t_far)
    else:
        own = own.transpose(1, 0, 2).reshape(n_own, blocks, B).transpose(1, 0, 2)
        r, c = sources()
        spots = table(places, r)
        pieces = jnp.concatenate([t_near, t_far], axis=0)
        tgt = jnp.zeros((rows * cols,) + pieces.shape[1:], F32).at[spots * cols + c].set(pieces)
        tgt = tgt.reshape(rows, cols, per * rank_max, piece_rows).transpose(0, 2, 1, 3).reshape(n_tgt, blocks, B)
        specs, operands = [VM, VM, VM], (inv, own, tgt.transpose(1, 0, 2))
    solved, core = pl.pallas_call(
        functools.partial(solve_kernel, masks, not fits, n_own, n_all, cols, rank_max),
        out_shape=[
            jax.ShapeDtypeStruct((blocks, n_own, B), F32),
            jax.ShapeDtypeStruct((cols, n_own, B), F32),
        ],
        in_specs=specs,
        out_specs=[VM, VM],
        scratch_shapes=[pltpu.VMEM((n_all, order), BF16)] * 2
        + [pltpu.VMEM((order, order), BF16)] * 2
        + [pltpu.VMEM((n_all, order), BF16)] * 2,
        compiler_params=pltpu.CompilerParams(vmem_limit_bytes=34 * MIB),
        cost_estimate=pl.CostEstimate(flops=6 * 10**9, bytes_accessed=12 * MIB, transcendentals=0),
    )(*operands)
    for step in range(3, length):
        core = far_tie(core, step)
        along(step + 1)
        over(step)
    core = lax.all_to_all(core, "col", split_axis=0, concat_axis=0, tiled=True).reshape(total, B)
    if not fits:
        solved = solved.transpose(1, 0, 2).reshape(n_own, cols, piece_rows).transpose(1, 0, 2)
    solved, core, cross[-2], cross[-1] = tie(solved, core, cross[-2], cross[-1])
    back = lax.all_to_all(solved, "col", split_axis=0, concat_axis=0, tiled=True).reshape(total, piece_rows)
    own_rows = pl.pallas_call(
        unpack_kernel,
        out_shape=jax.ShapeDtypeStruct((slots, rank_max, piece_rows), F32),
        in_specs=[SM, SM, VM],
        out_specs=VM,
        scratch_shapes=[pltpu.VMEM((total + rank_max, piece_rows), F32)],
        compiler_params=pltpu.CompilerParams(vmem_limit_bytes=16 * MIB),
    )(offs, own_ranks, back)

    pieces = [u] + up[1:] + down[1:] + cross
    spots = [col_index]
    for flip in (0, 1):
        ups = [jnp.where(col_index >= 2 * k, (col_index - 2 * k) ^ flip, -1) for k in range(1, length)]
        downs = [jnp.where(col_index < cols - 2 * k, (col_index + 2 * k) ^ flip, -1) for k in range(1, length)]
        if flip:
            spots += [col_index ^ 1] + [x for pair in zip(ups, downs) for x in pair]
        else:
            spots += ups + downs
    spots = jnp.stack(spots).astype(jnp.int32)
    if fits:
        anyspec = pl.BlockSpec(memory_space=pl.ANY)
        update = pl.pallas_call(
            functools.partial(update_kernel, cols, group, len(pieces)),
            out_shape=jax.ShapeDtypeStruct((slots, 1, rank_max, order), F32),
            grid_spec=pltpu.PrefetchScalarGridSpec(
                num_scalar_prefetch=5,
                grid=(cols,),
                in_specs=[anyspec] * (len(pieces) + 1),
                out_specs=pl.BlockSpec((group, 1, rank_max, order), lambda c, *_: (c, 0, 0, 0)),
                scratch_shapes=[
                    pltpu.VMEM((cols, total + rank_max, B), F32),
                    pltpu.VMEM((total + rank_max, B), F32),
                    pltpu.VMEM((2 * rank_max, order), BF16),
                    pltpu.SemaphoreType.DMA((len(pieces) + 1,)),
                ],
            ),
            compiler_params=pltpu.CompilerParams(vmem_limit_bytes=60 * MIB),
            cost_estimate=pl.CostEstimate(flops=2 * 10**9, bytes_accessed=24 * MIB, transcendentals=0),
        )(spots, offs, own_ranks, own_tiles, col_index[None].astype(jnp.int32), core, *pieces)
        update = jnp.transpose(update, (0, 1, 3, 2))
    else:
        where = jnp.where(spots < 0, cols, spots)
        full = jnp.zeros((cols + 1, total, piece_rows), F32)
        for i, piece in enumerate(pieces):
            full = lax.dynamic_update_index_in_dim(full, piece, where[i], 0)
        full = full[:cols].transpose(1, 0, 2).reshape(total, order)
        index = offs[:, None] + jnp.arange(rank_max, dtype=jnp.int32)[None, :]
        index = jnp.minimum(index, total - 1)
        keep = (jnp.arange(rank_max, dtype=jnp.int32)[None, :] < own_ranks[:, None]) & (own_tiles >= col_index)[:, None]
        cs = jnp.where(keep[:, :, None], core[index][:, :, :rank_max], 0.0)
        update = jnp.einsum("srn,srq->snq", full[index], cs, precision=HIGHEST)[:, None]
    return (jnp.transpose(own_rows, (0, 2, 1)), update)


def shards(rows, cols, diag_tile, panel_left, panel_right, ranks, tile_rows):
    slots, _, rank_max = panel_left.shape
    args = (diag_tile, jnp.transpose(panel_left, (0, 2, 1)), jnp.transpose(panel_right, (0, 2, 1)), ranks, tile_rows)
    most = slots * rank_max
    grain = 16 * cols
    some = -(-(most * 25) // (32 * grain)) * grain
    sums = jnp.sum(((ranks + 7) // 8 * 8).reshape(rows, slots), axis=1)
    return lax.cond(
        jnp.max(sums) <= some,
        functools.partial(body, rows, cols, some),
        functools.partial(body, rows, cols, most),
        args,
    )


def solution(mesh):
    return jax.shard_map(
        functools.partial(shards, mesh.shape["row"], mesh.shape["col"]),
        mesh=mesh,
        in_specs=(P("row", "col"), P("row", "col", None), P("row", "col", None), P(), P()),
        out_specs=(P("row", "col", None), P("row", "col", None, None)),
        check_vma=False,
    )
```

```python
import functools
import jax
import jax.numpy as jnp
from jax import lax
from jax.experimental import pallas as pl
from jax.experimental.pallas import tpu as pltpu
from jax.sharding import PartitionSpec as P

F32 = jnp.float32
BF16 = jnp.bfloat16
HIGHEST = lax.Precision.HIGHEST
B = 128
MIB = 2**20


def sub_row(v, k):
    return jnp.broadcast_to(v[k : k + 1, :], v.shape)


def lane_col(v, c):
    return jnp.broadcast_to(v[:, c : c + 1], v.shape)


def inverse_factor(rows):
    lane = lax.broadcasted_iota(jnp.int32, (8, B), 1)
    sub = lax.broadcasted_iota(jnp.int32, (8, B), 0)
    work, out = list(rows), []
    for p in range(len(rows)):
        base = 8 * p
        cols = {q: [lane_col(work[q], base + j) for j in range(8)] for q in range(p, len(rows))}
        t = list(cols[p])
        in_panel = (lane >= base) & (lane < base + 8)
        r = jnp.where(in_panel, jnp.where(lane - base == sub, 1.0, 0.0).astype(F32), work[p])
        g = jnp.zeros((8, B), F32)
        for k in range(0, 8, 2):
            a, b, c = sub_row(t[k], k), sub_row(t[k], k + 1), sub_row(t[k + 1], k + 1)
            det = a * c - b * b
            inv = 1.0 / det
            pivot = (sub == k) | (sub == k + 1)
            t0 = jnp.where(pivot, jnp.where(sub == k, -1.0, 0.0).astype(F32), t[k])
            t1 = jnp.where(pivot, jnp.where(sub == k, 0.0, -1.0).astype(F32), t[k + 1])
            alpha = (t0 * c - t1 * b) * inv
            beta = (t1 * a - t0 * b) * inv
            x, y = sub_row(r, k), sub_row(r, k + 1)
            g0 = x * lax.rsqrt(a)
            g1 = (a * y - b * x) * lax.rsqrt(a * det)
            g = jnp.where(sub == k, g0, jnp.where(sub == k + 1, g1, g))
            r = jnp.where(pivot, 0.0, r) - alpha * x - beta * y
            for j in range(k + 2, 8):
                t[j] = jnp.where(pivot, 0.0, t[j]) - alpha * sub_row(t[j], k) - beta * sub_row(t[j], k + 1)
        out.append(jnp.where(lane <= sub + base, g, 0.0))
        z = [sub_row(r, j) for j in range(8)]
        for q in range(p + 1, len(rows)):
            acc = jnp.where(in_panel, 0.0, work[q])
            for j in range(8):
                acc = acc - cols[q][j] * z[j]
            work[q] = acc
    return out


def eliminate(w, g, y, k0, k1, blocks):
    for k in range(k0, k1):
        lo = B * k
        rows = [w[lo + 8 * q : lo + 8 * q + 8, lo : lo + B] for q in range(B // 8)]
        for q, piece in enumerate(inverse_factor(rows)):
            g[8 * q : 8 * q + 8, :] = piece
        y[...] = jnp.dot(g[...], w[lo : lo + B, :], precision=HIGHEST, preferred_element_type=F32)
        y[:, lo : lo + B] = g[...]
        w[lo : lo + B, :] = y[...]

        def body(i, carry):
            at = pl.multiple_of(i * B, B)
            w[pl.ds(at, B), lo : lo + B] = jnp.zeros((B, B), F32)
            w[pl.ds(at, B), :] -= lax.dot_general(
                y[:, pl.ds(at, B)], y[...], (((0,), (0,)), ((), ())), precision=HIGHEST, preferred_element_type=F32
            )
            return carry

        if k + 1 < blocks:
            lax.fori_loop(k + 1, blocks, body, 0)


def first_kernel(k1, blocks, masks, place, near, far, w, g, y):
    height, width = near.shape[1:]
    me_row, me_col = place[0], place[1]
    core = me_row % 2
    for m, (even, odd) in enumerate(masks):
        for flip, buf in ((0, near), (1, far)):
            odd_core = (core + flip) % 2
            row = (me_row ^ flip) ^ jnp.where(odd_core == 0, even[0], odd[0])
            col = me_col ^ jnp.where(odd_core == 0, even[1], odd[1])
            w[pl.ds(pl.multiple_of(row * height, 8), height), pl.ds(pl.multiple_of(col * width, B), width)] = buf[m]
    eliminate(w, g, y, 0, k1, blocks)


def whole_kernel(k1, blocks, w_in, w, g, y):
    w[...] = w_in[...]
    eliminate(w, g, y, 0, k1, blocks)


def next_kernel(k0, k1, blocks, w_in, w, g, y):
    w[...] = w_in[...]
    eliminate(w, g, y, k0, k1, blocks)


VM = pl.BlockSpec(memory_space=pltpu.VMEM)
SM = pl.BlockSpec(memory_space=pltpu.SMEM)


def elimination_call(kernel, order, specs, args):
    return pl.pallas_call(
        kernel,
        out_shape=jax.ShapeDtypeStruct((order, order), F32),
        in_specs=specs,
        out_specs=VM,
        scratch_shapes=[pltpu.VMEM((B, B), F32), pltpu.VMEM((B, order), F32)],
        compiler_params=pltpu.CompilerParams(vmem_limit_bytes=20 * MIB),
        cost_estimate=pl.CostEstimate(flops=4 * 10**9, bytes_accessed=8 * MIB, transcendentals=0),
    )(*args)


def split(v):
    high = v.astype(BF16)
    return high, (v - high.astype(F32)).astype(BF16)


def dot_tt(a, b):
    return lax.dot_general(a, b, (((1,), (1,)), ((), ())), preferred_element_type=F32)


def solve_kernel(masks, joined, n_own, n_all, width_cols, rank_max, *refs):
    if joined:
        inv, own, tgt, solved, core, xh, xl, ih, il, sh, sl = refs
    else:
        place, inv, own, near, far, solved, core, xh, xl, ih, il, sh, sl = refs
    blocks = inv.shape[0] // B
    for i in range(blocks):
        rows = slice(B * i, B * i + B)
        wide = B * (i + 1)
        ih[rows, :wide], il[rows, :wide] = split(inv[rows, :wide])
        if i % 2 == 0:
            ih[rows, wide : wide + B] = jnp.zeros((B, B), BF16)
            il[rows, wide : wide + B] = jnp.zeros((B, B), BF16)
    for c in range(blocks):
        xh[:n_own, B * c : B * c + B], xl[:n_own, B * c : B * c + B] = split(own[c])
        if joined:
            xh[n_own:, B * c : B * c + B], xl[n_own:, B * c : B * c + B] = split(tgt[c])
    if not joined:
        height, width = near.shape[1:]
        me_row, me_col = place[0], place[1]
        core_bit = me_row % 2
        for m, (even, odd) in enumerate(masks):
            for flip, buf in ((0, near), (1, far)):
                odd_core = (core_bit + flip) % 2
                row = (me_row ^ flip) ^ jnp.where(odd_core == 0, even[0], odd[0])
                col = me_col ^ jnp.where(odd_core == 0, even[1], odd[1])
                part = place[2 + row]
                high, low = split(buf[m])
                at = (pl.ds(pl.multiple_of(n_own + part * height, 16), height), pl.ds(pl.multiple_of(col * width, B), width))
                xh[at] = high
                xl[at] = low
    own_rows, tgt_rows = slice(0, n_own), (n_all - n_own) // 2

    def rows_of(at, keep):
        for i in range(blocks // 2):
            deep = 2 * B * (i + 1)
            out = slice(2 * B * i, deep)
            h, l = xh[at, :deep], xl[at, :deep]
            gh, gl = ih[out, :deep], il[out, :deep]
            res = dot_tt(h, gh) + dot_tt(h, gl) + dot_tt(l, gh)
            sh[at, out], sl[at, out] = split(res)
            if keep:
                solved[2 * i] = res[:, :B]
                solved[2 * i + 1] = res[:, B:]

    rows_of(own_rows, True)

    def body(t, carry):
        rows_of(pl.ds(pl.multiple_of(n_own + t * tgt_rows, 16), tgt_rows), False)
        return carry

    lax.fori_loop(0, 2, body, 0)
    oh, ol = sh.at[:n_own], sl.at[:n_own]

    def core_body(j, carry):
        at = pl.ds(pl.multiple_of(n_own + 2 * j * rank_max, 16), 2 * rank_max)
        h, l = sh[at, :], sl[at, :]
        res = dot_tt(oh[...], h) + dot_tt(oh[...], l) + dot_tt(ol[...], h)
        core[2 * j, :, :rank_max] = res[:, :rank_max]
        core[2 * j + 1, :, :rank_max] = res[:, rank_max:]
        return carry

    lax.fori_loop(0, width_cols // 2, core_body, 0)


def rows_iota(shape):
    return lax.broadcasted_iota(jnp.int32, shape, 0)


def aligned(i):
    return pl.multiple_of(i, 8)


def pack_kernel(offs, ranks, t_slot, t_rank, left, right, v, u, t, pv, pu):
    slots, rank_max, width = right.shape
    total = v.shape[0]
    rows = rows_iota((rank_max, width))
    for j in range(t.shape[0]):
        t[j] = jnp.where(rows < t_rank[j], right[t_slot[j]], 0.0)
    pv[...] = jnp.zeros_like(pv)
    pu[...] = jnp.zeros_like(pu)
    for s in range(slots):
        at = pl.ds(aligned(offs[s]), rank_max)
        keep = rows < ranks[s]
        pv[at, :] = jnp.where(keep, right[s], 0.0)
        pu[at, :] = jnp.where(keep, left[s], 0.0)
    v[...] = pv[:total]
    u[...] = pu[:total]


def unpack_kernel(offs, ranks, packed, out, held):
    slots, rank_max, width = out.shape
    held[: packed.shape[0]] = packed[...]
    rows = rows_iota((rank_max, width))
    for s in range(slots):
        out[s] = jnp.where(rows < ranks[s], held[pl.ds(aligned(offs[s]), rank_max), :], 0.0)


def update_kernel(n, group, count, spots, offs, ranks, tiles, col, core, *refs):
    pieces, (out, us, cs, u, sems) = refs[:count], refs[count:]
    step = pl.program_id(0)
    rank_max = out.shape[2]
    total = pieces[0].shape[0]

    @pl.when(step == 0)
    def _():
        def fetch(i):
            return pltpu.make_async_copy(pieces[i], us.at[jnp.maximum(spots[i], 0), :total], sems.at[i])

        cores = pltpu.make_async_copy(core, cs.at[:total], sems.at[count])
        cores.start()
        for i in range(count):
            pl.when(spots[i] >= 0)(fetch(i).start)
        us[:, total:] = jnp.zeros((n, rank_max, B), F32)
        cores.wait()
        for i in range(count):
            pl.when(spots[i] >= 0)(fetch(i).wait)

    rows = rows_iota((rank_max, B))
    for s in range(group):
        slot = step * group + s
        at = pl.ds(aligned(offs[slot]), rank_max)
        for k in range(n):
            lanes = slice(B * k, B * k + B)
            u[:rank_max, lanes], u[rank_max:, lanes] = split(us[k, at, :])
        keep = rows < jnp.where(tiles[slot] >= col[0], ranks[slot], 0)
        c = jnp.where(keep, cs[at, :], 0.0)
        ch, cl = split(jnp.transpose(c)[:rank_max])
        w = u[...]
        res = jnp.dot(jnp.concatenate([ch, ch], axis=1), w, preferred_element_type=F32)
        out[s, 0] = res + jnp.dot(cl, w[:rank_max], preferred_element_type=F32)


def phases(rows, cols):
    even = []
    bit = cols // 2
    while bit > 1:
        even.append((0, bit))
        bit //= 2
    bit = rows // 2
    while bit > 2:
        even.append((bit, 0))
        bit //= 2
    odd = even + [(2, 0), (0, 1)]
    even = even + [(0, 1), (2, 0)]
    return even, odd


def gather_masks(rows, cols):
    even, odd = phases(rows, cols)

    def masks(steps):
        got = [(0, 0)]
        for r, c in steps:
            got = got + [(a ^ r, b ^ c) for a, b in got]
        return got

    return list(zip(masks(even), masks(odd)))


def link_pairs(rows, cols, even, odd):
    pairs = []
    for r in range(rows):
        dr, dc = odd if r % 2 else even
        for c in range(cols):
            pairs.append((r * cols + c, (r ^ dr) * cols + (c ^ dc)))
    return pairs


def tie(*values):
    return lax.optimization_barrier(values)


def table(values, index):
    return jnp.array(values, jnp.int32)[index]


def body(rows, cols, total, args):
    diag_tile, left, right, ranks, tile_rows = args
    slots, rank_max, piece_rows = left.shape
    order = piece_rows * cols
    blocks = order // B
    group = slots // cols
    n_own, n_tgt = total // cols, cols * rank_max
    n_all = n_own + n_tgt
    row_index = lax.axis_index("row")
    col_index = lax.axis_index("col")
    masks = gather_masks(rows, cols)
    fits = piece_rows % B == 0 and blocks == cols
    own_ranks = lax.dynamic_slice_in_dim(ranks, row_index * slots, slots)
    own_tiles = lax.dynamic_slice_in_dim(tile_rows, row_index * slots, slots)
    padded = (own_ranks + 7) // 8 * 8
    before = jnp.arange(slots, dtype=jnp.int32)
    offs = jnp.sum(jnp.where(before[None, :] < before[:, None], padded[None, :], 0), axis=1)
    wanted = jnp.arange(cols, dtype=jnp.int32)
    every_slot = jnp.arange(tile_rows.shape[0], dtype=jnp.int32)
    hit = tile_rows[None, :] == wanted[:, None]
    holder = jnp.sum(jnp.where(hit, every_slot[None, :], 0), axis=1)
    t_rank = jnp.sum(jnp.where(hit, ranks[None, :], 0), axis=1)
    t_rank = jnp.where(holder // slots == row_index, t_rank, 0)

    v, u, part = pl.pallas_call(
        pack_kernel,
        out_shape=[
            jax.ShapeDtypeStruct((total, piece_rows), F32),
            jax.ShapeDtypeStruct((total, piece_rows), F32),
            jax.ShapeDtypeStruct((cols, rank_max, piece_rows), F32),
        ],
        in_specs=[SM] * 4 + [VM] * 2,
        out_specs=[VM] * 3,
        scratch_shapes=[pltpu.VMEM((total + rank_max, piece_rows), F32)] * 2,
        compiler_params=pltpu.CompilerParams(vmem_limit_bytes=24 * MIB),
    )(offs, own_ranks, holder % slots, t_rank, left, right)

    length = cols // 2
    up, down, cross = [u], [u], []

    def along(step):
        if step < length:
            up.append(lax.ppermute(up[-1], "col", [(c, c + 2) for c in range(2 * step - 2, cols - 2)]))
            down.append(lax.ppermute(down[-1], "col", [(c + 2, c) for c in range(cols - 2 * step)]))

    def reach(z):
        ways = [(k, 0 if (z >= k) == (side == (z >= length // 2)) else 1, side) for k in range(1, length) for side in (True, False)]
        return [(side, k) for k, _, side in sorted(ways) if (z >= k if side else z + k < length)]

    paths = [reach(z) for z in range(length)]
    here = col_index // 2

    def over(step):
        if 0 < step < length:
            picks = [paths[z][step - 1] for z in range(length)]
            piece = None
            for pick in sorted(set(picks)):
                side, k = pick
                got = (up if side else down)[k]
                if piece is None:
                    piece = got
                else:
                    at = functools.reduce(jnp.logical_or, [here == z for z in range(length) if picks[z] == pick])
                    piece = jnp.where(at, got, piece)
            up[step], down[step], piece = tie(up[step], down[step], piece)
            cross.append(lax.ppermute(piece, "col", [(c, c ^ 1) for c in range(cols)]))

    def along_tie(x, step):
        if step < length:
            x, up[step], down[step] = tie(x, up[step], down[step])
        return x

    def over_tie(x, step):
        if step < length:
            x, cross[step] = tie(x, cross[step])
        return x

    even, odd = phases(rows, cols)
    links = len(even)
    swap = [(r, r ^ 1) for r in range(rows)]

    t_steps = []
    bit = 1
    while bit < rows:
        t_steps.append(("sum", bit))
        bit *= 2
    t_steps += [("link", i) for i in range(links)] + [("core", 0)]
    state = dict(part=part, t=None, t_far=None)

    def t_step():
        if not t_steps:
            return
        kind, which = t_steps.pop(0)
        if kind == "sum":
            p = state["part"]
            h = p.shape[0] // 2
            side = (row_index // which) % 2
            kept = lax.dynamic_slice_in_dim(p, side * h, h, 0)
            sent = lax.dynamic_slice_in_dim(p, (1 - side) * h, h, 0)
            state["part"] = kept + lax.ppermute(sent, "row", [(r, r ^ which) for r in range(rows)])
            if t_steps[0][0] == "link":
                p = state["part"]
                state["per"] = p.shape[0]
                state["t"] = p.reshape(1, p.shape[0] * rank_max, piece_rows)
        elif kind == "link":
            t = state["t"]
            got = lax.ppermute(t, ("row", "col"), link_pairs(rows, cols, even[which], odd[which]))
            state["t"] = jnp.concatenate([t, got], axis=0)
        else:
            state["t_far"] = lax.ppermute(state["t"], "row", swap)

    def t_tie(x):
        key = "t" if state["t"] is not None else "part"
        x, state[key] = tie(x, state[key])
        return x

    near = diag_tile[None]
    for i in range(links):
        got = lax.ppermute(near, ("row", "col"), link_pairs(rows, cols, even[i], odd[i]))
        t_step()
        near = jnp.concatenate([near, got], axis=0)
        near = t_tie(near)
        if i == 0:
            near, u = tie(near, u)
            up[0] = down[0] = u
            cross.append(lax.ppermute(u, "col", [(c, c ^ 1) for c in range(cols)]))
            along(1)
    far = lax.ppermute(near, "row", swap)
    t_step()
    far = t_tie(far)

    far, v = tie(far, v)
    own = lax.all_to_all(v.reshape(cols, n_own, piece_rows), "col", split_axis=0, concat_axis=0, tiled=True)

    places = []
    for r in range(rows):
        at, h, bb = 0, rows // 2, 1
        while bb < rows:
            at += h * ((r // bb) % 2)
            h //= 2
            bb *= 2
        places.append(at)

    def sources():
        near_m = jnp.where(row_index % 2 == 0, table([e for e, _ in masks], slice(None)), table([o for _, o in masks], slice(None)))
        far_m = jnp.where(row_index % 2 == 0, table([o for _, o in masks], slice(None)), table([e for e, _ in masks], slice(None)))
        r = jnp.concatenate([row_index ^ near_m[:, 0], row_index ^ 1 ^ far_m[:, 0]])
        c = jnp.concatenate([col_index ^ near_m[:, 1], col_index ^ far_m[:, 1]])
        return r, c

    place = jnp.concatenate([jnp.stack([row_index, col_index]).astype(jnp.int32), jnp.array(places, jnp.int32)])
    per_call = 2
    t_step()
    if fits:
        inv = elimination_call(
            functools.partial(first_kernel, per_call, blocks, masks), order, [SM, VM, VM], (place, near, far)
        )
    else:
        r, c = sources()
        pieces = jnp.concatenate([near, far], axis=0)
        tile = jnp.zeros((rows * cols,) + pieces.shape[1:], F32).at[r * cols + c].set(pieces)
        tile = tile.reshape(rows, cols, order // rows, piece_rows).transpose(0, 2, 1, 3).reshape(order, order)
        inv = elimination_call(functools.partial(whole_kernel, per_call, blocks), order, [VM], (tile,))
    inv = t_tie(inv)
    for k in range(per_call, blocks, per_call):
        while t_steps:
            t_step()
        if k == per_call:
            inv = over_tie(along_tie(inv, 1), 0)
            over(1)
            along(2)
        if k == 2 * per_call:
            inv, own, state["t_far"] = tie(along_tie(inv, 2), own, state["t_far"])
            over(2)
            along(3)
        if k == 3 * per_call:
            inv = over_tie(inv, 1)
        inv = elimination_call(functools.partial(next_kernel, k, k + per_call, blocks), order, [VM], (inv,))
    t_near, t_far = state["t"], state["t_far"]
    per = state["per"]

    inv = over_tie(along_tie(inv, 3), 2)
    own = own.reshape(cols, n_own, piece_rows)
    if fits:
        specs, operands = [SM, VM, VM, VM, VM], (place, inv, own, t_near, t_far)
    else:
        own = own.transpose(1, 0, 2).reshape(n_own, blocks, B).transpose(1, 0, 2)
        r, c = sources()
        spots = table(places, r)
        pieces = jnp.concatenate([t_near, t_far], axis=0)
        tgt = jnp.zeros((rows * cols,) + pieces.shape[1:], F32).at[spots * cols + c].set(pieces)
        tgt = tgt.reshape(rows, cols, per * rank_max, piece_rows).transpose(0, 2, 1, 3).reshape(n_tgt, blocks, B)
        specs, operands = [VM, VM, VM], (inv, own, tgt.transpose(1, 0, 2))
    solved, core = pl.pallas_call(
        functools.partial(solve_kernel, masks, not fits, n_own, n_all, cols, rank_max),
        out_shape=[
            jax.ShapeDtypeStruct((blocks, n_own, B), F32),
            jax.ShapeDtypeStruct((cols, n_own, B), F32),
        ],
        in_specs=specs,
        out_specs=[VM, VM],
        scratch_shapes=[pltpu.VMEM((n_all, order), BF16)] * 2
        + [pltpu.VMEM((order, order), BF16)] * 2
        + [pltpu.VMEM((n_all, order), BF16)] * 2,
        compiler_params=pltpu.CompilerParams(vmem_limit_bytes=34 * MIB),
        cost_estimate=pl.CostEstimate(flops=6 * 10**9, bytes_accessed=12 * MIB, transcendentals=0),
    )(*operands)
    if not fits:
        solved = solved.transpose(1, 0, 2).reshape(n_own, cols, piece_rows).transpose(1, 0, 2)
    over(3)
    for step in range(4, length):
        along(step)
        core = over_tie(along_tie(core, step), step - 1)
        over(step)
    core = lax.all_to_all(core, "col", split_axis=0, concat_axis=0, tiled=True).reshape(total, B)
    solved, core, cross[-1] = tie(solved, core, cross[-1])
    back = lax.all_to_all(solved, "col", split_axis=0, concat_axis=0, tiled=True).reshape(total, piece_rows)
    own_rows = pl.pallas_call(
        unpack_kernel,
        out_shape=jax.ShapeDtypeStruct((slots, rank_max, piece_rows), F32),
        in_specs=[SM, SM, VM],
        out_specs=VM,
        scratch_shapes=[pltpu.VMEM((total + rank_max, piece_rows), F32)],
        compiler_params=pltpu.CompilerParams(vmem_limit_bytes=16 * MIB),
    )(offs, own_ranks, back)

    pieces = [u] + up[1:] + down[1:] + cross
    spots = [col_index]
    spots += [jnp.where(col_index >= 2 * k, col_index - 2 * k, -1) for k in range(1, length)]
    spots += [jnp.where(col_index < cols - 2 * k, col_index + 2 * k, -1) for k in range(1, length)]
    spots += [col_index ^ 1]
    for step in range(1, length):
        origin = [z - paths[z][step - 1][1] if paths[z][step - 1][0] else z + paths[z][step - 1][1] for z in range(length)]
        spots.append((2 * table(origin, here) + col_index % 2) ^ 1)
    spots = jnp.stack(spots).astype(jnp.int32)
    if fits:
        anyspec = pl.BlockSpec(memory_space=pl.ANY)
        update = pl.pallas_call(
            functools.partial(update_kernel, cols, group, len(pieces)),
            out_shape=jax.ShapeDtypeStruct((slots, 1, rank_max, order), F32),
            grid_spec=pltpu.PrefetchScalarGridSpec(
                num_scalar_prefetch=5,
                grid=(cols,),
                in_specs=[anyspec] * (len(pieces) + 1),
                out_specs=pl.BlockSpec((group, 1, rank_max, order), lambda c, *_: (c, 0, 0, 0)),
                scratch_shapes=[
                    pltpu.VMEM((cols, total + rank_max, B), F32),
                    pltpu.VMEM((total + rank_max, B), F32),
                    pltpu.VMEM((2 * rank_max, order), BF16),
                    pltpu.SemaphoreType.DMA((len(pieces) + 1,)),
                ],
            ),
            compiler_params=pltpu.CompilerParams(vmem_limit_bytes=60 * MIB),
            cost_estimate=pl.CostEstimate(flops=2 * 10**9, bytes_accessed=24 * MIB, transcendentals=0),
        )(spots, offs, own_ranks, own_tiles, col_index[None].astype(jnp.int32), core, *pieces)
        update = jnp.transpose(update, (0, 1, 3, 2))
    else:
        where = jnp.where(spots < 0, cols, spots)
        full = jnp.zeros((cols + 1, total, piece_rows), F32)
        for i, piece in enumerate(pieces):
            full = lax.dynamic_update_index_in_dim(full, piece, where[i], 0)
        full = full[:cols].transpose(1, 0, 2).reshape(total, order)
        index = offs[:, None] + jnp.arange(rank_max, dtype=jnp.int32)[None, :]
        index = jnp.minimum(index, total - 1)
        keep = (jnp.arange(rank_max, dtype=jnp.int32)[None, :] < own_ranks[:, None]) & (own_tiles >= col_index)[:, None]
        cs = jnp.where(keep[:, :, None], core[index][:, :, :rank_max], 0.0)
        update = jnp.einsum("srn,srq->snq", full[index], cs, precision=HIGHEST)[:, None]
    return (jnp.transpose(own_rows, (0, 2, 1)), update)


def shards(rows, cols, diag_tile, panel_left, panel_right, ranks, tile_rows):
    slots, _, rank_max = panel_left.shape
    args = (diag_tile, jnp.transpose(panel_left, (0, 2, 1)), jnp.transpose(panel_right, (0, 2, 1)), ranks, tile_rows)
    most = slots * rank_max
    grain = 16 * cols
    some = -(-(most * 25) // (32 * grain)) * grain
    sums = jnp.sum(((ranks + 7) // 8 * 8).reshape(rows, slots), axis=1)
    return lax.cond(
        jnp.max(sums) <= some,
        functools.partial(body, rows, cols, some),
        functools.partial(body, rows, cols, most),
        args,
    )


def solution(mesh):
    return jax.shard_map(
        functools.partial(shards, mesh.shape["row"], mesh.shape["col"]),
        mesh=mesh,
        in_specs=(P("row", "col"), P("row", "col", None), P("row", "col", None), P(), P()),
        out_specs=(P("row", "col", None), P("row", "col", None, None)),
        check_vma=False,
    )
```

```python
import functools
import jax
import jax.numpy as jnp
from jax import lax
from jax.experimental import pallas as pl
from jax.experimental.pallas import tpu as pltpu
from jax.sharding import PartitionSpec as P

F32 = jnp.float32
BF16 = jnp.bfloat16
HIGHEST = lax.Precision.HIGHEST
B = 128
MIB = 2**20


def sub_row(v, k):
    return jnp.broadcast_to(v[k : k + 1, :], v.shape)


def lane_col(v, c):
    return jnp.broadcast_to(v[:, c : c + 1], v.shape)


def inverse_factor(rows):
    lane = lax.broadcasted_iota(jnp.int32, (8, B), 1)
    sub = lax.broadcasted_iota(jnp.int32, (8, B), 0)
    work, out = list(rows), []
    for p in range(len(rows)):
        base = 8 * p
        cols = {q: [lane_col(work[q], base + j) for j in range(8)] for q in range(p, len(rows))}
        t = list(cols[p])
        in_panel = (lane >= base) & (lane < base + 8)
        r = jnp.where(in_panel, jnp.where(lane - base == sub, 1.0, 0.0).astype(F32), work[p])
        g = jnp.zeros((8, B), F32)
        for k in range(0, 8, 2):
            a, b, c = sub_row(t[k], k), sub_row(t[k], k + 1), sub_row(t[k + 1], k + 1)
            det = a * c - b * b
            inv = 1.0 / det
            pivot = (sub == k) | (sub == k + 1)
            t0 = jnp.where(pivot, jnp.where(sub == k, -1.0, 0.0).astype(F32), t[k])
            t1 = jnp.where(pivot, jnp.where(sub == k, 0.0, -1.0).astype(F32), t[k + 1])
            alpha = (t0 * c - t1 * b) * inv
            beta = (t1 * a - t0 * b) * inv
            x, y = sub_row(r, k), sub_row(r, k + 1)
            g0 = x * lax.rsqrt(a)
            g1 = (a * y - b * x) * lax.rsqrt(a * det)
            g = jnp.where(sub == k, g0, jnp.where(sub == k + 1, g1, g))
            r = jnp.where(pivot, 0.0, r) - alpha * x - beta * y
            for j in range(k + 2, 8):
                t[j] = jnp.where(pivot, 0.0, t[j]) - alpha * sub_row(t[j], k) - beta * sub_row(t[j], k + 1)
        out.append(jnp.where(lane <= sub + base, g, 0.0))
        z = [sub_row(r, j) for j in range(8)]
        for q in range(p + 1, len(rows)):
            acc = jnp.where(in_panel, 0.0, work[q])
            for j in range(8):
                acc = acc - cols[q][j] * z[j]
            work[q] = acc
    return out


def eliminate(w, g, y, k0, k1, blocks):
    for k in range(k0, k1):
        lo = B * k
        rows = [w[lo + 8 * q : lo + 8 * q + 8, lo : lo + B] for q in range(B // 8)]
        for q, piece in enumerate(inverse_factor(rows)):
            g[8 * q : 8 * q + 8, :] = piece
        y[...] = jnp.dot(g[...], w[lo : lo + B, :], precision=HIGHEST, preferred_element_type=F32)
        y[:, lo : lo + B] = g[...]
        w[lo : lo + B, :] = y[...]

        def body(i, carry):
            at = pl.multiple_of(i * B, B)
            w[pl.ds(at, B), lo : lo + B] = jnp.zeros((B, B), F32)
            w[pl.ds(at, B), :] -= lax.dot_general(
                y[:, pl.ds(at, B)], y[...], (((0,), (0,)), ((), ())), precision=HIGHEST, preferred_element_type=F32
            )
            return carry

        if k + 1 < blocks:
            lax.fori_loop(k + 1, blocks, body, 0)


def first_kernel(k1, blocks, masks, place, near, far, w, g, y):
    height, width = near.shape[1:]
    me_row, me_col = place[0], place[1]
    core = me_row % 2
    for m, (even, odd) in enumerate(masks):
        for flip, buf in ((0, near), (1, far)):
            odd_core = (core + flip) % 2
            row = (me_row ^ flip) ^ jnp.where(odd_core == 0, even[0], odd[0])
            col = me_col ^ jnp.where(odd_core == 0, even[1], odd[1])
            w[pl.ds(pl.multiple_of(row * height, 8), height), pl.ds(pl.multiple_of(col * width, B), width)] = buf[m]
    eliminate(w, g, y, 0, k1, blocks)


def whole_kernel(k1, blocks, w_in, w, g, y):
    w[...] = w_in[...]
    eliminate(w, g, y, 0, k1, blocks)


def next_kernel(k0, k1, blocks, w_in, w, g, y):
    w[...] = w_in[...]
    eliminate(w, g, y, k0, k1, blocks)


VM = pl.BlockSpec(memory_space=pltpu.VMEM)
SM = pl.BlockSpec(memory_space=pltpu.SMEM)


def elimination_call(kernel, order, specs, args):
    return pl.pallas_call(
        kernel,
        out_shape=jax.ShapeDtypeStruct((order, order), F32),
        in_specs=specs,
        out_specs=VM,
        scratch_shapes=[pltpu.VMEM((B, B), F32), pltpu.VMEM((B, order), F32)],
        compiler_params=pltpu.CompilerParams(vmem_limit_bytes=20 * MIB),
        cost_estimate=pl.CostEstimate(flops=4 * 10**9, bytes_accessed=8 * MIB, transcendentals=0),
    )(*args)


def split(v):
    high = v.astype(BF16)
    return high, (v - high.astype(F32)).astype(BF16)


def dot_tt(a, b):
    return lax.dot_general(a, b, (((1,), (1,)), ((), ())), preferred_element_type=F32)


def solve_kernel(masks, joined, n_own, n_all, width_cols, rank_max, *refs):
    if joined:
        inv, own, tgt, solved, core, xh, xl, ih, il, sh, sl = refs
    else:
        place, inv, own, near, far, solved, core, xh, xl, ih, il, sh, sl = refs
    blocks = inv.shape[0] // B
    for i in range(blocks):
        rows = slice(B * i, B * i + B)
        wide = B * (i + 1)
        ih[rows, :wide], il[rows, :wide] = split(inv[rows, :wide])
        if i % 2 == 0:
            ih[rows, wide : wide + B] = jnp.zeros((B, B), BF16)
            il[rows, wide : wide + B] = jnp.zeros((B, B), BF16)
    for c in range(blocks):
        xh[:n_own, B * c : B * c + B], xl[:n_own, B * c : B * c + B] = split(own[c])
        if joined:
            xh[n_own:, B * c : B * c + B], xl[n_own:, B * c : B * c + B] = split(tgt[c])
    if not joined:
        height, width = near.shape[1:]
        me_row, me_col = place[0], place[1]
        core_bit = me_row % 2
        for m, (even, odd) in enumerate(masks):
            for flip, buf in ((0, near), (1, far)):
                odd_core = (core_bit + flip) % 2
                row = (me_row ^ flip) ^ jnp.where(odd_core == 0, even[0], odd[0])
                col = me_col ^ jnp.where(odd_core == 0, even[1], odd[1])
                part = place[2 + row]
                high, low = split(buf[m])
                at = (pl.ds(pl.multiple_of(n_own + part * height, 16), height), pl.ds(pl.multiple_of(col * width, B), width))
                xh[at] = high
                xl[at] = low
    own_rows, tgt_rows = slice(0, n_own), (n_all - n_own) // 2

    def rows_of(at, keep):
        for i in range(blocks // 2):
            deep = 2 * B * (i + 1)
            out = slice(2 * B * i, deep)
            h, l = xh[at, :deep], xl[at, :deep]
            gh, gl = ih[out, :deep], il[out, :deep]
            res = dot_tt(h, gh) + dot_tt(h, gl) + dot_tt(l, gh)
            sh[at, out], sl[at, out] = split(res)
            if keep:
                solved[2 * i] = res[:, :B]
                solved[2 * i + 1] = res[:, B:]

    rows_of(own_rows, True)

    def body(t, carry):
        rows_of(pl.ds(pl.multiple_of(n_own + t * tgt_rows, 16), tgt_rows), False)
        return carry

    lax.fori_loop(0, 2, body, 0)
    oh, ol = sh.at[:n_own], sl.at[:n_own]

    def core_body(j, carry):
        at = pl.ds(pl.multiple_of(n_own + 2 * j * rank_max, 16), 2 * rank_max)
        h, l = sh[at, :], sl[at, :]
        res = dot_tt(oh[...], h) + dot_tt(oh[...], l) + dot_tt(ol[...], h)
        core[2 * j, :, :rank_max] = res[:, :rank_max]
        core[2 * j + 1, :, :rank_max] = res[:, rank_max:]
        return carry

    lax.fori_loop(0, width_cols // 2, core_body, 0)


def rows_iota(shape):
    return lax.broadcasted_iota(jnp.int32, shape, 0)


def pack_kernel(offs, ranks, t_slot, t_rank, left, right, v, u, t, pv, pu):
    slots, rank_max, width = right.shape
    total = v.shape[0]
    rows = rows_iota((rank_max, width))
    for j in range(t.shape[0]):
        t[j] = jnp.where(rows < t_rank[j], right[t_slot[j]], 0.0)
    pv[...] = jnp.zeros_like(pv)
    pu[...] = jnp.zeros_like(pu)
    for s in range(slots):
        at = pl.ds(offs[s], rank_max)
        keep = rows < ranks[s]
        pv[at, :] = jnp.where(keep, right[s], 0.0)
        pu[at, :] = jnp.where(keep, left[s], 0.0)
    v[...] = pv[:total]
    u[...] = pu[:total]


def unpack_kernel(offs, ranks, packed, out, held):
    slots, rank_max, width = out.shape
    held[: packed.shape[0]] = packed[...]
    rows = rows_iota((rank_max, width))
    for s in range(slots):
        out[s] = jnp.where(rows < ranks[s], held[pl.ds(offs[s], rank_max), :], 0.0)


def update_kernel(n, group, count, spots, offs, ranks, tiles, col, core, *refs):
    pieces, (out, us, cs, u, sems) = refs[:count], refs[count:]
    step = pl.program_id(0)
    rank_max = out.shape[2]
    total = pieces[0].shape[0]

    @pl.when(step == 0)
    def _():
        def fetch(i):
            return pltpu.make_async_copy(pieces[i], us.at[jnp.maximum(spots[i], 0), :total], sems.at[i])

        cores = pltpu.make_async_copy(core, cs.at[:total], sems.at[count])
        cores.start()
        for i in range(count):
            pl.when(spots[i] >= 0)(fetch(i).start)
        us[:, total:] = jnp.zeros((n, rank_max, B), F32)
        cores.wait()
        for i in range(count):
            pl.when(spots[i] >= 0)(fetch(i).wait)

    rows = rows_iota((rank_max, B))
    for s in range(group):
        slot = step * group + s
        at = pl.ds(offs[slot], rank_max)
        for k in range(n):
            lanes = slice(B * k, B * k + B)
            u[:rank_max, lanes], u[rank_max:, lanes] = split(us[k, at, :])
        keep = rows < jnp.where(tiles[slot] >= col[0], ranks[slot], 0)
        c = jnp.where(keep, cs[at, :], 0.0)
        ch, cl = split(jnp.transpose(c)[:rank_max])
        w = u[...]
        res = jnp.dot(jnp.concatenate([ch, ch], axis=1), w, preferred_element_type=F32)
        out[s, 0] = res + jnp.dot(cl, w[:rank_max], preferred_element_type=F32)


def phases(rows, cols):
    even = []
    bit = cols // 2
    while bit > 1:
        even.append((0, bit))
        bit //= 2
    bit = rows // 2
    while bit > 2:
        even.append((bit, 0))
        bit //= 2
    odd = even + [(2, 0), (0, 1)]
    even = even + [(0, 1), (2, 0)]
    return even, odd


def gather_masks(rows, cols):
    even, odd = phases(rows, cols)

    def masks(steps):
        got = [(0, 0)]
        for r, c in steps:
            got = got + [(a ^ r, b ^ c) for a, b in got]
        return got

    return list(zip(masks(even), masks(odd)))


def link_pairs(rows, cols, even, odd):
    pairs = []
    for r in range(rows):
        dr, dc = odd if r % 2 else even
        for c in range(cols):
            pairs.append((r * cols + c, (r ^ dr) * cols + (c ^ dc)))
    return pairs


def tie(*values):
    return lax.optimization_barrier(values)


def table(values, index):
    return jnp.array(values, jnp.int32)[index]


def body(rows, cols, total, args):
    diag_tile, left, right, ranks, tile_rows = args
    slots, rank_max, piece_rows = left.shape
    order = piece_rows * cols
    blocks = order // B
    group = slots // cols
    n_own, n_tgt = total // cols, cols * rank_max
    n_all = n_own + n_tgt
    row_index = lax.axis_index("row")
    col_index = lax.axis_index("col")
    masks = gather_masks(rows, cols)
    fits = piece_rows % B == 0 and blocks == cols
    own_ranks = lax.dynamic_slice_in_dim(ranks, row_index * slots, slots)
    own_tiles = lax.dynamic_slice_in_dim(tile_rows, row_index * slots, slots)
    before = jnp.arange(slots, dtype=jnp.int32)
    offs = jnp.sum(jnp.where(before[None, :] < before[:, None], own_ranks[None, :], 0), axis=1)
    wanted = jnp.arange(cols, dtype=jnp.int32)
    every_slot = jnp.arange(tile_rows.shape[0], dtype=jnp.int32)
    hit = tile_rows[None, :] == wanted[:, None]
    holder = jnp.sum(jnp.where(hit, every_slot[None, :], 0), axis=1)
    t_rank = jnp.sum(jnp.where(hit, ranks[None, :], 0), axis=1)
    t_rank = jnp.where(holder // slots == row_index, t_rank, 0)

    v, u, part = pl.pallas_call(
        pack_kernel,
        out_shape=[
            jax.ShapeDtypeStruct((total, piece_rows), F32),
            jax.ShapeDtypeStruct((total, piece_rows), F32),
            jax.ShapeDtypeStruct((cols, rank_max, piece_rows), F32),
        ],
        in_specs=[SM] * 4 + [VM] * 2,
        out_specs=[VM] * 3,
        scratch_shapes=[pltpu.VMEM((total + rank_max, piece_rows), F32)] * 2,
        compiler_params=pltpu.CompilerParams(vmem_limit_bytes=24 * MIB),
    )(offs, own_ranks, holder % slots, t_rank, left, right)

    length = cols // 2
    up, down, cross = [u], [u], []

    def along(step):
        if step < length:
            up.append(lax.ppermute(up[-1], "col", [(c, c + 2) for c in range(2 * step - 2, cols - 2)]))
            down.append(lax.ppermute(down[-1], "col", [(c + 2, c) for c in range(cols - 2 * step)]))

    def reach(z):
        ways = [(k, 0 if (z >= k) == (side == (z >= length // 2)) else 1, side) for k in range(1, length) for side in (True, False)]
        return [(side, k) for k, _, side in sorted(ways) if (z >= k if side else z + k < length)]

    paths = [reach(z) for z in range(length)]
    here = col_index // 2

    def over(step):
        if 0 < step < length:
            picks = [paths[z][step - 1] for z in range(length)]
            piece = None
            for pick in sorted(set(picks)):
                side, k = pick
                got = (up if side else down)[k]
                if piece is None:
                    piece = got
                else:
                    at = functools.reduce(jnp.logical_or, [here == z for z in range(length) if picks[z] == pick])
                    piece = jnp.where(at, got, piece)
            up[step], down[step], piece = tie(up[step], down[step], piece)
            cross.append(lax.ppermute(piece, "col", [(c, c ^ 1) for c in range(cols)]))

    def along_tie(x, step):
        if step < length:
            x, up[step], down[step] = tie(x, up[step], down[step])
        return x

    def over_tie(x, step):
        if step < length:
            x, cross[step] = tie(x, cross[step])
        return x

    even, odd = phases(rows, cols)
    links = len(even)
    swap = [(r, r ^ 1) for r in range(rows)]

    t_steps = []
    bit = 1
    while bit < rows:
        t_steps.append(("sum", bit))
        bit *= 2
    t_steps += [("link", i) for i in range(links)] + [("core", 0)]
    state = dict(part=part, t=None, t_far=None)

    def t_step():
        if not t_steps:
            return
        kind, which = t_steps.pop(0)
        if kind == "sum":
            p = state["part"]
            h = p.shape[0] // 2
            side = (row_index // which) % 2
            kept = lax.dynamic_slice_in_dim(p, side * h, h, 0)
            sent = lax.dynamic_slice_in_dim(p, (1 - side) * h, h, 0)
            state["part"] = kept + lax.ppermute(sent, "row", [(r, r ^ which) for r in range(rows)])
            if t_steps[0][0] == "link":
                p = state["part"]
                state["per"] = p.shape[0]
                state["t"] = p.reshape(1, p.shape[0] * rank_max, piece_rows)
        elif kind == "link":
            t = state["t"]
            got = lax.ppermute(t, ("row", "col"), link_pairs(rows, cols, even[which], odd[which]))
            state["t"] = jnp.concatenate([t, got], axis=0)
        else:
            state["t_far"] = lax.ppermute(state["t"], "row", swap)

    def t_tie(x):
        key = "t" if state["t"] is not None else "part"
        x, state[key] = tie(x, state[key])
        return x

    near = diag_tile[None]
    for i in range(links):
        got = lax.ppermute(near, ("row", "col"), link_pairs(rows, cols, even[i], odd[i]))
        if i:
            t_step()
        near = jnp.concatenate([near, got], axis=0)
        near = t_tie(near) if i else near
        if i == 1:
            near, u = tie(near, u)
            up[0] = down[0] = u
            cross.append(lax.ppermute(u, "col", [(c, c ^ 1) for c in range(cols)]))
            along(1)
    far = lax.ppermute(near, "row", swap)
    t_step()
    far = t_tie(far)

    far, v = tie(far, v)
    own = lax.all_to_all(v.reshape(cols, n_own, piece_rows), "col", split_axis=0, concat_axis=0, tiled=True)

    places = []
    for r in range(rows):
        at, h, bb = 0, rows // 2, 1
        while bb < rows:
            at += h * ((r // bb) % 2)
            h //= 2
            bb *= 2
        places.append(at)

    def sources():
        near_m = jnp.where(row_index % 2 == 0, table([e for e, _ in masks], slice(None)), table([o for _, o in masks], slice(None)))
        far_m = jnp.where(row_index % 2 == 0, table([o for _, o in masks], slice(None)), table([e for e, _ in masks], slice(None)))
        r = jnp.concatenate([row_index ^ near_m[:, 0], row_index ^ 1 ^ far_m[:, 0]])
        c = jnp.concatenate([col_index ^ near_m[:, 1], col_index ^ far_m[:, 1]])
        return r, c

    place = jnp.concatenate([jnp.stack([row_index, col_index]).astype(jnp.int32), jnp.array(places, jnp.int32)])
    per_call = 2
    t_step()
    if fits:
        inv = elimination_call(
            functools.partial(first_kernel, per_call, blocks, masks), order, [SM, VM, VM], (place, near, far)
        )
    else:
        r, c = sources()
        pieces = jnp.concatenate([near, far], axis=0)
        tile = jnp.zeros((rows * cols,) + pieces.shape[1:], F32).at[r * cols + c].set(pieces)
        tile = tile.reshape(rows, cols, order // rows, piece_rows).transpose(0, 2, 1, 3).reshape(order, order)
        inv = elimination_call(functools.partial(whole_kernel, per_call, blocks), order, [VM], (tile,))
    inv = t_tie(inv)
    for k in range(per_call, blocks, per_call):
        while t_steps:
            t_step()
        if k == per_call:
            inv = over_tie(along_tie(inv, 1), 0)
            over(1)
            along(2)
        if k == 2 * per_call:
            inv, own, state["t_far"] = tie(along_tie(inv, 2), own, state["t_far"])
            over(2)
            along(3)
        if k == 3 * per_call:
            inv = over_tie(inv, 1)
        inv = elimination_call(functools.partial(next_kernel, k, k + per_call, blocks), order, [VM], (inv,))
    t_near, t_far = state["t"], state["t_far"]
    per = state["per"]

    inv = over_tie(along_tie(inv, 3), 2)
    own = own.reshape(cols, n_own, piece_rows)
    if fits:
        specs, operands = [SM, VM, VM, VM, VM], (place, inv, own, t_near, t_far)
    else:
        own = own.transpose(1, 0, 2).reshape(n_own, blocks, B).transpose(1, 0, 2)
        r, c = sources()
        spots = table(places, r)
        pieces = jnp.concatenate([t_near, t_far], axis=0)
        tgt = jnp.zeros((rows * cols,) + pieces.shape[1:], F32).at[spots * cols + c].set(pieces)
        tgt = tgt.reshape(rows, cols, per * rank_max, piece_rows).transpose(0, 2, 1, 3).reshape(n_tgt, blocks, B)
        specs, operands = [VM, VM, VM], (inv, own, tgt.transpose(1, 0, 2))
    solved, core = pl.pallas_call(
        functools.partial(solve_kernel, masks, not fits, n_own, n_all, cols, rank_max),
        out_shape=[
            jax.ShapeDtypeStruct((blocks, n_own, B), F32),
            jax.ShapeDtypeStruct((cols, n_own, B), F32),
        ],
        in_specs=specs,
        out_specs=[VM, VM],
        scratch_shapes=[pltpu.VMEM((n_all, order), BF16)] * 2
        + [pltpu.VMEM((order, order), BF16)] * 2
        + [pltpu.VMEM((n_all, order), BF16)] * 2,
        compiler_params=pltpu.CompilerParams(vmem_limit_bytes=34 * MIB),
        cost_estimate=pl.CostEstimate(flops=6 * 10**9, bytes_accessed=12 * MIB, transcendentals=0),
    )(*operands)
    if not fits:
        solved = solved.transpose(1, 0, 2).reshape(n_own, cols, piece_rows).transpose(1, 0, 2)
    over(3)
    for step in range(4, length):
        along(step)
        core = over_tie(along_tie(core, step), step - 1)
        over(step)
    core = lax.all_to_all(core, "col", split_axis=0, concat_axis=0, tiled=True).reshape(total, B)
    solved, core, cross[-1] = tie(solved, core, cross[-1])
    back = lax.all_to_all(solved, "col", split_axis=0, concat_axis=0, tiled=True).reshape(total, piece_rows)
    own_rows = pl.pallas_call(
        unpack_kernel,
        out_shape=jax.ShapeDtypeStruct((slots, rank_max, piece_rows), F32),
        in_specs=[SM, SM, VM],
        out_specs=VM,
        scratch_shapes=[pltpu.VMEM((total + rank_max, piece_rows), F32)],
        compiler_params=pltpu.CompilerParams(vmem_limit_bytes=16 * MIB),
    )(offs, own_ranks, back)

    pieces = [u] + up[1:] + down[1:] + cross
    spots = [col_index]
    spots += [jnp.where(col_index >= 2 * k, col_index - 2 * k, -1) for k in range(1, length)]
    spots += [jnp.where(col_index < cols - 2 * k, col_index + 2 * k, -1) for k in range(1, length)]
    spots += [col_index ^ 1]
    for step in range(1, length):
        origin = [z - paths[z][step - 1][1] if paths[z][step - 1][0] else z + paths[z][step - 1][1] for z in range(length)]
        spots.append((2 * table(origin, here) + col_index % 2) ^ 1)
    spots = jnp.stack(spots).astype(jnp.int32)
    if fits:
        anyspec = pl.BlockSpec(memory_space=pl.ANY)
        update = pl.pallas_call(
            functools.partial(update_kernel, cols, group, len(pieces)),
            out_shape=jax.ShapeDtypeStruct((slots, 1, rank_max, order), F32),
            grid_spec=pltpu.PrefetchScalarGridSpec(
                num_scalar_prefetch=5,
                grid=(cols,),
                in_specs=[anyspec] * (len(pieces) + 1),
                out_specs=pl.BlockSpec((group, 1, rank_max, order), lambda c, *_: (c, 0, 0, 0)),
                scratch_shapes=[
                    pltpu.VMEM((cols, total + rank_max, B), F32),
                    pltpu.VMEM((total + rank_max, B), F32),
                    pltpu.VMEM((2 * rank_max, order), BF16),
                    pltpu.SemaphoreType.DMA((len(pieces) + 1,)),
                ],
            ),
            compiler_params=pltpu.CompilerParams(vmem_limit_bytes=60 * MIB),
            cost_estimate=pl.CostEstimate(flops=2 * 10**9, bytes_accessed=24 * MIB, transcendentals=0),
        )(spots, offs, own_ranks, own_tiles, col_index[None].astype(jnp.int32), core, *pieces)
        update = jnp.transpose(update, (0, 1, 3, 2))
    else:
        where = jnp.where(spots < 0, cols, spots)
        full = jnp.zeros((cols + 1, total, piece_rows), F32)
        for i, piece in enumerate(pieces):
            full = lax.dynamic_update_index_in_dim(full, piece, where[i], 0)
        full = full[:cols].transpose(1, 0, 2).reshape(total, order)
        index = offs[:, None] + jnp.arange(rank_max, dtype=jnp.int32)[None, :]
        index = jnp.minimum(index, total - 1)
        keep = (jnp.arange(rank_max, dtype=jnp.int32)[None, :] < own_ranks[:, None]) & (own_tiles >= col_index)[:, None]
        cs = jnp.where(keep[:, :, None], core[index][:, :, :rank_max], 0.0)
        update = jnp.einsum("srn,srq->snq", full[index], cs, precision=HIGHEST)[:, None]
    return (jnp.transpose(own_rows, (0, 2, 1)), update)


def shards(rows, cols, diag_tile, panel_left, panel_right, ranks, tile_rows):
    slots, _, rank_max = panel_left.shape
    args = (diag_tile, jnp.transpose(panel_left, (0, 2, 1)), jnp.transpose(panel_right, (0, 2, 1)), ranks, tile_rows)
    most = slots * rank_max
    grain = 16 * cols
    sizes = sorted({-(-(most * part) // (24 * grain)) * grain for part in (17, 18, 24)})
    need = jnp.max(jnp.sum(ranks.reshape(rows, slots), axis=1))
    which = sum((need > size).astype(jnp.int32) for size in sizes[:-1])
    return lax.switch(which, [functools.partial(body, rows, cols, size) for size in sizes], args)


def solution(mesh):
    return jax.shard_map(
        functools.partial(shards, mesh.shape["row"], mesh.shape["col"]),
        mesh=mesh,
        in_specs=(P("row", "col"), P("row", "col", None), P("row", "col", None), P(), P()),
        out_specs=(P("row", "col", None), P("row", "col", None, None)),
        check_vma=False,
    )
```

```python
import functools
import jax
import jax.numpy as jnp
from jax import lax
from jax.experimental import pallas as pl
from jax.experimental.pallas import tpu as pltpu
from jax.sharding import PartitionSpec as P

F32 = jnp.float32
BF16 = jnp.bfloat16
HIGHEST = lax.Precision.HIGHEST
B = 128
MIB = 2**20


def sub_row(v, k):
    return jnp.broadcast_to(v[k : k + 1, :], v.shape)


def lane_col(v, c):
    return jnp.broadcast_to(v[:, c : c + 1], v.shape)


def inverse_factor(rows):
    lane = lax.broadcasted_iota(jnp.int32, (8, B), 1)
    sub = lax.broadcasted_iota(jnp.int32, (8, B), 0)
    work, out = list(rows), []
    for p in range(len(rows)):
        base = 8 * p
        cols = {q: [lane_col(work[q], base + j) for j in range(8)] for q in range(p, len(rows))}
        t = list(cols[p])
        in_panel = (lane >= base) & (lane < base + 8)
        r = jnp.where(in_panel, jnp.where(lane - base == sub, 1.0, 0.0).astype(F32), work[p])
        g = jnp.zeros((8, B), F32)
        for k in range(0, 8, 2):
            a, b, c = sub_row(t[k], k), sub_row(t[k], k + 1), sub_row(t[k + 1], k + 1)
            det = a * c - b * b
            inv = 1.0 / det
            pivot = (sub == k) | (sub == k + 1)
            t0 = jnp.where(pivot, jnp.where(sub == k, -1.0, 0.0).astype(F32), t[k])
            t1 = jnp.where(pivot, jnp.where(sub == k, 0.0, -1.0).astype(F32), t[k + 1])
            alpha = (t0 * c - t1 * b) * inv
            beta = (t1 * a - t0 * b) * inv
            x, y = sub_row(r, k), sub_row(r, k + 1)
            g0 = x * lax.rsqrt(a)
            g1 = (a * y - b * x) * lax.rsqrt(a * det)
            g = jnp.where(sub == k, g0, jnp.where(sub == k + 1, g1, g))
            r = jnp.where(pivot, 0.0, r) - alpha * x - beta * y
            for j in range(k + 2, 8):
                t[j] = jnp.where(pivot, 0.0, t[j]) - alpha * sub_row(t[j], k) - beta * sub_row(t[j], k + 1)
        out.append(jnp.where(lane <= sub + base, g, 0.0))
        z = [sub_row(r, j) for j in range(8)]
        for q in range(p + 1, len(rows)):
            acc = jnp.where(in_panel, 0.0, work[q])
            for j in range(8):
                acc = acc - cols[q][j] * z[j]
            work[q] = acc
    return out


def eliminate(w, g, y, k0, k1, blocks):
    for k in range(k0, k1):
        lo = B * k
        rows = [w[lo + 8 * q : lo + 8 * q + 8, lo : lo + B] for q in range(B // 8)]
        for q, piece in enumerate(inverse_factor(rows)):
            g[8 * q : 8 * q + 8, :] = piece
        y[...] = jnp.dot(g[...], w[lo : lo + B, :], precision=HIGHEST, preferred_element_type=F32)
        y[:, lo : lo + B] = g[...]
        w[lo : lo + B, :] = y[...]

        def body(i, carry):
            at = pl.multiple_of(i * B, B)
            w[pl.ds(at, B), lo : lo + B] = jnp.zeros((B, B), F32)
            w[pl.ds(at, B), :] -= lax.dot_general(
                y[:, pl.ds(at, B)], y[...], (((0,), (0,)), ((), ())), precision=HIGHEST, preferred_element_type=F32
            )
            return carry

        if k + 1 < blocks:
            lax.fori_loop(k + 1, blocks, body, 0)


def first_kernel(k1, blocks, masks, place, near, far, w, g, y):
    height, width = near.shape[1:]
    me_row, me_col = place[0], place[1]
    core = me_row % 2
    for m, (even, odd) in enumerate(masks):
        for flip, buf in ((0, near), (1, far)):
            odd_core = (core + flip) % 2
            row = (me_row ^ flip) ^ jnp.where(odd_core == 0, even[0], odd[0])
            col = me_col ^ jnp.where(odd_core == 0, even[1], odd[1])
            w[pl.ds(pl.multiple_of(row * height, 8), height), pl.ds(pl.multiple_of(col * width, B), width)] = buf[m]
    eliminate(w, g, y, 0, k1, blocks)


def whole_kernel(k1, blocks, w_in, w, g, y):
    w[...] = w_in[...]
    eliminate(w, g, y, 0, k1, blocks)


def next_kernel(k0, k1, blocks, w_in, w, g, y):
    w[...] = w_in[...]
    eliminate(w, g, y, k0, k1, blocks)


VM = pl.BlockSpec(memory_space=pltpu.VMEM)
SM = pl.BlockSpec(memory_space=pltpu.SMEM)


def elimination_call(kernel, order, specs, args):
    return pl.pallas_call(
        kernel,
        out_shape=jax.ShapeDtypeStruct((order, order), F32),
        in_specs=specs,
        out_specs=VM,
        scratch_shapes=[pltpu.VMEM((B, B), F32), pltpu.VMEM((B, order), F32)],
        compiler_params=pltpu.CompilerParams(vmem_limit_bytes=20 * MIB),
        cost_estimate=pl.CostEstimate(flops=4 * 10**9, bytes_accessed=8 * MIB, transcendentals=0),
    )(*args)


def split(v):
    high = v.astype(BF16)
    return high, (v - high.astype(F32)).astype(BF16)


def dot_tt(a, b):
    return lax.dot_general(a, b, (((1,), (1,)), ((), ())), preferred_element_type=F32)


def solve_kernel(masks, joined, n_own, n_all, width_cols, rank_max, *refs):
    if joined:
        inv, own, tgt, solved, core, xh, xl, ih, il, sh, sl = refs
    else:
        place, inv, own, near, far, solved, core, xh, xl, ih, il, sh, sl = refs
    blocks = inv.shape[0] // B
    for i in range(blocks):
        rows = slice(B * i, B * i + B)
        wide = B * (i + 1)
        ih[rows, :wide], il[rows, :wide] = split(inv[rows, :wide])
        if i % 2 == 0:
            ih[rows, wide : wide + B] = jnp.zeros((B, B), BF16)
            il[rows, wide : wide + B] = jnp.zeros((B, B), BF16)
    for c in range(blocks):
        xh[:n_own, B * c : B * c + B], xl[:n_own, B * c : B * c + B] = split(own[c])
        if joined:
            xh[n_own:, B * c : B * c + B], xl[n_own:, B * c : B * c + B] = split(tgt[c])
    if not joined:
        height, width = near.shape[1:]
        me_row, me_col = place[0], place[1]
        core_bit = me_row % 2
        for m, (even, odd) in enumerate(masks):
            for flip, buf in ((0, near), (1, far)):
                odd_core = (core_bit + flip) % 2
                row = (me_row ^ flip) ^ jnp.where(odd_core == 0, even[0], odd[0])
                col = me_col ^ jnp.where(odd_core == 0, even[1], odd[1])
                part = place[2 + row]
                high, low = split(buf[m])
                at = (pl.ds(pl.multiple_of(n_own + part * height, 16), height), pl.ds(pl.multiple_of(col * width, B), width))
                xh[at] = high
                xl[at] = low
    own_rows, tgt_rows = slice(0, n_own), (n_all - n_own) // 2

    def rows_of(at, keep):
        for i in range(blocks // 2):
            deep = 2 * B * (i + 1)
            out = slice(2 * B * i, deep)
            h, l = xh[at, :deep], xl[at, :deep]
            gh, gl = ih[out, :deep], il[out, :deep]
            res = dot_tt(h, gh) + dot_tt(h, gl) + dot_tt(l, gh)
            sh[at, out], sl[at, out] = split(res)
            if keep:
                solved[2 * i] = res[:, :B]
                solved[2 * i + 1] = res[:, B:]

    rows_of(own_rows, True)

    def body(t, carry):
        rows_of(pl.ds(pl.multiple_of(n_own + t * tgt_rows, 16), tgt_rows), False)
        return carry

    lax.fori_loop(0, 2, body, 0)
    oh, ol = sh.at[:n_own], sl.at[:n_own]

    def core_body(j, carry):
        at = pl.ds(pl.multiple_of(n_own + 2 * j * rank_max, 16), 2 * rank_max)
        h, l = sh[at, :], sl[at, :]
        res = dot_tt(oh[...], h) + dot_tt(oh[...], l) + dot_tt(ol[...], h)
        core[2 * j, :, :rank_max] = res[:, :rank_max]
        core[2 * j + 1, :, :rank_max] = res[:, rank_max:]
        return carry

    lax.fori_loop(0, width_cols // 2, core_body, 0)


def rows_iota(shape):
    return lax.broadcasted_iota(jnp.int32, shape, 0)


def pack_kernel(offs, ranks, t_slot, t_rank, left, right, v, u, t, pv, pu):
    slots, rank_max, width = right.shape
    total = v.shape[0]
    rows = rows_iota((rank_max, width))
    for j in range(t.shape[0]):
        t[j] = jnp.where(rows < t_rank[j], right[t_slot[j]], 0.0)
    pv[...] = jnp.zeros_like(pv)
    pu[...] = jnp.zeros_like(pu)
    for s in range(slots):
        at = pl.ds(offs[s], rank_max)
        keep = rows < ranks[s]
        pv[at, :] = jnp.where(keep, right[s], 0.0)
        pu[at, :] = jnp.where(keep, left[s], 0.0)
    v[...] = pv[:total]
    u[...] = pu[:total]


def unpack_kernel(offs, ranks, packed, out, held):
    slots, rank_max, width = out.shape
    held[: packed.shape[0]] = packed[...]
    rows = rows_iota((rank_max, width))
    for s in range(slots):
        out[s] = jnp.where(rows < ranks[s], held[pl.ds(offs[s], rank_max), :], 0.0)


def update_kernel(n, group, count, spots, offs, ranks, tiles, col, core, *refs):
    pieces, (out, us, cs, u, sems) = refs[:count], refs[count:]
    step = pl.program_id(0)
    rank_max = out.shape[2]
    total = pieces[0].shape[0]

    @pl.when(step == 0)
    def _():
        def fetch(i):
            return pltpu.make_async_copy(pieces[i], us.at[jnp.maximum(spots[i], 0), :total], sems.at[i])

        cores = pltpu.make_async_copy(core, cs.at[:total], sems.at[count])
        cores.start()
        for i in range(count):
            pl.when(spots[i] >= 0)(fetch(i).start)
        us[:, total:] = jnp.zeros((n, rank_max, B), F32)
        cores.wait()
        for i in range(count):
            pl.when(spots[i] >= 0)(fetch(i).wait)

    rows = rows_iota((rank_max, B))
    for s in range(group):
        slot = step * group + s
        at = pl.ds(offs[slot], rank_max)
        for k in range(n):
            lanes = slice(B * k, B * k + B)
            u[:rank_max, lanes], u[rank_max:, lanes] = split(us[k, at, :])
        keep = rows < jnp.where(tiles[slot] >= col[0], ranks[slot], 0)
        c = jnp.where(keep, cs[at, :], 0.0)
        ch, cl = split(jnp.transpose(c)[:rank_max])
        w = u[...]
        res = jnp.dot(jnp.concatenate([ch, ch], axis=1), w, preferred_element_type=F32)
        out[s, 0] = res + jnp.dot(cl, w[:rank_max], preferred_element_type=F32)


def phases(rows, cols):
    even = []
    bit = cols // 2
    while bit > 1:
        even.append((0, bit))
        bit //= 2
    bit = rows // 2
    while bit > 2:
        even.append((bit, 0))
        bit //= 2
    odd = even + [(2, 0), (0, 1)]
    even = even + [(0, 1), (2, 0)]
    return even, odd


def gather_masks(rows, cols):
    even, odd = phases(rows, cols)

    def masks(steps):
        got = [(0, 0)]
        for r, c in steps:
            got = got + [(a ^ r, b ^ c) for a, b in got]
        return got

    return list(zip(masks(even), masks(odd)))


def link_pairs(rows, cols, even, odd):
    pairs = []
    for r in range(rows):
        dr, dc = odd if r % 2 else even
        for c in range(cols):
            pairs.append((r * cols + c, (r ^ dr) * cols + (c ^ dc)))
    return pairs


def tie(*values):
    return lax.optimization_barrier(values)


def table(values, index):
    return jnp.array(values, jnp.int32)[index]


def body(rows, cols, total, args):
    diag_tile, left, right, ranks, tile_rows = args
    slots, rank_max, piece_rows = left.shape
    order = piece_rows * cols
    blocks = order // B
    group = slots // cols
    n_own, n_tgt = total // cols, cols * rank_max
    n_all = n_own + n_tgt
    row_index = lax.axis_index("row")
    col_index = lax.axis_index("col")
    masks = gather_masks(rows, cols)
    fits = piece_rows % B == 0 and blocks == cols
    own_ranks = lax.dynamic_slice_in_dim(ranks, row_index * slots, slots)
    own_tiles = lax.dynamic_slice_in_dim(tile_rows, row_index * slots, slots)
    before = jnp.arange(slots, dtype=jnp.int32)
    offs = jnp.sum(jnp.where(before[None, :] < before[:, None], own_ranks[None, :], 0), axis=1)
    wanted = jnp.arange(cols, dtype=jnp.int32)
    every_slot = jnp.arange(tile_rows.shape[0], dtype=jnp.int32)
    hit = tile_rows[None, :] == wanted[:, None]
    holder = jnp.sum(jnp.where(hit, every_slot[None, :], 0), axis=1)
    t_rank = jnp.sum(jnp.where(hit, ranks[None, :], 0), axis=1)
    t_rank = jnp.where(holder // slots == row_index, t_rank, 0)

    v, u, part = pl.pallas_call(
        pack_kernel,
        out_shape=[
            jax.ShapeDtypeStruct((total, piece_rows), F32),
            jax.ShapeDtypeStruct((total, piece_rows), F32),
            jax.ShapeDtypeStruct((cols, rank_max, piece_rows), F32),
        ],
        in_specs=[SM] * 4 + [VM] * 2,
        out_specs=[VM] * 3,
        scratch_shapes=[pltpu.VMEM((total + rank_max, piece_rows), F32)] * 2,
        compiler_params=pltpu.CompilerParams(vmem_limit_bytes=24 * MIB),
    )(offs, own_ranks, holder % slots, t_rank, left, right)

    length = cols // 2
    up, down, cross = [u], [u], []

    def along(step):
        if step < length:
            up.append(lax.ppermute(up[-1], "col", [(c, c + 2) for c in range(2 * step - 2, cols - 2)]))
            down.append(lax.ppermute(down[-1], "col", [(c + 2, c) for c in range(cols - 2 * step)]))

    def reach(z):
        ways = [(k, 0 if (z >= k) == (side == (z >= length // 2)) else 1, side) for k in range(1, length) for side in (True, False)]
        return [(side, k) for k, _, side in sorted(ways) if (z >= k if side else z + k < length)]

    paths = [reach(z) for z in range(length)]
    here = col_index // 2

    def over(step):
        if 0 < step < length:
            picks = [paths[z][step - 1] for z in range(length)]
            piece = None
            for pick in sorted(set(picks)):
                side, k = pick
                got = (up if side else down)[k]
                if piece is None:
                    piece = got
                else:
                    at = functools.reduce(jnp.logical_or, [here == z for z in range(length) if picks[z] == pick])
                    piece = jnp.where(at, got, piece)
            up[step], down[step], piece = tie(up[step], down[step], piece)
            cross.append(lax.ppermute(piece, "col", [(c, c ^ 1) for c in range(cols)]))

    def along_tie(x, step):
        if step < length:
            x, up[step], down[step] = tie(x, up[step], down[step])
        return x

    def over_tie(x, step):
        if step < length:
            x, cross[step] = tie(x, cross[step])
        return x

    even, odd = phases(rows, cols)
    links = len(even)
    swap = [(r, r ^ 1) for r in range(rows)]

    t_steps = []
    bit = 1
    while bit < rows:
        t_steps.append(("sum", bit))
        bit *= 2
    t_steps += [("link", i) for i in range(links)] + [("core", 0)]
    state = dict(part=part, t=None, t_far=None)

    def t_step():
        if not t_steps:
            return
        kind, which = t_steps.pop(0)
        if kind == "sum":
            p = state["part"]
            h = p.shape[0] // 2
            side = (row_index // which) % 2
            kept = lax.dynamic_slice_in_dim(p, side * h, h, 0)
            sent = lax.dynamic_slice_in_dim(p, (1 - side) * h, h, 0)
            state["part"] = kept + lax.ppermute(sent, "row", [(r, r ^ which) for r in range(rows)])
            if t_steps[0][0] == "link":
                p = state["part"]
                state["per"] = p.shape[0]
                state["t"] = p.reshape(1, p.shape[0] * rank_max, piece_rows)
        elif kind == "link":
            t = state["t"]
            got = lax.ppermute(t, ("row", "col"), link_pairs(rows, cols, even[which], odd[which]))
            state["t"] = jnp.concatenate([t, got], axis=0)
        else:
            state["t_far"] = lax.ppermute(state["t"], "row", swap)

    def t_tie(x):
        key = "t" if state["t"] is not None else "part"
        x, state[key] = tie(x, state[key])
        return x

    near = diag_tile[None]
    for i in range(links):
        got = lax.ppermute(near, ("row", "col"), link_pairs(rows, cols, even[i], odd[i]))
        t_step()
        near = jnp.concatenate([near, got], axis=0)
        near = t_tie(near)
        if i == 0:
            near, u = tie(near, u)
            up[0] = down[0] = u
            cross.append(lax.ppermute(u, "col", [(c, c ^ 1) for c in range(cols)]))
            along(1)
    far = lax.ppermute(near, "row", swap)
    t_step()
    far = t_tie(far)

    far, v = tie(far, v)
    own = lax.all_to_all(v.reshape(cols, n_own, piece_rows), "col", split_axis=0, concat_axis=0, tiled=True)

    places = []
    for r in range(rows):
        at, h, bb = 0, rows // 2, 1
        while bb < rows:
            at += h * ((r // bb) % 2)
            h //= 2
            bb *= 2
        places.append(at)

    def sources():
        near_m = jnp.where(row_index % 2 == 0, table([e for e, _ in masks], slice(None)), table([o for _, o in masks], slice(None)))
        far_m = jnp.where(row_index % 2 == 0, table([o for _, o in masks], slice(None)), table([e for e, _ in masks], slice(None)))
        r = jnp.concatenate([row_index ^ near_m[:, 0], row_index ^ 1 ^ far_m[:, 0]])
        c = jnp.concatenate([col_index ^ near_m[:, 1], col_index ^ far_m[:, 1]])
        return r, c

    place = jnp.concatenate([jnp.stack([row_index, col_index]).astype(jnp.int32), jnp.array(places, jnp.int32)])
    per_call = 2
    t_step()
    if fits:
        inv = elimination_call(
            functools.partial(first_kernel, per_call, blocks, masks), order, [SM, VM, VM], (place, near, far)
        )
    else:
        r, c = sources()
        pieces = jnp.concatenate([near, far], axis=0)
        tile = jnp.zeros((rows * cols,) + pieces.shape[1:], F32).at[r * cols + c].set(pieces)
        tile = tile.reshape(rows, cols, order // rows, piece_rows).transpose(0, 2, 1, 3).reshape(order, order)
        inv = elimination_call(functools.partial(whole_kernel, per_call, blocks), order, [VM], (tile,))
    inv = t_tie(inv)
    for k in range(per_call, blocks, per_call):
        while t_steps:
            t_step()
        if k == per_call:
            inv, own = tie(over_tie(along_tie(inv, 1), 0), own)
            over(1)
            along(2)
        if k == 2 * per_call:
            inv, state["t_far"] = tie(along_tie(inv, 2), state["t_far"])
            over(2)
            along(3)
        if k == 3 * per_call:
            inv = over_tie(inv, 1)
        inv = elimination_call(functools.partial(next_kernel, k, k + per_call, blocks), order, [VM], (inv,))
    t_near, t_far = state["t"], state["t_far"]
    per = state["per"]

    inv = over_tie(along_tie(inv, 3), 2)
    own = own.reshape(cols, n_own, piece_rows)
    if fits:
        specs, operands = [SM, VM, VM, VM, VM], (place, inv, own, t_near, t_far)
    else:
        own = own.transpose(1, 0, 2).reshape(n_own, blocks, B).transpose(1, 0, 2)
        r, c = sources()
        spots = table(places, r)
        pieces = jnp.concatenate([t_near, t_far], axis=0)
        tgt = jnp.zeros((rows * cols,) + pieces.shape[1:], F32).at[spots * cols + c].set(pieces)
        tgt = tgt.reshape(rows, cols, per * rank_max, piece_rows).transpose(0, 2, 1, 3).reshape(n_tgt, blocks, B)
        specs, operands = [VM, VM, VM], (inv, own, tgt.transpose(1, 0, 2))
    solved, core = pl.pallas_call(
        functools.partial(solve_kernel, masks, not fits, n_own, n_all, cols, rank_max),
        out_shape=[
            jax.ShapeDtypeStruct((blocks, n_own, B), F32),
            jax.ShapeDtypeStruct((cols, n_own, B), F32),
        ],
        in_specs=specs,
        out_specs=[VM, VM],
        scratch_shapes=[pltpu.VMEM((n_all, order), BF16)] * 2
        + [pltpu.VMEM((order, order), BF16)] * 2
        + [pltpu.VMEM((n_all, order), BF16)] * 2,
        compiler_params=pltpu.CompilerParams(vmem_limit_bytes=34 * MIB),
        cost_estimate=pl.CostEstimate(flops=6 * 10**9, bytes_accessed=12 * MIB, transcendentals=0),
    )(*operands)
    if not fits:
        solved = solved.transpose(1, 0, 2).reshape(n_own, cols, piece_rows).transpose(1, 0, 2)
    over(3)
    for step in range(4, length):
        along(step)
        core = over_tie(along_tie(core, step), step - 1)
        over(step)
    core = lax.all_to_all(core, "col", split_axis=0, concat_axis=0, tiled=True).reshape(total, B)
    solved, core, cross[-1] = tie(solved, core, cross[-1])
    back = lax.all_to_all(solved, "col", split_axis=0, concat_axis=0, tiled=True).reshape(total, piece_rows)
    own_rows = pl.pallas_call(
        unpack_kernel,
        out_shape=jax.ShapeDtypeStruct((slots, rank_max, piece_rows), F32),
        in_specs=[SM, SM, VM],
        out_specs=VM,
        scratch_shapes=[pltpu.VMEM((total + rank_max, piece_rows), F32)],
        compiler_params=pltpu.CompilerParams(vmem_limit_bytes=16 * MIB),
    )(offs, own_ranks, back)

    pieces = [u] + up[1:] + down[1:] + cross
    spots = [col_index]
    spots += [jnp.where(col_index >= 2 * k, col_index - 2 * k, -1) for k in range(1, length)]
    spots += [jnp.where(col_index < cols - 2 * k, col_index + 2 * k, -1) for k in range(1, length)]
    spots += [col_index ^ 1]
    for step in range(1, length):
        origin = [z - paths[z][step - 1][1] if paths[z][step - 1][0] else z + paths[z][step - 1][1] for z in range(length)]
        spots.append((2 * table(origin, here) + col_index % 2) ^ 1)
    spots = jnp.stack(spots).astype(jnp.int32)
    if fits:
        anyspec = pl.BlockSpec(memory_space=pl.ANY)
        update = pl.pallas_call(
            functools.partial(update_kernel, cols, group, len(pieces)),
            out_shape=jax.ShapeDtypeStruct((slots, 1, rank_max, order), F32),
            grid_spec=pltpu.PrefetchScalarGridSpec(
                num_scalar_prefetch=5,
                grid=(cols,),
                in_specs=[anyspec] * (len(pieces) + 1),
                out_specs=pl.BlockSpec((group, 1, rank_max, order), lambda c, *_: (c, 0, 0, 0)),
                scratch_shapes=[
                    pltpu.VMEM((cols, total + rank_max, B), F32),
                    pltpu.VMEM((total + rank_max, B), F32),
                    pltpu.VMEM((2 * rank_max, order), BF16),
                    pltpu.SemaphoreType.DMA((len(pieces) + 1,)),
                ],
            ),
            compiler_params=pltpu.CompilerParams(vmem_limit_bytes=60 * MIB),
            cost_estimate=pl.CostEstimate(flops=2 * 10**9, bytes_accessed=24 * MIB, transcendentals=0),
        )(spots, offs, own_ranks, own_tiles, col_index[None].astype(jnp.int32), core, *pieces)
        update = jnp.transpose(update, (0, 1, 3, 2))
    else:
        where = jnp.where(spots < 0, cols, spots)
        full = jnp.zeros((cols + 1, total, piece_rows), F32)
        for i, piece in enumerate(pieces):
            full = lax.dynamic_update_index_in_dim(full, piece, where[i], 0)
        full = full[:cols].transpose(1, 0, 2).reshape(total, order)
        index = offs[:, None] + jnp.arange(rank_max, dtype=jnp.int32)[None, :]
        index = jnp.minimum(index, total - 1)
        keep = (jnp.arange(rank_max, dtype=jnp.int32)[None, :] < own_ranks[:, None]) & (own_tiles >= col_index)[:, None]
        cs = jnp.where(keep[:, :, None], core[index][:, :, :rank_max], 0.0)
        update = jnp.einsum("srn,srq->snq", full[index], cs, precision=HIGHEST)[:, None]
    return (jnp.transpose(own_rows, (0, 2, 1)), update)


def shards(rows, cols, diag_tile, panel_left, panel_right, ranks, tile_rows):
    slots, _, rank_max = panel_left.shape
    args = (diag_tile, jnp.transpose(panel_left, (0, 2, 1)), jnp.transpose(panel_right, (0, 2, 1)), ranks, tile_rows)
    most = slots * rank_max
    grain = 16 * cols
    sizes = sorted({-(-(most * part) // (24 * grain)) * grain for part in (17, 18, 24)})
    need = jnp.max(jnp.sum(ranks.reshape(rows, slots), axis=1))
    which = sum((need > size).astype(jnp.int32) for size in sizes[:-1])
    return lax.switch(which, [functools.partial(body, rows, cols, size) for size in sizes], args)


def solution(mesh):
    return jax.shard_map(
        functools.partial(shards, mesh.shape["row"], mesh.shape["col"]),
        mesh=mesh,
        in_specs=(P("row", "col"), P("row", "col", None), P("row", "col", None), P(), P()),
        out_specs=(P("row", "col", None), P("row", "col", None, None)),
        check_vma=False,
    )
```

```python
import functools
import jax
import jax.numpy as jnp
from jax import lax
from jax.experimental import pallas as pl
from jax.experimental.pallas import tpu as pltpu
from jax.sharding import PartitionSpec as P

F32 = jnp.float32
BF16 = jnp.bfloat16
HIGHEST = lax.Precision.HIGHEST
B = 128
MIB = 2**20


def sub_row(v, k):
    return jnp.broadcast_to(v[k : k + 1, :], v.shape)


def lane_col(v, c):
    return jnp.broadcast_to(v[:, c : c + 1], v.shape)


def inverse_factor(rows):
    lane = lax.broadcasted_iota(jnp.int32, (8, B), 1)
    sub = lax.broadcasted_iota(jnp.int32, (8, B), 0)
    work, out = list(rows), []
    for p in range(len(rows)):
        base = 8 * p
        cols = {q: [lane_col(work[q], base + j) for j in range(8)] for q in range(p, len(rows))}
        t = list(cols[p])
        in_panel = (lane >= base) & (lane < base + 8)
        r = jnp.where(in_panel, jnp.where(lane - base == sub, 1.0, 0.0).astype(F32), work[p])
        g = jnp.zeros((8, B), F32)
        for k in range(0, 8, 2):
            a, b, c = sub_row(t[k], k), sub_row(t[k], k + 1), sub_row(t[k + 1], k + 1)
            det = a * c - b * b
            inv = 1.0 / det
            pivot = (sub == k) | (sub == k + 1)
            t0 = jnp.where(pivot, jnp.where(sub == k, -1.0, 0.0).astype(F32), t[k])
            t1 = jnp.where(pivot, jnp.where(sub == k, 0.0, -1.0).astype(F32), t[k + 1])
            alpha = (t0 * c - t1 * b) * inv
            beta = (t1 * a - t0 * b) * inv
            x, y = sub_row(r, k), sub_row(r, k + 1)
            g0 = x * lax.rsqrt(a)
            g1 = (a * y - b * x) * lax.rsqrt(a * det)
            g = jnp.where(sub == k, g0, jnp.where(sub == k + 1, g1, g))
            r = jnp.where(pivot, 0.0, r) - alpha * x - beta * y
            for j in range(k + 2, 8):
                t[j] = jnp.where(pivot, 0.0, t[j]) - alpha * sub_row(t[j], k) - beta * sub_row(t[j], k + 1)
        out.append(jnp.where(lane <= sub + base, g, 0.0))
        z = [sub_row(r, j) for j in range(8)]
        for q in range(p + 1, len(rows)):
            acc = jnp.where(in_panel, 0.0, work[q])
            for j in range(8):
                acc = acc - cols[q][j] * z[j]
            work[q] = acc
    return out


def eliminate(w, g, y, k0, k1, blocks):
    for k in range(k0, k1):
        lo = B * k
        rows = [w[lo + 8 * q : lo + 8 * q + 8, lo : lo + B] for q in range(B // 8)]
        for q, piece in enumerate(inverse_factor(rows)):
            g[8 * q : 8 * q + 8, :] = piece
        y[...] = jnp.dot(g[...], w[lo : lo + B, :], precision=HIGHEST, preferred_element_type=F32)
        y[:, lo : lo + B] = g[...]
        w[lo : lo + B, :] = y[...]

        def body(i, carry):
            at = pl.multiple_of(i * B, B)
            w[pl.ds(at, B), lo : lo + B] = jnp.zeros((B, B), F32)
            w[pl.ds(at, B), :] -= lax.dot_general(
                y[:, pl.ds(at, B)], y[...], (((0,), (0,)), ((), ())), precision=HIGHEST, preferred_element_type=F32
            )
            return carry

        if k + 1 < blocks:
            lax.fori_loop(k + 1, blocks, body, 0)


def first_kernel(k1, blocks, masks, place, near, far, w, g, y):
    height, width = near.shape[1:]
    me_row, me_col = place[0], place[1]
    core = me_row % 2
    for m, (even, odd) in enumerate(masks):
        for flip, buf in ((0, near), (1, far)):
            odd_core = (core + flip) % 2
            row = (me_row ^ flip) ^ jnp.where(odd_core == 0, even[0], odd[0])
            col = me_col ^ jnp.where(odd_core == 0, even[1], odd[1])
            w[pl.ds(pl.multiple_of(row * height, 8), height), pl.ds(pl.multiple_of(col * width, B), width)] = buf[m]
    eliminate(w, g, y, 0, k1, blocks)


def whole_kernel(k1, blocks, w_in, w, g, y):
    w[...] = w_in[...]
    eliminate(w, g, y, 0, k1, blocks)


def next_kernel(k0, k1, blocks, w_in, w, g, y):
    w[...] = w_in[...]
    eliminate(w, g, y, k0, k1, blocks)


VM = pl.BlockSpec(memory_space=pltpu.VMEM)
SM = pl.BlockSpec(memory_space=pltpu.SMEM)


def elimination_call(kernel, order, specs, args):
    return pl.pallas_call(
        kernel,
        out_shape=jax.ShapeDtypeStruct((order, order), F32),
        in_specs=specs,
        out_specs=VM,
        scratch_shapes=[pltpu.VMEM((B, B), F32), pltpu.VMEM((B, order), F32)],
        compiler_params=pltpu.CompilerParams(vmem_limit_bytes=8 * MIB),
        cost_estimate=pl.CostEstimate(flops=4 * 10**9, bytes_accessed=8 * MIB, transcendentals=0),
    )(*args)


def split(v):
    high = v.astype(BF16)
    return high, (v - high.astype(F32)).astype(BF16)


def dot_tt(a, b):
    return lax.dot_general(a, b, (((1,), (1,)), ((), ())), preferred_element_type=F32)


def solve_kernel(masks, joined, n_own, n_all, width_cols, rank_max, *refs):
    if joined:
        inv, own, tgt, solved, core, xh, xl, ih, il, sh, sl = refs
    else:
        place, inv, own, near, far, solved, core, xh, xl, ih, il, sh, sl = refs
    blocks = inv.shape[0] // B
    for i in range(blocks):
        rows = slice(B * i, B * i + B)
        wide = B * (i + 1)
        ih[rows, :wide], il[rows, :wide] = split(inv[rows, :wide])
        if i % 2 == 0:
            ih[rows, wide : wide + B] = jnp.zeros((B, B), BF16)
            il[rows, wide : wide + B] = jnp.zeros((B, B), BF16)
    for c in range(blocks):
        xh[:n_own, B * c : B * c + B], xl[:n_own, B * c : B * c + B] = split(own[c])
        if joined:
            xh[n_own:, B * c : B * c + B], xl[n_own:, B * c : B * c + B] = split(tgt[c])
    if not joined:
        height, width = near.shape[1:]
        me_row, me_col = place[0], place[1]
        core_bit = me_row % 2
        for m, (even, odd) in enumerate(masks):
            for flip, buf in ((0, near), (1, far)):
                odd_core = (core_bit + flip) % 2
                row = (me_row ^ flip) ^ jnp.where(odd_core == 0, even[0], odd[0])
                col = me_col ^ jnp.where(odd_core == 0, even[1], odd[1])
                part = place[2 + row]
                high, low = split(buf[m])
                at = (pl.ds(pl.multiple_of(n_own + part * height, 16), height), pl.ds(pl.multiple_of(col * width, B), width))
                xh[at] = high
                xl[at] = low
    own_rows, tgt_rows = slice(0, n_own), (n_all - n_own) // 2

    def rows_of(at, keep):
        for i in range(blocks // 2):
            deep = 2 * B * (i + 1)
            out = slice(2 * B * i, deep)
            h, l = xh[at, :deep], xl[at, :deep]
            gh, gl = ih[out, :deep], il[out, :deep]
            res = dot_tt(h, gh) + dot_tt(h, gl) + dot_tt(l, gh)
            sh[at, out], sl[at, out] = split(res)
            if keep:
                solved[2 * i] = res[:, :B]
                solved[2 * i + 1] = res[:, B:]

    rows_of(own_rows, True)

    def body(t, carry):
        rows_of(pl.ds(pl.multiple_of(n_own + t * tgt_rows, 16), tgt_rows), False)
        return carry

    lax.fori_loop(0, 2, body, 0)
    oh, ol = sh.at[:n_own], sl.at[:n_own]

    def core_body(j, carry):
        at = pl.ds(pl.multiple_of(n_own + 2 * j * rank_max, 16), 2 * rank_max)
        h, l = sh[at, :], sl[at, :]
        res = dot_tt(oh[...], h) + dot_tt(oh[...], l) + dot_tt(ol[...], h)
        core[2 * j, :, :rank_max] = res[:, :rank_max]
        core[2 * j + 1, :, :rank_max] = res[:, rank_max:]
        return carry

    lax.fori_loop(0, width_cols // 2, core_body, 0)


def rows_iota(shape):
    return lax.broadcasted_iota(jnp.int32, shape, 0)


def pack_kernel(offs, ranks, t_slot, t_rank, left, right, v, u, t, pv, pu):
    slots, rank_max, width = right.shape
    total = v.shape[0]
    rows = rows_iota((rank_max, width))
    for j in range(t.shape[0]):
        t[j] = jnp.where(rows < t_rank[j], right[t_slot[j]], 0.0)
    pv[...] = jnp.zeros_like(pv)
    pu[...] = jnp.zeros_like(pu)
    for s in range(slots):
        at = pl.ds(offs[s], rank_max)
        keep = rows < ranks[s]
        pv[at, :] = jnp.where(keep, right[s], 0.0)
        pu[at, :] = jnp.where(keep, left[s], 0.0)
    v[...] = pv[:total]
    u[...] = pu[:total]


def unpack_kernel(offs, ranks, packed, out, held):
    slots, rank_max, width = out.shape
    held[: packed.shape[0]] = packed[...]
    rows = rows_iota((rank_max, width))
    for s in range(slots):
        out[s] = jnp.where(rows < ranks[s], held[pl.ds(offs[s], rank_max), :], 0.0)


def update_kernel(n, group, count, spots, offs, ranks, tiles, col, core, *refs):
    pieces, (out, us, cs, u, sems) = refs[:count], refs[count:]
    step = pl.program_id(0)
    rank_max = out.shape[2]
    total = pieces[0].shape[0]

    early = 2 * group * rank_max
    cores = pltpu.make_async_copy(core, cs.at[:total], sems.at[2 * count])

    def fetch(i, late):
        at = slice(early, total) if late else slice(0, early)
        return pltpu.make_async_copy(pieces[i].at[at], us.at[jnp.maximum(spots[i], 0), at], sems.at[2 * i + late])

    @pl.when(step == 0)
    def _():
        cores.start()
        for late in (0, 1):
            for i in range(count):
                pl.when(spots[i] >= 0)(fetch(i, late).start)
        us[:, total:] = jnp.zeros((n, rank_max, B), F32)
        cores.wait()
        for i in range(count):
            pl.when(spots[i] >= 0)(fetch(i, 0).wait)

    @pl.when(step == 2)
    def _():
        for i in range(count):
            pl.when(spots[i] >= 0)(fetch(i, 1).wait)

    rows = rows_iota((rank_max, B))
    for s in range(group):
        slot = step * group + s
        at = pl.ds(offs[slot], rank_max)
        for k in range(n):
            lanes = slice(B * k, B * k + B)
            u[:rank_max, lanes], u[rank_max:, lanes] = split(us[k, at, :])
        keep = rows < jnp.where(tiles[slot] >= col[0], ranks[slot], 0)
        c = jnp.where(keep, cs[at, :], 0.0)
        ch, cl = split(jnp.transpose(c)[:rank_max])
        w = u[...]
        res = jnp.dot(jnp.concatenate([ch, ch], axis=1), w, preferred_element_type=F32)
        out[s, 0] = res + jnp.dot(cl, w[:rank_max], preferred_element_type=F32)


def phases(rows, cols):
    even = []
    bit = cols // 2
    while bit > 1:
        even.append((0, bit))
        bit //= 2
    bit = rows // 2
    while bit > 2:
        even.append((bit, 0))
        bit //= 2
    odd = even + [(2, 0), (0, 1)]
    even = even + [(0, 1), (2, 0)]
    return even, odd


def gather_masks(rows, cols):
    even, odd = phases(rows, cols)

    def masks(steps):
        got = [(0, 0)]
        for r, c in steps:
            got = got + [(a ^ r, b ^ c) for a, b in got]
        return got

    return list(zip(masks(even), masks(odd)))


def link_pairs(rows, cols, even, odd):
    pairs = []
    for r in range(rows):
        dr, dc = odd if r % 2 else even
        for c in range(cols):
            pairs.append((r * cols + c, (r ^ dr) * cols + (c ^ dc)))
    return pairs


def tie(*values):
    return lax.optimization_barrier(values)


def table(values, index):
    return jnp.array(values, jnp.int32)[index]


def body(rows, cols, total, args):
    diag_tile, left, right, ranks, tile_rows = args
    slots, rank_max, piece_rows = left.shape
    order = piece_rows * cols
    blocks = order // B
    group = slots // cols
    n_own, n_tgt = total // cols, cols * rank_max
    n_all = n_own + n_tgt
    row_index = lax.axis_index("row")
    col_index = lax.axis_index("col")
    masks = gather_masks(rows, cols)
    fits = piece_rows % B == 0 and blocks == cols
    own_ranks = lax.dynamic_slice_in_dim(ranks, row_index * slots, slots)
    own_tiles = lax.dynamic_slice_in_dim(tile_rows, row_index * slots, slots)
    before = jnp.arange(slots, dtype=jnp.int32)
    offs = jnp.sum(jnp.where(before[None, :] < before[:, None], own_ranks[None, :], 0), axis=1)
    wanted = jnp.arange(cols, dtype=jnp.int32)
    every_slot = jnp.arange(tile_rows.shape[0], dtype=jnp.int32)
    hit = tile_rows[None, :] == wanted[:, None]
    holder = jnp.sum(jnp.where(hit, every_slot[None, :], 0), axis=1)
    t_rank = jnp.sum(jnp.where(hit, ranks[None, :], 0), axis=1)
    t_rank = jnp.where(holder // slots == row_index, t_rank, 0)

    v, u, part = pl.pallas_call(
        pack_kernel,
        out_shape=[
            jax.ShapeDtypeStruct((total, piece_rows), F32),
            jax.ShapeDtypeStruct((total, piece_rows), F32),
            jax.ShapeDtypeStruct((cols, rank_max, piece_rows), F32),
        ],
        in_specs=[SM] * 4 + [VM] * 2,
        out_specs=[VM] * 3,
        scratch_shapes=[pltpu.VMEM((total + rank_max, piece_rows), F32)] * 2,
        compiler_params=pltpu.CompilerParams(vmem_limit_bytes=8 * MIB),
    )(offs, own_ranks, holder % slots, t_rank, left, right)

    length = cols // 2
    up, down, cross = [u], [u], []

    def along(step):
        if step < length:
            up.append(lax.ppermute(up[-1], "col", [(c, c + 2) for c in range(2 * step - 2, cols - 2)]))
            down.append(lax.ppermute(down[-1], "col", [(c + 2, c) for c in range(cols - 2 * step)]))

    def reach(z):
        ways = [(k, 0 if (z >= k) == (side == (z >= length // 2)) else 1, side) for k in range(1, length) for side in (True, False)]
        return [(side, k) for k, _, side in sorted(ways) if (z >= k if side else z + k < length)]

    paths = [reach(z) for z in range(length)]
    here = col_index // 2

    def over(step):
        if 0 < step < length:
            picks = [paths[z][step - 1] for z in range(length)]
            piece = None
            for pick in sorted(set(picks)):
                side, k = pick
                got = (up if side else down)[k]
                if piece is None:
                    piece = got
                else:
                    at = functools.reduce(jnp.logical_or, [here == z for z in range(length) if picks[z] == pick])
                    piece = jnp.where(at, got, piece)
            up[step], down[step], piece = tie(up[step], down[step], piece)
            cross.append(lax.ppermute(piece, "col", [(c, c ^ 1) for c in range(cols)]))

    def along_tie(x, step):
        if step < length:
            x, up[step], down[step] = tie(x, up[step], down[step])
        return x

    def over_tie(x, step):
        if step < length:
            x, cross[step] = tie(x, cross[step])
        return x

    even, odd = phases(rows, cols)
    links = len(even)
    swap = [(r, r ^ 1) for r in range(rows)]

    t_steps = []
    bit = 1
    while bit < rows:
        t_steps.append(("sum", bit))
        bit *= 2
    t_steps += [("link", i) for i in range(links)] + [("core", 0)]
    state = dict(part=part, t=None, t_far=None)

    def t_step():
        if not t_steps:
            return
        kind, which = t_steps.pop(0)
        if kind == "sum":
            p = state["part"]
            h = p.shape[0] // 2
            side = (row_index // which) % 2
            kept = lax.dynamic_slice_in_dim(p, side * h, h, 0)
            sent = lax.dynamic_slice_in_dim(p, (1 - side) * h, h, 0)
            state["part"] = kept + lax.ppermute(sent, "row", [(r, r ^ which) for r in range(rows)])
            if t_steps[0][0] == "link":
                p = state["part"]
                state["per"] = p.shape[0]
                state["t"] = p.reshape(1, p.shape[0] * rank_max, piece_rows)
        elif kind == "link":
            t = state["t"]
            got = lax.ppermute(t, ("row", "col"), link_pairs(rows, cols, even[which], odd[which]))
            state["t"] = jnp.concatenate([t, got], axis=0)
        else:
            state["t_far"] = lax.ppermute(state["t"], "row", swap)

    def t_tie(x):
        key = "t" if state["t"] is not None else "part"
        x, state[key] = tie(x, state[key])
        return x

    near = diag_tile[None]
    for i in range(links):
        got = lax.ppermute(near, ("row", "col"), link_pairs(rows, cols, even[i], odd[i]))
        t_step()
        near = jnp.concatenate([near, got], axis=0)
        near = t_tie(near)
        if i == 0:
            near, u = tie(near, u)
            up[0] = down[0] = u
            cross.append(lax.ppermute(u, "col", [(c, c ^ 1) for c in range(cols)]))
            along(1)
    far = lax.ppermute(near, "row", swap)
    t_step()
    far = t_tie(far)

    far, v = tie(far, v)
    own = lax.all_to_all(v.reshape(cols, n_own, piece_rows), "col", split_axis=0, concat_axis=0, tiled=True)

    places = []
    for r in range(rows):
        at, h, bb = 0, rows // 2, 1
        while bb < rows:
            at += h * ((r // bb) % 2)
            h //= 2
            bb *= 2
        places.append(at)

    def sources():
        near_m = jnp.where(row_index % 2 == 0, table([e for e, _ in masks], slice(None)), table([o for _, o in masks], slice(None)))
        far_m = jnp.where(row_index % 2 == 0, table([o for _, o in masks], slice(None)), table([e for e, _ in masks], slice(None)))
        r = jnp.concatenate([row_index ^ near_m[:, 0], row_index ^ 1 ^ far_m[:, 0]])
        c = jnp.concatenate([col_index ^ near_m[:, 1], col_index ^ far_m[:, 1]])
        return r, c

    spots = [col_index]
    spots += [jnp.where(col_index >= 2 * k, col_index - 2 * k, -1) for k in range(1, length)]
    spots += [jnp.where(col_index < cols - 2 * k, col_index + 2 * k, -1) for k in range(1, length)]
    spots += [col_index ^ 1]
    for step in range(1, length):
        origin = [z - paths[z][step - 1][1] if paths[z][step - 1][0] else z + paths[z][step - 1][1] for z in range(length)]
        spots.append((2 * table(origin, here) + col_index % 2) ^ 1)
    spots = jnp.stack(spots).astype(jnp.int32)

    place = jnp.concatenate([jnp.stack([row_index, col_index]).astype(jnp.int32), jnp.array(places, jnp.int32)])
    per_call = 2
    t_step()
    if fits:
        inv = elimination_call(
            functools.partial(first_kernel, per_call, blocks, masks), order, [SM, VM, VM], (place, near, far)
        )
    else:
        r, c = sources()
        pieces = jnp.concatenate([near, far], axis=0)
        tile = jnp.zeros((rows * cols,) + pieces.shape[1:], F32).at[r * cols + c].set(pieces)
        tile = tile.reshape(rows, cols, order // rows, piece_rows).transpose(0, 2, 1, 3).reshape(order, order)
        inv = elimination_call(functools.partial(whole_kernel, per_call, blocks), order, [VM], (tile,))
    inv = t_tie(inv)
    for k in range(per_call, blocks, per_call):
        while t_steps:
            t_step()
        if k == per_call:
            inv, own = tie(over_tie(along_tie(inv, 1), 0), own)
            over(1)
            along(2)
        if k == 2 * per_call:
            inv, state["t_far"] = tie(along_tie(inv, 2), state["t_far"])
            over(2)
            along(3)
        if k == 3 * per_call:
            inv, spots, own_tiles, me_col = tie(over_tie(inv, 1), spots, own_tiles, col_index[None].astype(jnp.int32))
        inv = elimination_call(functools.partial(next_kernel, k, k + per_call, blocks), order, [VM], (inv,))
    t_near, t_far = state["t"], state["t_far"]
    per = state["per"]

    inv = over_tie(along_tie(inv, 3), 2)
    own = own.reshape(cols, n_own, piece_rows)
    if fits:
        specs, operands = [SM, VM, VM, VM, VM], (place, inv, own, t_near, t_far)
    else:
        own = own.transpose(1, 0, 2).reshape(n_own, blocks, B).transpose(1, 0, 2)
        r, c = sources()
        spots = table(places, r)
        pieces = jnp.concatenate([t_near, t_far], axis=0)
        tgt = jnp.zeros((rows * cols,) + pieces.shape[1:], F32).at[spots * cols + c].set(pieces)
        tgt = tgt.reshape(rows, cols, per * rank_max, piece_rows).transpose(0, 2, 1, 3).reshape(n_tgt, blocks, B)
        specs, operands = [VM, VM, VM], (inv, own, tgt.transpose(1, 0, 2))
    solved, core = pl.pallas_call(
        functools.partial(solve_kernel, masks, not fits, n_own, n_all, cols, rank_max),
        out_shape=[
            jax.ShapeDtypeStruct((blocks, n_own, B), F32),
            jax.ShapeDtypeStruct((cols, n_own, B), F32),
        ],
        in_specs=specs,
        out_specs=[VM, VM],
        scratch_shapes=[pltpu.VMEM((n_all, order), BF16)] * 2
        + [pltpu.VMEM((order, order), BF16)] * 2
        + [pltpu.VMEM((n_all, order), BF16)] * 2,
        compiler_params=pltpu.CompilerParams(vmem_limit_bytes=24 * MIB),
        cost_estimate=pl.CostEstimate(flops=6 * 10**9, bytes_accessed=12 * MIB, transcendentals=0),
    )(*operands)
    if not fits:
        solved = solved.transpose(1, 0, 2).reshape(n_own, cols, piece_rows).transpose(1, 0, 2)
    over(3)
    for step in range(4, length):
        along(step)
        core = over_tie(along_tie(core, step), step - 1)
        over(step)
    core = lax.all_to_all(core, "col", split_axis=0, concat_axis=0, tiled=True).reshape(total, B)
    solved, core, cross[-1] = tie(solved, core, cross[-1])
    back = lax.all_to_all(solved, "col", split_axis=0, concat_axis=0, tiled=True).reshape(total, piece_rows)
    own_rows = pl.pallas_call(
        unpack_kernel,
        out_shape=jax.ShapeDtypeStruct((slots, rank_max, piece_rows), F32),
        in_specs=[SM, SM, VM],
        out_specs=VM,
        scratch_shapes=[pltpu.VMEM((total + rank_max, piece_rows), F32)],
        compiler_params=pltpu.CompilerParams(vmem_limit_bytes=16 * MIB),
    )(offs, own_ranks, back)

    pieces = [u] + up[1:] + down[1:] + cross
    if fits:
        anyspec = pl.BlockSpec(memory_space=pl.ANY)
        update = pl.pallas_call(
            functools.partial(update_kernel, cols, group, len(pieces)),
            out_shape=jax.ShapeDtypeStruct((slots, 1, rank_max, order), F32),
            grid_spec=pltpu.PrefetchScalarGridSpec(
                num_scalar_prefetch=5,
                grid=(cols,),
                in_specs=[anyspec] * (len(pieces) + 1),
                out_specs=pl.BlockSpec((group, 1, rank_max, order), lambda c, *_: (c, 0, 0, 0)),
                scratch_shapes=[
                    pltpu.VMEM((cols, total + rank_max, B), F32),
                    pltpu.VMEM((total + rank_max, B), F32),
                    pltpu.VMEM((2 * rank_max, order), BF16),
                    pltpu.SemaphoreType.DMA((2 * len(pieces) + 1,)),
                ],
            ),
            compiler_params=pltpu.CompilerParams(vmem_limit_bytes=60 * MIB),
            cost_estimate=pl.CostEstimate(flops=2 * 10**9, bytes_accessed=24 * MIB, transcendentals=0),
        )(spots, offs, own_ranks, own_tiles, me_col, core, *pieces)
        update = jnp.transpose(update, (0, 1, 3, 2))
    else:
        where = jnp.where(spots < 0, cols, spots)
        full = jnp.zeros((cols + 1, total, piece_rows), F32)
        for i, piece in enumerate(pieces):
            full = lax.dynamic_update_index_in_dim(full, piece, where[i], 0)
        full = full[:cols].transpose(1, 0, 2).reshape(total, order)
        index = offs[:, None] + jnp.arange(rank_max, dtype=jnp.int32)[None, :]
        index = jnp.minimum(index, total - 1)
        keep = (jnp.arange(rank_max, dtype=jnp.int32)[None, :] < own_ranks[:, None]) & (own_tiles >= col_index)[:, None]
        cs = jnp.where(keep[:, :, None], core[index][:, :, :rank_max], 0.0)
        update = jnp.einsum("srn,srq->snq", full[index], cs, precision=HIGHEST)[:, None]
    return (jnp.transpose(own_rows, (0, 2, 1)), update)


def shards(rows, cols, diag_tile, panel_left, panel_right, ranks, tile_rows):
    slots, _, rank_max = panel_left.shape
    args = (diag_tile, jnp.transpose(panel_left, (0, 2, 1)), jnp.transpose(panel_right, (0, 2, 1)), ranks, tile_rows)
    most = slots * rank_max
    grain = 16 * cols
    sizes = sorted({-(-(most * part) // (24 * grain)) * grain for part in (17, 18, 24)})
    need = jnp.max(jnp.sum(ranks.reshape(rows, slots), axis=1))
    which = sum((need > size).astype(jnp.int32) for size in sizes[:-1])
    return lax.switch(which, [functools.partial(body, rows, cols, size) for size in sizes], args)


def solution(mesh):
    return jax.shard_map(
        functools.partial(shards, mesh.shape["row"], mesh.shape["col"]),
        mesh=mesh,
        in_specs=(P("row", "col"), P("row", "col", None), P("row", "col", None), P(), P()),
        out_specs=(P("row", "col", None), P("row", "col", None, None)),
        check_vma=False,
    )
```

```python
import functools
import jax
import jax.numpy as jnp
from jax import lax
from jax.experimental import pallas as pl
from jax.experimental.pallas import tpu as pltpu
from jax.sharding import PartitionSpec as P

F32 = jnp.float32
BF16 = jnp.bfloat16
HIGHEST = lax.Precision.HIGHEST
B = 128
MIB = 2**20


def sub_row(v, k):
    return jnp.broadcast_to(v[k : k + 1, :], v.shape)


def lane_col(v, c):
    return jnp.broadcast_to(v[:, c : c + 1], v.shape)


def inverse_factor(rows):
    lane = lax.broadcasted_iota(jnp.int32, (8, B), 1)
    sub = lax.broadcasted_iota(jnp.int32, (8, B), 0)
    work, out = list(rows), []
    for p in range(len(rows)):
        base = 8 * p
        cols = {q: [lane_col(work[q], base + j) for j in range(8)] for q in range(p, len(rows))}
        t = list(cols[p])
        in_panel = (lane >= base) & (lane < base + 8)
        r = jnp.where(in_panel, jnp.where(lane - base == sub, 1.0, 0.0).astype(F32), work[p])
        g = jnp.zeros((8, B), F32)
        for k in range(0, 8, 2):
            a, b, c = sub_row(t[k], k), sub_row(t[k], k + 1), sub_row(t[k + 1], k + 1)
            det = a * c - b * b
            inv = 1.0 / det
            pivot = (sub == k) | (sub == k + 1)
            t0 = jnp.where(pivot, jnp.where(sub == k, -1.0, 0.0).astype(F32), t[k])
            t1 = jnp.where(pivot, jnp.where(sub == k, 0.0, -1.0).astype(F32), t[k + 1])
            alpha = (t0 * c - t1 * b) * inv
            beta = (t1 * a - t0 * b) * inv
            x, y = sub_row(r, k), sub_row(r, k + 1)
            g0 = x * lax.rsqrt(a)
            g1 = (a * y - b * x) * lax.rsqrt(a * det)
            g = jnp.where(sub == k, g0, jnp.where(sub == k + 1, g1, g))
            r = jnp.where(pivot, 0.0, r) - alpha * x - beta * y
            for j in range(k + 2, 8):
                t[j] = jnp.where(pivot, 0.0, t[j]) - alpha * sub_row(t[j], k) - beta * sub_row(t[j], k + 1)
        out.append(jnp.where(lane <= sub + base, g, 0.0))
        z = [sub_row(r, j) for j in range(8)]
        for q in range(p + 1, len(rows)):
            acc = jnp.where(in_panel, 0.0, work[q])
            for j in range(8):
                acc = acc - cols[q][j] * z[j]
            work[q] = acc
    return out


def eliminate(w, g, y, k0, k1, blocks):
    for k in range(k0, k1):
        lo = B * k
        rows = [w[lo + 8 * q : lo + 8 * q + 8, lo : lo + B] for q in range(B // 8)]
        for q, piece in enumerate(inverse_factor(rows)):
            g[8 * q : 8 * q + 8, :] = piece
        y[...] = jnp.dot(g[...], w[lo : lo + B, :], precision=HIGHEST, preferred_element_type=F32)
        y[:, lo : lo + B] = g[...]
        w[lo : lo + B, :] = y[...]

        def body(i, carry):
            at = pl.multiple_of(i * B, B)
            w[pl.ds(at, B), lo : lo + B] = jnp.zeros((B, B), F32)
            w[pl.ds(at, B), :] -= lax.dot_general(
                y[:, pl.ds(at, B)], y[...], (((0,), (0,)), ((), ())), precision=HIGHEST, preferred_element_type=F32
            )
            return carry

        if k + 1 < blocks:
            lax.fori_loop(k + 1, blocks, body, 0)


def first_kernel(k1, blocks, masks, place, near, far, w, g, y):
    height, width = near.shape[1:]
    me_row, me_col = place[0], place[1]
    core = me_row % 2
    for m, (even, odd) in enumerate(masks):
        for flip, buf in ((0, near), (1, far)):
            odd_core = (core + flip) % 2
            row = (me_row ^ flip) ^ jnp.where(odd_core == 0, even[0], odd[0])
            col = me_col ^ jnp.where(odd_core == 0, even[1], odd[1])
            w[pl.ds(pl.multiple_of(row * height, 8), height), pl.ds(pl.multiple_of(col * width, B), width)] = buf[m]
    eliminate(w, g, y, 0, k1, blocks)


def whole_kernel(k1, blocks, w_in, w, g, y):
    w[...] = w_in[...]
    eliminate(w, g, y, 0, k1, blocks)


def next_kernel(k0, k1, blocks, w_in, w, g, y):
    w[...] = w_in[...]
    eliminate(w, g, y, k0, k1, blocks)


VM = pl.BlockSpec(memory_space=pltpu.VMEM)
SM = pl.BlockSpec(memory_space=pltpu.SMEM)


def elimination_call(kernel, order, specs, args):
    return pl.pallas_call(
        kernel,
        out_shape=jax.ShapeDtypeStruct((order, order), F32),
        in_specs=specs,
        out_specs=VM,
        scratch_shapes=[pltpu.VMEM((B, B), F32), pltpu.VMEM((B, order), F32)],
        compiler_params=pltpu.CompilerParams(vmem_limit_bytes=8 * MIB),
        cost_estimate=pl.CostEstimate(flops=4 * 10**9, bytes_accessed=8 * MIB, transcendentals=0),
    )(*args)


def split(v):
    high = v.astype(BF16)
    return high, (v - high.astype(F32)).astype(BF16)


def dot_tt(a, b):
    return lax.dot_general(a, b, (((1,), (1,)), ((), ())), preferred_element_type=F32)


def solve_kernel(masks, joined, n_own, n_all, width_cols, rank_max, *refs):
    if joined:
        inv, own, tgt, solved, core, xh, xl, ih, il, sh, sl = refs
    else:
        place, inv, own, near, far, solved, core, xh, xl, ih, il, sh, sl = refs
    blocks = inv.shape[0] // B
    for i in range(blocks):
        rows = slice(B * i, B * i + B)
        wide = B * (i + 1)
        ih[rows, :wide], il[rows, :wide] = split(inv[rows, :wide])
        if i % 2 == 0:
            ih[rows, wide : wide + B] = jnp.zeros((B, B), BF16)
            il[rows, wide : wide + B] = jnp.zeros((B, B), BF16)
    for c in range(blocks):
        xh[:n_own, B * c : B * c + B], xl[:n_own, B * c : B * c + B] = split(own[c])
        if joined:
            xh[n_own:, B * c : B * c + B], xl[n_own:, B * c : B * c + B] = split(tgt[c])
    if not joined:
        height, width = near.shape[1:]
        me_row, me_col = place[0], place[1]
        core_bit = me_row % 2
        for m, (even, odd) in enumerate(masks):
            for flip, buf in ((0, near), (1, far)):
                odd_core = (core_bit + flip) % 2
                row = (me_row ^ flip) ^ jnp.where(odd_core == 0, even[0], odd[0])
                col = me_col ^ jnp.where(odd_core == 0, even[1], odd[1])
                part = place[2 + row]
                high, low = split(buf[m])
                at = (pl.ds(pl.multiple_of(n_own + part * height, 16), height), pl.ds(pl.multiple_of(col * width, B), width))
                xh[at] = high
                xl[at] = low
    own_rows, tgt_rows = slice(0, n_own), (n_all - n_own) // 2

    def rows_of(at, keep):
        for i in range(blocks // 2):
            deep = 2 * B * (i + 1)
            out = slice(2 * B * i, deep)
            h, l = xh[at, :deep], xl[at, :deep]
            gh, gl = ih[out, :deep], il[out, :deep]
            res = dot_tt(h, gh) + dot_tt(h, gl) + dot_tt(l, gh)
            sh[at, out], sl[at, out] = split(res)
            if keep:
                solved[2 * i] = res[:, :B]
                solved[2 * i + 1] = res[:, B:]

    rows_of(own_rows, True)

    def body(t, carry):
        rows_of(pl.ds(pl.multiple_of(n_own + t * tgt_rows, 16), tgt_rows), False)
        return carry

    lax.fori_loop(0, 2, body, 0)
    oh, ol = sh.at[:n_own], sl.at[:n_own]

    def core_body(j, carry):
        at = pl.ds(pl.multiple_of(n_own + 2 * j * rank_max, 16), 2 * rank_max)
        h, l = sh[at, :], sl[at, :]
        res = dot_tt(oh[...], h) + dot_tt(oh[...], l) + dot_tt(ol[...], h)
        core[2 * j, :, :rank_max] = res[:, :rank_max]
        core[2 * j + 1, :, :rank_max] = res[:, rank_max:]
        return carry

    lax.fori_loop(0, width_cols // 2, core_body, 0)


def rows_iota(shape):
    return lax.broadcasted_iota(jnp.int32, shape, 0)


def pack_kernel(offs, ranks, t_slot, t_rank, left, right, v, u, t, pv, pu):
    slots, rank_max, width = right.shape
    total = v.shape[0]
    rows = rows_iota((rank_max, width))
    for j in range(t.shape[0]):
        t[j] = jnp.where(rows < t_rank[j], right[t_slot[j]], 0.0)
    pv[...] = jnp.zeros_like(pv)
    pu[...] = jnp.zeros_like(pu)
    for s in range(slots):
        at = pl.ds(offs[s], rank_max)
        keep = rows < ranks[s]
        pv[at, :] = jnp.where(keep, right[s], 0.0)
        pu[at, :] = jnp.where(keep, left[s], 0.0)
    v[...] = pv[:total]
    u[...] = pu[:total]


def unpack_kernel(offs, ranks, packed, out, held):
    slots, rank_max, width = out.shape
    held[: packed.shape[0]] = packed[...]
    rows = rows_iota((rank_max, width))
    for s in range(slots):
        out[s] = jnp.where(rows < ranks[s], held[pl.ds(offs[s], rank_max), :], 0.0)


def update_kernel(n, group, count, spots, offs, ranks, tiles, col, core, *refs):
    pieces, (out, us, cs, u, sems) = refs[:count], refs[count:]
    step = pl.program_id(0)
    rank_max = out.shape[2]
    total = pieces[0].shape[0]

    early = 2 * group * rank_max
    cores = pltpu.make_async_copy(core, cs.at[:total], sems.at[2 * count])

    def fetch(i, late):
        at = slice(early, total) if late else slice(0, early)
        return pltpu.make_async_copy(pieces[i].at[at], us.at[jnp.maximum(spots[i], 0), at], sems.at[2 * i + late])

    @pl.when(step == 0)
    def _():
        cores.start()
        for late in (0, 1):
            for i in range(count):
                pl.when(spots[i] >= 0)(fetch(i, late).start)
        us[:, total:] = jnp.zeros((n, rank_max, B), F32)
        cores.wait()
        for i in range(count):
            pl.when(spots[i] >= 0)(fetch(i, 0).wait)

    @pl.when(step == 2)
    def _():
        for i in range(count):
            pl.when(spots[i] >= 0)(fetch(i, 1).wait)

    rows = rows_iota((rank_max, B))
    for s in range(group):
        slot = step * group + s
        at = pl.ds(offs[slot], rank_max)
        for k in range(n):
            lanes = slice(B * k, B * k + B)
            u[:rank_max, lanes], u[rank_max:, lanes] = split(us[k, at, :])
        keep = rows < jnp.where(tiles[slot] >= col[0], ranks[slot], 0)
        c = jnp.where(keep, cs[at, :], 0.0)
        ch, cl = split(jnp.transpose(c)[:rank_max])
        w = u[...]
        res = jnp.dot(jnp.concatenate([ch, ch], axis=1), w, preferred_element_type=F32)
        out[s, 0] = res + jnp.dot(cl, w[:rank_max], preferred_element_type=F32)


def phases(rows, cols):
    even = []
    bit = cols // 2
    while bit > 1:
        even.append((0, bit))
        bit //= 2
    bit = rows // 2
    while bit > 2:
        even.append((bit, 0))
        bit //= 2
    odd = even + [(2, 0), (0, 1)]
    even = even + [(0, 1), (2, 0)]
    return even, odd


def gather_masks(rows, cols):
    even, odd = phases(rows, cols)

    def masks(steps):
        got = [(0, 0)]
        for r, c in steps:
            got = got + [(a ^ r, b ^ c) for a, b in got]
        return got

    return list(zip(masks(even), masks(odd)))


def link_pairs(rows, cols, even, odd):
    pairs = []
    for r in range(rows):
        dr, dc = odd if r % 2 else even
        for c in range(cols):
            pairs.append((r * cols + c, (r ^ dr) * cols + (c ^ dc)))
    return pairs


def tie(*values):
    return lax.optimization_barrier(values)


def table(values, index):
    return jnp.array(values, jnp.int32)[index]


def body(rows, cols, total, args):
    diag_tile, left, right, ranks, tile_rows = args
    slots, rank_max, piece_rows = left.shape
    order = piece_rows * cols
    blocks = order // B
    group = slots // cols
    n_own, n_tgt = total // cols, cols * rank_max
    n_all = n_own + n_tgt
    row_index = lax.axis_index("row")
    col_index = lax.axis_index("col")
    masks = gather_masks(rows, cols)
    fits = piece_rows % B == 0 and blocks == cols
    own_ranks = lax.dynamic_slice_in_dim(ranks, row_index * slots, slots)
    own_tiles = lax.dynamic_slice_in_dim(tile_rows, row_index * slots, slots)
    before = jnp.arange(slots, dtype=jnp.int32)
    offs = jnp.sum(jnp.where(before[None, :] < before[:, None], own_ranks[None, :], 0), axis=1)
    wanted = jnp.arange(cols, dtype=jnp.int32)
    every_slot = jnp.arange(tile_rows.shape[0], dtype=jnp.int32)
    hit = tile_rows[None, :] == wanted[:, None]
    holder = jnp.sum(jnp.where(hit, every_slot[None, :], 0), axis=1)
    t_rank = jnp.sum(jnp.where(hit, ranks[None, :], 0), axis=1)
    t_rank = jnp.where(holder // slots == row_index, t_rank, 0)

    v, u, part = pl.pallas_call(
        pack_kernel,
        out_shape=[
            jax.ShapeDtypeStruct((total, piece_rows), F32),
            jax.ShapeDtypeStruct((total, piece_rows), F32),
            jax.ShapeDtypeStruct((cols, rank_max, piece_rows), F32),
        ],
        in_specs=[SM] * 4 + [VM] * 2,
        out_specs=[VM] * 3,
        scratch_shapes=[pltpu.VMEM((total + rank_max, piece_rows), F32)] * 2,
        compiler_params=pltpu.CompilerParams(vmem_limit_bytes=8 * MIB),
    )(offs, own_ranks, holder % slots, t_rank, left, right)

    length = cols // 2
    up, down, cross = [u], [u], []

    def along(step):
        if step < length:
            up.append(lax.ppermute(up[-1], "col", [(c, c + 2) for c in range(2 * step - 2, cols - 2)]))
            down.append(lax.ppermute(down[-1], "col", [(c + 2, c) for c in range(cols - 2 * step)]))

    def reach(z):
        ways = [(k, 0 if (z >= k) == (side == (z >= length // 2)) else 1, side) for k in range(1, length) for side in (True, False)]
        return [(side, k) for k, _, side in sorted(ways) if (z >= k if side else z + k < length)]

    paths = [reach(z) for z in range(length)]
    here = col_index // 2

    def over(step):
        if 0 < step < length:
            picks = [paths[z][step - 1] for z in range(length)]
            piece = None
            for pick in sorted(set(picks)):
                side, k = pick
                got = (up if side else down)[k]
                if piece is None:
                    piece = got
                else:
                    at = functools.reduce(jnp.logical_or, [here == z for z in range(length) if picks[z] == pick])
                    piece = jnp.where(at, got, piece)
            up[step], down[step], piece = tie(up[step], down[step], piece)
            cross.append(lax.ppermute(piece, "col", [(c, c ^ 1) for c in range(cols)]))

    def along_tie(x, step):
        if step < length:
            x, up[step], down[step] = tie(x, up[step], down[step])
        return x

    def over_tie(x, step):
        if step < length:
            x, cross[step] = tie(x, cross[step])
        return x

    even, odd = phases(rows, cols)
    links = len(even)
    swap = [(r, r ^ 1) for r in range(rows)]

    t_steps = []
    bit = 1
    while bit < rows:
        t_steps.append(("sum", bit))
        bit *= 2
    t_steps += [("link", i) for i in range(links)] + [("core", 0)]
    state = dict(part=part, t=None, t_far=None)

    def t_step():
        if not t_steps:
            return
        kind, which = t_steps.pop(0)
        if kind == "sum":
            p = state["part"]
            h = p.shape[0] // 2
            side = (row_index // which) % 2
            kept = lax.dynamic_slice_in_dim(p, side * h, h, 0)
            sent = lax.dynamic_slice_in_dim(p, (1 - side) * h, h, 0)
            state["part"] = kept + lax.ppermute(sent, "row", [(r, r ^ which) for r in range(rows)])
            if t_steps[0][0] == "link":
                p = state["part"]
                state["per"] = p.shape[0]
                state["t"] = p.reshape(1, p.shape[0] * rank_max, piece_rows)
        elif kind == "link":
            t = state["t"]
            got = lax.ppermute(t, ("row", "col"), link_pairs(rows, cols, even[which], odd[which]))
            state["t"] = jnp.concatenate([t, got], axis=0)
        else:
            state["t_far"] = lax.ppermute(state["t"], "row", swap)

    def t_tie(x):
        key = "t" if state["t"] is not None else "part"
        x, state[key] = tie(x, state[key])
        return x

    near = diag_tile[None]
    for i in range(links):
        got = lax.ppermute(near, ("row", "col"), link_pairs(rows, cols, even[i], odd[i]))
        t_step()
        near = jnp.concatenate([near, got], axis=0)
        near = t_tie(near)
        if i == 0:
            near, u = tie(near, u)
            up[0] = down[0] = u
            cross.append(lax.ppermute(u, "col", [(c, c ^ 1) for c in range(cols)]))
            along(1)
    far = lax.ppermute(near, "row", swap)
    t_step()
    far = t_tie(far)

    far, v = tie(far, v)
    own = lax.all_to_all(v.reshape(cols, n_own, piece_rows), "col", split_axis=0, concat_axis=0, tiled=True)

    places = []
    for r in range(rows):
        at, h, bb = 0, rows // 2, 1
        while bb < rows:
            at += h * ((r // bb) % 2)
            h //= 2
            bb *= 2
        places.append(at)

    def sources():
        near_m = jnp.where(row_index % 2 == 0, table([e for e, _ in masks], slice(None)), table([o for _, o in masks], slice(None)))
        far_m = jnp.where(row_index % 2 == 0, table([o for _, o in masks], slice(None)), table([e for e, _ in masks], slice(None)))
        r = jnp.concatenate([row_index ^ near_m[:, 0], row_index ^ 1 ^ far_m[:, 0]])
        c = jnp.concatenate([col_index ^ near_m[:, 1], col_index ^ far_m[:, 1]])
        return r, c

    spots = [col_index]
    spots += [jnp.where(col_index >= 2 * k, col_index - 2 * k, -1) for k in range(1, length)]
    spots += [jnp.where(col_index < cols - 2 * k, col_index + 2 * k, -1) for k in range(1, length)]
    spots += [col_index ^ 1]
    for step in range(1, length):
        origin = [z - paths[z][step - 1][1] if paths[z][step - 1][0] else z + paths[z][step - 1][1] for z in range(length)]
        spots.append((2 * table(origin, here) + col_index % 2) ^ 1)
    spots = jnp.stack(spots).astype(jnp.int32)

    place = jnp.concatenate([jnp.stack([row_index, col_index]).astype(jnp.int32), jnp.array(places, jnp.int32)])
    per_call = 2
    t_step()
    if fits:
        inv = elimination_call(
            functools.partial(first_kernel, per_call, blocks, masks), order, [SM, VM, VM], (place, near, far)
        )
    else:
        r, c = sources()
        pieces = jnp.concatenate([near, far], axis=0)
        tile = jnp.zeros((rows * cols,) + pieces.shape[1:], F32).at[r * cols + c].set(pieces)
        tile = tile.reshape(rows, cols, order // rows, piece_rows).transpose(0, 2, 1, 3).reshape(order, order)
        inv = elimination_call(functools.partial(whole_kernel, per_call, blocks), order, [VM], (tile,))
    inv = t_tie(inv)
    for k in range(per_call, blocks, per_call):
        while t_steps:
            t_step()
        if k == per_call:
            inv, own = tie(over_tie(along_tie(inv, 1), 0), own)
            over(1)
            along(2)
        if k == 2 * per_call:
            inv, state["t_far"] = tie(along_tie(inv, 2), state["t_far"])
            over(2)
            along(3)
        if k == 3 * per_call:
            inv, spots, own_tiles, me_col = tie(over_tie(inv, 1), spots, own_tiles, col_index[None].astype(jnp.int32))
        inv = elimination_call(functools.partial(next_kernel, k, k + per_call, blocks), order, [VM], (inv,))
    t_near, t_far = state["t"], state["t_far"]
    per = state["per"]

    inv = over_tie(along_tie(inv, 3), 2)
    own = own.reshape(cols, n_own, piece_rows)
    if fits:
        specs, operands = [SM, VM, VM, VM, VM], (place, inv, own, t_near, t_far)
    else:
        own = own.transpose(1, 0, 2).reshape(n_own, blocks, B).transpose(1, 0, 2)
        r, c = sources()
        spots = table(places, r)
        pieces = jnp.concatenate([t_near, t_far], axis=0)
        tgt = jnp.zeros((rows * cols,) + pieces.shape[1:], F32).at[spots * cols + c].set(pieces)
        tgt = tgt.reshape(rows, cols, per * rank_max, piece_rows).transpose(0, 2, 1, 3).reshape(n_tgt, blocks, B)
        specs, operands = [VM, VM, VM], (inv, own, tgt.transpose(1, 0, 2))
    solved, core = pl.pallas_call(
        functools.partial(solve_kernel, masks, not fits, n_own, n_all, cols, rank_max),
        out_shape=[
            jax.ShapeDtypeStruct((blocks, n_own, B), F32),
            jax.ShapeDtypeStruct((cols, n_own, B), F32),
        ],
        in_specs=specs,
        out_specs=[VM, VM],
        scratch_shapes=[pltpu.VMEM((n_all, order), BF16)] * 2
        + [pltpu.VMEM((order, order), BF16)] * 2
        + [pltpu.VMEM((n_all, order), BF16)] * 2,
        compiler_params=pltpu.CompilerParams(vmem_limit_bytes=24 * MIB),
        cost_estimate=pl.CostEstimate(flops=6 * 10**9, bytes_accessed=12 * MIB, transcendentals=0),
    )(*operands)
    if not fits:
        solved = solved.transpose(1, 0, 2).reshape(n_own, cols, piece_rows).transpose(1, 0, 2)
    over(3)
    for step in range(4, length):
        along(step)
        core = over_tie(along_tie(core, step), step - 1)
        over(step)
    core = lax.all_to_all(core, "col", split_axis=0, concat_axis=0, tiled=True).reshape(total, B)
    back = lax.all_to_all(solved, "col", split_axis=0, concat_axis=0, tiled=True).reshape(total, piece_rows)
    core, back, cross[-1] = tie(core, back, cross[-1])
    own_rows = pl.pallas_call(
        unpack_kernel,
        out_shape=jax.ShapeDtypeStruct((slots, rank_max, piece_rows), F32),
        in_specs=[SM, SM, VM],
        out_specs=VM,
        scratch_shapes=[pltpu.VMEM((total + rank_max, piece_rows), F32)],
        compiler_params=pltpu.CompilerParams(vmem_limit_bytes=16 * MIB),
    )(offs, own_ranks, back)

    pieces = [u] + up[1:] + down[1:] + cross
    if fits:
        anyspec = pl.BlockSpec(memory_space=pl.ANY)
        update = pl.pallas_call(
            functools.partial(update_kernel, cols, group, len(pieces)),
            out_shape=jax.ShapeDtypeStruct((slots, 1, rank_max, order), F32),
            grid_spec=pltpu.PrefetchScalarGridSpec(
                num_scalar_prefetch=5,
                grid=(cols,),
                in_specs=[anyspec] * (len(pieces) + 1),
                out_specs=pl.BlockSpec((group, 1, rank_max, order), lambda c, *_: (c, 0, 0, 0)),
                scratch_shapes=[
                    pltpu.VMEM((cols, total + rank_max, B), F32),
                    pltpu.VMEM((total + rank_max, B), F32),
                    pltpu.VMEM((2 * rank_max, order), BF16),
                    pltpu.SemaphoreType.DMA((2 * len(pieces) + 1,)),
                ],
            ),
            compiler_params=pltpu.CompilerParams(vmem_limit_bytes=60 * MIB),
            cost_estimate=pl.CostEstimate(flops=2 * 10**9, bytes_accessed=24 * MIB, transcendentals=0),
        )(spots, offs, own_ranks, own_tiles, me_col, core, *pieces)
        update = jnp.transpose(update, (0, 1, 3, 2))
    else:
        where = jnp.where(spots < 0, cols, spots)
        full = jnp.zeros((cols + 1, total, piece_rows), F32)
        for i, piece in enumerate(pieces):
            full = lax.dynamic_update_index_in_dim(full, piece, where[i], 0)
        full = full[:cols].transpose(1, 0, 2).reshape(total, order)
        index = offs[:, None] + jnp.arange(rank_max, dtype=jnp.int32)[None, :]
        index = jnp.minimum(index, total - 1)
        keep = (jnp.arange(rank_max, dtype=jnp.int32)[None, :] < own_ranks[:, None]) & (own_tiles >= col_index)[:, None]
        cs = jnp.where(keep[:, :, None], core[index][:, :, :rank_max], 0.0)
        update = jnp.einsum("srn,srq->snq", full[index], cs, precision=HIGHEST)[:, None]
    return (jnp.transpose(own_rows, (0, 2, 1)), update)


def shards(rows, cols, diag_tile, panel_left, panel_right, ranks, tile_rows):
    slots, _, rank_max = panel_left.shape
    args = (diag_tile, jnp.transpose(panel_left, (0, 2, 1)), jnp.transpose(panel_right, (0, 2, 1)), ranks, tile_rows)
    most = slots * rank_max
    grain = 16 * cols
    sizes = sorted({-(-(most * part) // (24 * grain)) * grain for part in (17, 18, 24)})
    need = jnp.max(jnp.sum(ranks.reshape(rows, slots), axis=1))
    which = sum((need > size).astype(jnp.int32) for size in sizes[:-1])
    return lax.switch(which, [functools.partial(body, rows, cols, size) for size in sizes], args)


def solution(mesh):
    return jax.shard_map(
        functools.partial(shards, mesh.shape["row"], mesh.shape["col"]),
        mesh=mesh,
        in_specs=(P("row", "col"), P("row", "col", None), P("row", "col", None), P(), P()),
        out_specs=(P("row", "col", None), P("row", "col", None, None)),
        check_vma=False,
    )
```
